32 devices in a mesh: dp: 2 (over y), ctx: 16 (over z, x, core).
Axes of the slice: x: 2, y: 2, z: 4, core: 2. Of those that a mesh axis runs over, the one named last changes fastest.
Arguments:
- tokens: bfloat16 [4096, 2048], P(('dp', 'ctx')), may hold values from -6 to 6
- doc_starts: int32 [4096], P(('dp', 'ctx')), may hold values from 0 to 1, as said below
- routes: int32 [4096, 8], P(('dp', 'ctx')), may hold values from 0 to 15, all different within a row; in each aligned block of 128 rows (0 to 127, 128 to 255, ...) at most 96 rows name the same one
- norm_attn: float32 [2048], replicated, may hold values from 0.5 to 1.5
- norm_query: float32 [2048], replicated, may hold values from 0.5 to 1.5
- norm_key: float32 [2048], replicated, may hold values from 0.5 to 1.5
- norm_ffn: float32 [2048], replicated, may hold values from 0.5 to 1.5
- w_query: bfloat16 [2048, 2048], P('ctx'), may hold values from -0.125 to 0.125
- w_key: bfloat16 [2048, 2048], P('ctx'), may hold values from -0.125 to 0.125
- w_value: bfloat16 [2048, 2048], P('ctx'), may hold values from -0.125 to 0.125
- w_output: bfloat16 [2048, 2048], P('ctx'), may hold values from -1.5 to 1.5
- router: bfloat16 [2048, 16], replicated, may hold values from -0.0625 to 0.0625
- expert_gate: bfloat16 [16, 2048, 1024], P('ctx'), may hold values from -0.125 to 0.125
- expert_up: bfloat16 [16, 2048, 1024], P('ctx'), may hold values from -0.125 to 0.125
- expert_down: bfloat16 [16, 1024, 2048], P('ctx'), may hold values from -4 to 4
- out_grad: bfloat16 [4096, 2048], P(('dp', 'ctx')), may hold values from -6 to 6
Outputs:
- block_out: bfloat16 [4096, 2048], P(('dp', 'ctx'))
- tokens_grad: bfloat16 [4096, 2048], P(('dp', 'ctx'))
- norm_attn_grad: float32 [2048], replicated
- norm_query_grad: float32 [2048], replicated
- norm_key_grad: float32 [2048], replicated
- norm_ffn_grad: float32 [2048], replicated
- w_query_grad: float32 [2048, 2048], P(('dp', 'ctx'))
- w_key_grad: float32 [2048, 2048], P(('dp', 'ctx'))
- w_value_grad: float32 [2048, 2048], P(('dp', 'ctx'))
- w_output_grad: float32 [2048, 2048], P(('dp', 'ctx'))
- router_grad: float32 [2048, 16], replicated
- expert_gate_grad: float32 [16, 2048, 1024], P('ctx', None, 'dp')
- expert_up_grad: float32 [16, 2048, 1024], P('ctx', None, 'dp')
- expert_down_grad: float32 [16, 1024, 2048], P('ctx', 'dp')
The draws below stay inside these ranges and needn't reach their ends.
Inputs may be any that keep to these rules, and one draw needn't show every extreme that they name: `doc_starts`: 1 where a document begins, else 0. Each group of 2048 tokens begins a document at its first token; other starts lie only among the first 128 and the last 127 tokens of the group. So one document of each group runs from its first device's tokens into its last device's. `routes`: A token names 8 different experts. In each aligned block of 128 rows (the rows of one device) no expert is named more than 96 times.
All inputs are finite; a program needn't handle non-finite values.
Results may differ from the reference program's by a relative error of at most 0.025.
Values may be sent and summed in bfloat16 or wider, within the bound.
No kernel may reach another device: no remote copies, remote signals or barrier semaphores. Data moves between devices by JAX's collectives and lax.ppermute only.
A program may use at most 384 MiB of HBM per device.

```python
import math
import jax
import jax.numpy as jnp
import numpy as np
from jax import lax

D = 2048
HEADS = 16
HD = 128
FF = 1024
TOPK = 8
TOK_DEV = 128
GROUP = 2048
TOKENS = 4096
EXPERTS = 16
CAP = 96


def draw_doc_starts(key, part):
    key = jax.random.fold_in(key, 7)
    period = max(2, TOK_DEV // 8)
    picks = jax.random.randint(key, (TOKENS // GROUP, GROUP), 0, period)
    inner = jnp.arange(GROUP, dtype=jnp.int32)[None, :]
    edge = (inner < TOK_DEV) | (inner > GROUP - TOK_DEV)
    flags = jnp.where(edge & (picks == 0), 1, 0)
    flags = jnp.where(inner == 0, 1, flags)
    return flags.reshape(TOKENS).astype(jnp.int32)


def steps_of(own_key, shape, cuts, least, largest):
    level, own = 1.0, jax.random.fold_in(own_key, 6)
    for position, blocks in cuts:
        heights = jnp.exp(jax.random.uniform(jax.random.fold_in(own, position), (blocks,), jnp.float32, least / len(cuts), largest / len(cuts)))
        level = level * jnp.repeat(heights, shape[position] // blocks).reshape([-1 if axis == position else 1 for axis in range(len(shape))])
    return level


def routed_block(key, own, number, rows, count, top, limit, skew):
    order = jax.random.permutation(key, count)
    packed, usual = shares(count, rows * top, limit, skew, True), shares(count, rows * top, limit, skew, False)
    places = jnp.arange(count)

    def named(sizes, offset_by):
        used = int((sizes > 0).sum())
        fixed = max(1, used // 4)
        shifted = fixed + (places - fixed + offset_by * (used - fixed)) % max(1, count - fixed)
        return jnp.zeros((count,), jnp.int32).at[order[jnp.where(places < fixed, places, shifted)]].set(jnp.asarray(sizes, jnp.int32))

    sizes = jnp.where(number % 4 == 0, named(packed, number // 4), named(usual, number - number // 4 - 1))
    mixed = jax.random.permutation(jax.random.fold_in(own, 3), count)
    giver, taker = mixed[0:count // 2 * 2:2], mixed[1:count // 2 * 2:2]
    slack = jnp.minimum(sizes[giver] - 1, limit - sizes[taker]) // 2
    slack = jnp.where((giver == order[0]) | (taker == order[0]) | (sizes[taker] == 0), 0, jnp.maximum(slack, 0))
    shifted = jax.random.randint(jax.random.fold_in(own, 4), (count // 2,), 0, 1 << 20) % (slack + 1)
    sizes = sizes.at[giver].add(-shifted).at[taker].add(shifted)
    labels = jnp.searchsorted(jnp.cumsum(sizes), jnp.arange(rows * top), side="right").astype(jnp.int32)
    listing = labels.reshape(top, rows).T
    listing = listing[jax.random.permutation(jax.random.fold_in(own, 1), rows)]
    offset_by = jax.random.randint(jax.random.fold_in(own, 2), (rows, 1), 0, top)
    return jnp.take_along_axis(listing, (jnp.arange(top)[None, :] + offset_by) % top, axis=1)


def shares(number_of, total, most, lean, full):
    portions = [(1 << 20) // math.isqrt(standing ** lean) + 1 for standing in range(1, number_of + 1)]
    largest = most if full else min(most, max(-(-total // number_of), total * portions[0] // sum(portions)))
    least = 1 if total - largest >= number_of - 1 else 0
    given, surplus = [largest] + [least] * (number_of - 1), total - largest - least * (number_of - 1)
    while surplus > 0:
        movable = [i for i in range(1, number_of) if given[i] < largest] or [i for i in range(1, number_of) if given[i] < most]
        pool, budget = sum([portions[i] for i in movable]), surplus
        for i in movable:
            more = min(most - given[i], max(1, budget * portions[i] // pool), surplus)
            given[i] = given[i] + more
            surplus = surplus - more
    return np.array(given)


def scatter_about(stream_key, shape, width, most, cuts=(), kind=jnp.bfloat16):
    values = width * jax.random.normal(stream_key, shape, jnp.float32)
    if cuts:
        values = values * steps_of(stream_key, shape, cuts, -0.22, 0.18)
    return jnp.clip(values, -most, most).astype(kind)


def setup_inputs(seed: int = 0) -> dict:
    key_list = jax.random.split(jax.random.key(seed), 17)
    tokens = scatter_about(key_list[0], (TOKENS, D), 1.0, 6.0, ((0, 32),))
    doc_starts = draw_doc_starts(jax.random.fold_in(key_list[16], 71), 0)
    routes_keys = jax.random.split(jax.random.fold_in(key_list[2], 1), TOKENS // TOK_DEV)
    routes_turns = jax.random.permutation(jax.random.fold_in(key_list[2], 3), TOKENS // TOK_DEV)
    routes = jax.vmap(lambda own, number: routed_block(jax.random.fold_in(key_list[2], 2), own, number, TOK_DEV, EXPERTS, TOPK, CAP, 1))(routes_keys, routes_turns).reshape((TOKENS, TOPK))
    norm_attn = jnp.clip(1.0 + 0.1 * jax.random.normal(key_list[3], (D,), jnp.float32), 0.5, 1.5)
    norm_query = jnp.clip(1.0 + 0.1 * jax.random.normal(key_list[4], (D,), jnp.float32), 0.5, 1.5)
    norm_key = jnp.clip(1.0 + 0.1 * jax.random.normal(key_list[5], (D,), jnp.float32), 0.5, 1.5)
    norm_ffn = jnp.clip(1.0 + 0.1 * jax.random.normal(key_list[6], (D,), jnp.float32), 0.5, 1.5)
    w_query = scatter_about(key_list[7], (D, D), D ** -0.5, 0.125, ((0, 16),))
    w_key = scatter_about(key_list[8], (D, D), D ** -0.5, 0.125, ((0, 16),))
    w_value = scatter_about(key_list[9], (D, D), D ** -0.5, 0.125, ((0, 16),))
    w_output = scatter_about(key_list[10], (D, D), 16 ** -0.5, 1.5, ((0, 16),))
    router = scatter_about(key_list[11], (D, EXPERTS), (4 * D) ** -0.5, 0.0625)
    expert_gate = scatter_about(key_list[12], (EXPERTS, D, FF), D ** -0.5, 0.125, ((0, 16),))
    expert_up = scatter_about(key_list[13], (EXPERTS, D, FF), D ** -0.5, 0.125, ((0, 16),))
    expert_down = scatter_about(key_list[14], (EXPERTS, FF, D), 2 ** -0.5, 4.0, ((0, 16),))
    out_grad = scatter_about(key_list[15], (TOKENS, D), 1.0, 6.0, ((0, 32),))
    return {"tokens": tokens, "doc_starts": doc_starts, "routes": routes, "norm_attn": norm_attn, "norm_query": norm_query, "norm_key": norm_key, "norm_ffn": norm_ffn, "w_query": w_query, "w_key": w_key, "w_value": w_value, "w_output": w_output, "router": router, "expert_gate": expert_gate, "expert_up": expert_up, "expert_down": expert_down, "out_grad": out_grad}


@jax.custom_vjp
def low(v):
    return lax.optimization_barrier(v.astype(jnp.bfloat16)).astype(jnp.float32)

@jax.custom_vjp
def low_back(v):
    return v

def low_keep(v):
    return (low(v), None)

def low_pass(kept, grad):
    return (grad,)

def back_keep(v):
    return (v, None)

def back_low(kept, grad):
    return (low(grad),)
low.defvjp(low_keep, low_pass)
low_back.defvjp(back_keep, back_low)
EPS = 1e-05
THETA = 10000.0
NEGATIVE = -1e+30
HIGH = lax.Precision.HIGHEST

def norm_rows(v, gain):
    return v * lax.rsqrt(lax.optimization_barrier(jnp.mean(v * v, axis=-1, keepdims=True)) + EPS) * gain

def rotate(v, place):
    half = v.shape[-1] // 2
    freq = THETA ** (-jnp.arange(half, dtype=jnp.float32) * 2.0 / v.shape[-1])
    angle = place.astype(jnp.float32)[:, None] * freq[None, :]
    cosine = jnp.cos(angle)[:, None, :]
    sine = jnp.sin(angle)[:, None, :]
    first = v[..., :half]
    second = v[..., half:]
    return jnp.concatenate([first * cosine - second * sine, second * cosine + first * sine], axis=-1)

def qk_post(proj, gain, place):
    count = proj.shape[0]
    normed = norm_rows(proj, gain).reshape(count, HEADS, HD)
    return rotate(normed, place).reshape(count, HEADS * HD)

def both(v):
    return low(low_back(v))

def matmul(a, b):
    return jnp.dot(a, b, precision=HIGH)

def group_attention(query, keys, values, seg):
    block = min(512, GROUP)
    count = GROUP // block
    places = jnp.arange(GROUP, dtype=jnp.int32)
    qh = query.reshape(count, block, HEADS, HD)
    kh = keys.reshape(GROUP, HEADS, HD)
    vh = values.reshape(GROUP, HEADS, HD)

    def one_block(pieces):
        qblock, qseg, qplace = pieces
        score = jnp.einsum('qhd,khd->hqk', qblock, kh, precision=HIGH) * HD ** (-0.5)
        score = low_back(score)
        keep = (places[None, :] <= qplace[:, None]) & (seg[None, :] == qseg[:, None])
        score = jnp.where(keep[None], score, NEGATIVE)
        prob = jax.nn.softmax(score, axis=-1)
        return jnp.einsum('hqk,khd->qhd', low(prob), vh, precision=HIGH)
    out = lax.map(jax.checkpoint(one_block), (qh, seg.reshape(count, block), places.reshape(count, block)))
    return out.reshape(GROUP, HEADS * HD)

def forward(tokens, norm_attn, norm_query, norm_key, norm_ffn, w_query, w_key, w_value, w_output, router, expert_gate, expert_up, expert_down, seg, place, chosen):
    groups = TOKENS // GROUP
    n1 = low(norm_rows(tokens, norm_attn))
    qp = low_back(matmul(n1, w_query))
    kp = low_back(matmul(n1, w_key))
    vp = matmul(n1, w_value)
    query = low(qk_post(qp, norm_query, place))
    keys = low(qk_post(kp, norm_key, place))
    values = both(vp)
    attn = lax.map(lambda pieces: group_attention(*pieces), (query.reshape(groups, GROUP, -1), keys.reshape(groups, GROUP, -1), values.reshape(groups, GROUP, -1), seg.reshape(groups, GROUP)))
    attn_low = both(attn.reshape(TOKENS, HEADS * HD))
    h1 = tokens + low_back(matmul(attn_low, w_output))
    n2 = low(norm_rows(h1, norm_ffn))
    probs = jax.nn.softmax(matmul(n2, router), axis=-1)
    gates = probs * chosen

    def expert_step(total, pieces):
        gate_w, up_w, down_w, column = pieces
        entry = low_back(n2)
        gate_pre = low_back(matmul(entry, gate_w))
        up_pre = low_back(matmul(entry, up_w))
        act = low(jax.nn.silu(gate_pre) * up_pre)
        result = both(matmul(act, down_w))
        return (total + column[:, None] * result, None)
    moe, _ = lax.scan(jax.checkpoint(expert_step), jnp.zeros_like(h1), (expert_gate, expert_up, expert_down, gates.T))
    return h1 + moe

def reference(tokens, doc_starts, routes, norm_attn, norm_query, norm_key, norm_ffn, w_query, w_key, w_value, w_output, router, expert_gate, expert_up, expert_down, out_grad):
    flags = doc_starts.reshape(TOKENS // GROUP, GROUP)
    seg = jnp.cumsum(flags, axis=1).astype(jnp.int32).reshape(TOKENS)
    place = jnp.tile(jnp.arange(GROUP, dtype=jnp.int32), TOKENS // GROUP)
    chosen = lax.optimization_barrier(jnp.sum((routes[:, :, None] == jnp.arange(EXPERTS, dtype=jnp.int32)[None, None, :]).astype(jnp.float32), axis=1))
    arrays = [a.astype(jnp.float32) for a in (tokens, norm_attn, norm_query, norm_key, norm_ffn, w_query, w_key, w_value, w_output, router, expert_gate, expert_up, expert_down)]

    def run(*values):
        return forward(*values, seg, place, chosen)
    out, pullback = jax.vjp(run, *arrays)
    grads = pullback(out_grad.astype(jnp.float32))
    return (out.astype(jnp.bfloat16), grads[0].astype(jnp.bfloat16), grads[1], grads[2], grads[3], grads[4], grads[5], grads[6], grads[7], grads[8], grads[9], grads[10], grads[11], grads[12])
```

```python
import functools

import jax
import jax.numpy as jnp
from jax import lax
from jax.experimental import pallas as pl
from jax.experimental.pallas import tpu as pltpu
from jax.sharding import PartitionSpec as P

HEADS = 16


EPS = 1e-05
THETA = 10000.0
NEGATIVE = -1e30
HIGH = lax.Precision.HIGHEST


def spread(block, axis, holder):
    block = jnp.where(lax.axis_index(axis) == holder, block, jnp.zeros_like(block))
    return lax.psum(block, axis)


def shifted(shard, axis, by):
    devices = lax.axis_size(axis)
    return lax.ppermute(shard, axis, [(i, (i + by) % devices) for i in range(devices)])


def norm_rows(v, gain):
    return v * lax.rsqrt(jnp.mean(v * v, axis=-1, keepdims=True) + EPS) * gain


def rotate(v, place):
    half = v.shape[-1] // 2
    freq = THETA ** (-jnp.arange(half, dtype=jnp.float32) * 2.0 / v.shape[-1])
    angle = place.astype(jnp.float32)[:, None] * freq[None, :]
    cosine = jnp.cos(angle)[:, None, :]
    sine = jnp.sin(angle)[:, None, :]
    first = v[..., :half]
    second = v[..., half:]
    return jnp.concatenate(
        [first * cosine - second * sine, second * cosine + first * sine], axis=-1
    )


def qk_post(proj, gain, place, heads):
    count, width = proj.shape
    normed = norm_rows(proj, gain).reshape(count, heads, width // heads)
    return rotate(normed, place).reshape(count, width)


def needed(q_place, q_seg, k_place, k_seg):
    return (k_place[0] <= q_place[-1]) & (k_seg[-1] >= q_seg[0])


def pair_mask(q_place, q_seg, k_place, k_seg):
    return (k_place[None, :] <= q_place[:, None]) & (k_seg[None, :] == q_seg[:, None])


def pair_grads(qh, gh, lse, delta, q_place, q_seg, kh, vh, k_place, k_seg, scale, wanted):

    def pair_compute(unused):
        score = jnp.einsum("qhd,khd->hqk", qh, kh, preferred_element_type=jnp.float32) * scale
        mask = pair_mask(q_place, q_seg, k_place, k_seg)
        prob = jnp.where(mask[None], jnp.exp(score - lse[:, :, None]), 0.0)
        dprob = jnp.einsum("qhd,khd->hqk", gh, vh, preferred_element_type=jnp.float32)
        dscore = (prob * (dprob - delta[:, :, None])).astype(jnp.bfloat16)
        prob_low = prob.astype(jnp.bfloat16)
        dq = jnp.einsum("hqk,khd->qhd", dscore, kh, preferred_element_type=jnp.float32) * scale
        dk = jnp.einsum("hqk,qhd->khd", dscore, qh, preferred_element_type=jnp.float32) * scale
        dv = jnp.einsum("hqk,qhd->khd", prob_low, gh, preferred_element_type=jnp.float32)
        return (dq, dk, dv)

    def skip(unused):
        return (
            jnp.zeros(qh.shape, jnp.float32),
            jnp.zeros(kh.shape, jnp.float32),
            jnp.zeros(vh.shape, jnp.float32),
        )

    return lax.cond(wanted, pair_compute, skip, 0)


def local_general(
    tokens,
    doc_starts,
    routes,
    norm_attn,
    norm_query,
    norm_key,
    norm_ffn,
    w_query,
    w_key,
    w_value,
    w_output,
    router,
    expert_gate,
    expert_up,
    expert_down,
    out_grad,
):
    f32 = jnp.float32
    b16 = jnp.bfloat16
    n_ctx = lax.axis_size("ctx")
    rank = lax.axis_index("ctx")
    rows, width = tokens.shape
    heads = HEADS
    head_dim = width // heads
    scale = head_dim ** (-0.5)
    experts = router.shape[1]
    topk = routes.shape[1]
    owned = expert_gate.shape[0]
    cap = max(2, rows * topk * 3 // (2 * experts))
    starts = jnp.sum(doc_starts)
    first_count = spread(starts, "ctx", 0)
    before = jnp.where(rank > 0, first_count, 0)
    seg = before + jnp.cumsum(doc_starts)
    place = rank * rows + jnp.arange(rows, dtype=jnp.int32)
    wq, wk, wv, wo = (
        lax.all_gather(w_query, "ctx", axis=0, tiled=True),
        lax.all_gather(w_key, "ctx", axis=0, tiled=True),
        lax.all_gather(w_value, "ctx", axis=0, tiled=True),
        lax.all_gather(w_output, "ctx", axis=0, tiled=True),
    )
    inputs = tokens.astype(f32)
    n1 = norm_rows(inputs, norm_attn).astype(b16)
    qp = jnp.dot(n1, wq, preferred_element_type=f32)
    kp = jnp.dot(n1, wk, preferred_element_type=f32)
    vp = jnp.dot(n1, wv, preferred_element_type=f32)
    query = qk_post(qp, norm_query, place, heads).astype(b16)
    keys = qk_post(kp, norm_key, place, heads).astype(b16)
    values = vp.astype(b16)
    qh = query.reshape(rows, heads, head_dim)
    start_state = (
        jnp.full((heads, rows), NEGATIVE, f32),
        jnp.zeros((heads, rows), f32),
        jnp.zeros((rows, heads, head_dim), f32),
    )
    k_piece = lax.all_gather(keys, "ctx", axis=0, tiled=True)
    v_piece = lax.all_gather(values, "ctx", axis=0, tiled=True)
    s_piece = lax.all_gather(seg, "ctx", axis=0, tiled=True)
    total_rows = k_piece.shape[0]
    block = min(rows, total_rows)
    count = total_rows // block

    def step(index, state):
        best, total, acc = state
        offset = index * block
        kh = lax.dynamic_slice_in_dim(k_piece, offset, block, 0).reshape(block, heads, head_dim)
        vh = lax.dynamic_slice_in_dim(v_piece, offset, block, 0).reshape(block, heads, head_dim)
        k_seg = lax.dynamic_slice_in_dim(s_piece, offset, block, 0)
        k_place = offset + jnp.arange(block, dtype=jnp.int32)

        def step_compute(unused):
            score = jnp.einsum("qhd,khd->hqk", qh, kh, preferred_element_type=f32) * scale
            mask = pair_mask(place, seg, k_place, k_seg)
            score = jnp.where(mask[None], score, NEGATIVE)
            new_best = jnp.maximum(best, jnp.max(score, axis=-1))
            shrink = jnp.exp(best - new_best)
            prob = jnp.exp(score - new_best[:, :, None])
            new_total = total * shrink + jnp.sum(prob, axis=-1)
            new_acc = acc * shrink.T[:, :, None] + jnp.einsum(
                "hqk,khd->qhd", prob.astype(b16), vh, preferred_element_type=f32
            )
            return (new_best, new_total, new_acc)

        return lax.cond(needed(place, seg, k_place, k_seg), step_compute, lambda unused: state, 0)

    best, total, acc = lax.fori_loop(0, count, step, start_state)
    attn_heads = acc / total.T[:, :, None]
    lse = best + jnp.log(total)
    attn = attn_heads.reshape(rows, width)
    attn_low = attn.astype(b16)
    h1 = inputs + jnp.dot(attn_low, wo, preferred_element_type=f32)
    n2 = norm_rows(h1, norm_ffn).astype(b16)
    probs = jax.nn.softmax(jnp.dot(n2, router, preferred_element_type=f32), axis=-1)
    choice_mask = routes[:, :, None] == jnp.arange(experts, dtype=jnp.int32)[None, None, :]
    gates = jnp.sum(jnp.where(choice_mask, probs[:, None, :], 0.0), axis=-1)
    flat = routes.reshape(-1)
    hits = (flat[:, None] == jnp.arange(experts, dtype=jnp.int32)[None, :]).astype(jnp.int32)
    slot = jnp.sum(jnp.cumsum(hits, axis=0) * hits, axis=1) - 1
    dest = flat * cap + slot
    route_ids = jnp.arange(rows * topk, dtype=jnp.int32)
    source = jnp.zeros((experts * cap,), jnp.int32).at[dest].set(route_ids)
    filled = jnp.zeros((experts * cap,), jnp.bool_).at[dest].set(True)
    send = jnp.where(filled[:, None], n2[source // topk], jnp.zeros((), b16)).reshape(
        experts, cap, width
    )
    received = lax.all_to_all(send, "ctx", split_axis=0, concat_axis=0, tiled=True)
    count = received.shape[1]
    grid = received.reshape(n_ctx, owned, count, width)
    gate_pre = jnp.einsum("secd,edh->sech", grid, expert_gate, preferred_element_type=f32)
    up_pre = jnp.einsum("secd,edh->sech", grid, expert_up, preferred_element_type=f32)
    act = (jax.nn.silu(gate_pre) * up_pre).astype(b16)
    result = jnp.einsum("sech,ehd->secd", act, expert_down, preferred_element_type=f32).astype(b16)
    returned = lax.all_to_all(
        result.reshape(n_ctx * owned, count, width), "ctx", split_axis=0, concat_axis=0, tiled=True
    )
    hidden = gate_pre.shape[-1]
    returned, kept_in, kept_gate, kept_up = (
        returned,
        received,
        gate_pre.reshape(n_ctx * owned, count, hidden),
        up_pre.reshape(n_ctx * owned, count, hidden),
    )
    picked = returned.reshape(experts * cap, width)[dest].reshape(rows, topk, width).astype(f32)
    moe = jnp.einsum("tk,tkd->td", gates, picked, precision=HIGH)
    block_out = (h1 + moe).astype(b16)
    grad_top = out_grad.astype(f32)
    gate_grad = jnp.einsum("td,tkd->tk", grad_top, picked, precision=HIGH)
    down_in = (gates[:, :, None] * grad_top[:, None, :]).astype(b16).reshape(rows * topk, width)
    back_send = jnp.where(filled[:, None], down_in[source], jnp.zeros((), b16)).reshape(
        experts, cap, width
    )
    back_recv = lax.all_to_all(back_send, "ctx", split_axis=0, concat_axis=0, tiled=True)
    hidden = kept_gate.shape[-1]
    grid_dy = back_recv.reshape(n_ctx, owned, cap, width)
    grid_x = kept_in.reshape(n_ctx, owned, cap, width)
    gate_pre = kept_gate.reshape(n_ctx, owned, cap, hidden)
    up_pre = kept_up.reshape(n_ctx, owned, cap, hidden)
    sigma = jax.nn.sigmoid(gate_pre)
    silu = jax.nn.silu(gate_pre)
    act = (silu * up_pre).astype(b16)
    dact = jnp.einsum("secd,ehd->sech", grid_dy, expert_down, preferred_element_type=f32)
    dgate_pre = (dact * up_pre * sigma * (1.0 + gate_pre * (1.0 - sigma))).astype(b16)
    dup_pre = (dact * silu).astype(b16)
    down_term = jnp.einsum("sech,secd->ehd", act, grid_dy, preferred_element_type=f32)
    gate_term = jnp.einsum("secd,sech->edh", grid_x, dgate_pre, preferred_element_type=f32)
    up_term = jnp.einsum("secd,sech->edh", grid_x, dup_pre, preferred_element_type=f32)
    entry_grad = (
        jnp.einsum("sech,edh->secd", dgate_pre, expert_gate, preferred_element_type=f32)
        + jnp.einsum("sech,edh->secd", dup_pre, expert_up, preferred_element_type=f32)
    ).astype(b16)
    entry_back = lax.all_to_all(
        entry_grad.reshape(n_ctx * owned, cap, width),
        "ctx",
        split_axis=0,
        concat_axis=0,
        tiled=True,
    )
    route_grad = jnp.sum(
        entry_back.reshape(experts * cap, width)[dest].reshape(rows, topk, width).astype(f32),
        axis=1,
    )
    gate_grad_out, up_grad_out, down_grad_out = (
        lax.psum_scatter(
            gate_term.astype(jnp.bfloat16), "dp", scatter_dimension=2, tiled=True
        ).astype(jnp.float32),
        lax.psum_scatter(
            up_term.astype(jnp.bfloat16), "dp", scatter_dimension=2, tiled=True
        ).astype(jnp.float32),
        lax.psum_scatter(
            down_term.astype(jnp.bfloat16), "dp", scatter_dimension=1, tiled=True
        ).astype(jnp.float32),
    )
    prob_grad = jnp.sum(jnp.where(choice_mask, gate_grad[:, :, None], 0.0), axis=1)
    logit_grad = probs * (prob_grad - jnp.sum(probs * prob_grad, axis=-1, keepdims=True))
    router_term = jnp.dot(n2.astype(f32).T, logit_grad, precision=HIGH)
    n2_grad = route_grad + jnp.dot(logit_grad, router.astype(f32).T, precision=HIGH)
    unused_value, ffn_back = jax.vjp(norm_rows, h1, norm_ffn)
    h1_part, ffn_gain_grad = ffn_back(n2_grad)
    h1_grad = grad_top + h1_part
    h1_low = h1_grad.astype(b16)
    attn_grad = jnp.dot(h1_low, wo.T, preferred_element_type=f32).astype(b16)
    gh = attn_grad.reshape(rows, heads, head_dim)
    delta = jnp.einsum("qhd,qhd->hq", gh.astype(f32), attn_heads, precision=HIGH)
    local_index = jnp.arange(rows, dtype=jnp.int32)

    def key_step(index, state):
        moving, query_grad = state
        k_move, v_move, s_move, key_acc, value_acc = moving
        anchor = (rank - index + n_ctx) % n_ctx
        k_place = anchor * rows + local_index
        dq, dk, dv = pair_grads(
            qh,
            gh,
            lse,
            delta,
            place,
            seg,
            k_move.astype(b16).reshape(rows, heads, head_dim),
            v_move.astype(b16).reshape(rows, heads, head_dim),
            k_place,
            s_move,
            scale,
            needed(place, seg, k_place, s_move),
        )
        moving = (
            shifted(k_move.astype(jnp.bfloat16), "ctx", 1).astype(k_move.dtype),
            shifted(v_move.astype(jnp.bfloat16), "ctx", 1).astype(v_move.dtype),
            shifted(s_move, "ctx", 1),
            shifted((key_acc + dk.reshape(rows, width)).astype(jnp.bfloat16), "ctx", 1).astype(
                jnp.float32
            ),
            shifted((value_acc + dv.reshape(rows, width)).astype(jnp.bfloat16), "ctx", 1).astype(
                jnp.float32
            ),
        )
        return (moving, query_grad + dq)

    start_keys = (
        (
            keys.astype(f32),
            values.astype(f32),
            seg,
            jnp.zeros((rows, width), f32),
            jnp.zeros((rows, width), f32),
        ),
        jnp.zeros((rows, heads, head_dim), f32),
    )
    (unused_k, unused_v, unused_s, key_grad, value_grad), query_grad = lax.fori_loop(
        0, n_ctx, key_step, start_keys
    )
    query_grad = query_grad.reshape(rows, width)
    unused_query, query_back = jax.vjp(
        lambda proj, gain: qk_post(proj, gain, place, heads), qp, norm_query
    )
    qp_grad, query_gain_grad = query_back(query_grad)
    unused_key, key_back = jax.vjp(
        lambda proj, gain: qk_post(proj, gain, place, heads), kp, norm_key
    )
    kp_grad, key_gain_grad = key_back(key_grad)
    qp_low = qp_grad.astype(b16)
    kp_low = kp_grad.astype(b16)
    vp_low = value_grad.astype(b16)
    n1_grad = (
        jnp.dot(qp_low, wq.T, preferred_element_type=f32)
        + jnp.dot(kp_low, wk.T, preferred_element_type=f32)
        + jnp.dot(vp_low, wv.T, preferred_element_type=f32)
    )
    unused_norm, attn_back = jax.vjp(norm_rows, inputs, norm_attn)
    input_part, attn_gain_grad = attn_back(n1_grad)
    tokens_grad = (h1_grad + input_part).astype(b16)
    contract = (((0,), (0,)), ((), ()))
    stacked = lax.psum_scatter(
        jnp.concatenate(
            [
                lax.dot_general(n1, qp_low, contract, preferred_element_type=f32),
                lax.dot_general(n1, kp_low, contract, preferred_element_type=f32),
                lax.dot_general(n1, vp_low, contract, preferred_element_type=f32),
                lax.dot_general(attn_low, h1_low, contract, preferred_element_type=f32),
            ],
            axis=1,
        ),
        ("dp", "ctx"),
        scatter_dimension=0,
        tiled=True,
    )
    wq_grad = stacked[:, :width]
    wk_grad = stacked[:, width : 2 * width]
    wv_grad = stacked[:, 2 * width : 3 * width]
    wo_grad = stacked[:, 3 * width :]
    attn_gain_sum, query_gain_sum, key_gain_sum, ffn_gain_sum, router_sum = lax.psum(
        (attn_gain_grad, query_gain_grad, key_gain_grad, ffn_gain_grad, router_term), ("dp", "ctx")
    )
    return (
        block_out,
        tokens_grad,
        attn_gain_sum,
        query_gain_sum,
        key_gain_sum,
        ffn_gain_sum,
        wq_grad,
        wk_grad,
        wv_grad,
        wo_grad,
        router_sum,
        gate_grad_out,
        up_grad_out,
        down_grad_out,
    )


B16 = jnp.bfloat16
F32 = jnp.float32
LANES = 128
NT = (((1,), (1,)), ((), ()))
TN = (((0,), (0,)), ((), ()))


def dot(a, b, dims=(((1,), (0,)), ((), ()))):
    return lax.dot_general(a, b, dims, preferred_element_type=F32)


def ring_of(chips):
    return [2 * p if p < chips // 2 else 2 * (chips - 1 - p) + 1 for p in range(chips)]


def attention_forward(q_ref, k_ref, v_ref, seg_row_ref, seg_col_ref, out_ref, lse_ref, *, block, scale):
    total = q_ref.shape[0]
    vt = v_ref[...].astype(F32).T.astype(B16)
    for index in range(total // block):
        low, high = index * block, (index + 1) * block
        score = dot(k_ref[:high], q_ref[low:high], NT) * scale
        key = lax.broadcasted_iota(jnp.int32, (high, block), 0)
        query = low + lax.broadcasted_iota(jnp.int32, (high, block), 1)
        seen = (key <= query) & (seg_col_ref[:high] == seg_row_ref[:, low:high])
        score = jnp.where(seen, score, NEGATIVE)
        best = jnp.max(score, axis=0, keepdims=True)
        prob = jnp.exp(score - best)
        norm = jnp.sum(prob, axis=0, keepdims=True)
        out = dot(vt[:, :high], prob.astype(B16)) / norm
        out_ref[low:high] = out.T
        lse_ref[:, low:high] = best + jnp.log(norm)


def attention_backward(
    q_ref, k_ref, v_ref, g_ref, out_ref, lse_ref, seg_row_ref, seg_col_ref, dq_ref, dk_ref, dv_ref, *, block, scale
):
    total = q_ref.shape[0]
    kt = k_ref[...].astype(F32).T.astype(B16)
    dk_ref[...] = jnp.zeros_like(dk_ref)
    dv_ref[...] = jnp.zeros_like(dv_ref)
    for index in range(total // block):
        low, high = index * block, (index + 1) * block
        q, g = q_ref[low:high], g_ref[low:high]
        delta = jnp.sum((g.astype(F32) * out_ref[low:high]).T, axis=0, keepdims=True)
        score = dot(k_ref[:high], q, NT) * scale
        key = lax.broadcasted_iota(jnp.int32, (high, block), 0)
        query = low + lax.broadcasted_iota(jnp.int32, (high, block), 1)
        seen = (key <= query) & (seg_col_ref[:high] == seg_row_ref[:, low:high])
        prob = jnp.where(seen, jnp.exp(score - lse_ref[:, low:high]), 0.0)
        dprob = dot(v_ref[:high], g, NT)
        dscore = (prob * (dprob - delta)).astype(B16)
        dk_ref[:high] += dot(dscore, q) * scale
        dv_ref[:high] += dot(prob.astype(B16), g)
        dq_ref[low:high] = dot(kt[:, :high], dscore).T * scale


def expert_kernel(ids_ref, *refs, shards, fresh):
    x_refs, refs = refs[:shards], refs[shards:]
    g_refs, refs = refs[:shards], refs[shards:]
    wg_ref, wu_ref, wd_ref = refs[:3]
    refs = refs[3 if fresh else 8 :]
    moe_ref, dx_ref, dgate_ref, ag_ref, dg_ref, du_ref, xs_ref, gs_ref, moe_acc, dx_acc = refs
    expert, step, steps = pl.program_id(0), pl.program_id(1), pl.num_programs(1)
    rows, width = g_refs[0].shape
    first = (expert == 0) & (step == 0)

    @pl.when(first)
    def _():
        for i in range(shards):
            xs_ref[i] = x_refs[i][:, :width]
            gs_ref[i] = g_refs[i][...]
        dgate_ref[...] = jnp.zeros_like(dgate_ref)

    x = xs_ref[...].reshape(shards * rows, width)
    g = gs_ref[...].reshape(shards * rows, width)
    lane = lax.broadcasted_iota(jnp.int32, (rows, LANES), 1)
    mine = (lane < 3 * ids_ref[2]) & (lax.rem(lane, ids_ref[2]) == ids_ref[expert])
    gate = jnp.concatenate(
        [
            jnp.sum(jnp.where(mine, x_refs[i][:, width:].astype(F32), 0.0), axis=1, keepdims=True)
            for i in range(shards)
        ],
        axis=0,
    )
    wg, wu, wd = wg_ref[0], wu_ref[0], wd_ref[0]
    gate_pre = dot(x, wg)
    up_pre = dot(x, wu)
    dact = dot(g, wd, NT)
    sigma = 1.0 / (1.0 + jnp.exp(-gate_pre))
    silu = gate_pre * sigma
    act = silu * up_pre
    part = jnp.sum(act * dact, axis=1, keepdims=True)
    lane = lax.broadcasted_iota(jnp.int32, (shards * rows, LANES), 1)
    dgate_ref[...] += jnp.where(lane == expert, part, 0.0).reshape(dgate_ref.shape)
    act_low = (gate * act).astype(B16)
    dact = gate * dact
    dgate_pre = (dact * up_pre * sigma * (1.0 + gate_pre * (1.0 - sigma))).astype(B16)
    dup_pre = (dact * silu).astype(B16)
    ag_ref[...] = act_low.reshape(ag_ref.shape)
    dg_ref[...] = dgate_pre.reshape(dg_ref.shape)
    du_ref[...] = dup_pre.reshape(du_ref.shape)
    moe = dot(act_low, wd)
    dx = dot(dgate_pre, wg, NT) + dot(dup_pre, wu, NT)

    @pl.when(first)
    def _():
        moe_acc[...] = moe
        dx_acc[...] = dx

    @pl.when(jnp.logical_not(first))
    def _():
        moe_acc[...] += moe
        dx_acc[...] += dx

    @pl.when((expert == pl.num_programs(0) - 1) & (step == steps - 1))
    def _():
        moe_ref[...] = moe_acc[...].astype(B16).reshape(moe_ref.shape)
        dx_ref[...] = dx_acc[...].astype(B16).reshape(dx_ref.shape)


def expert_rows(ids, xs, gs, wg, wu, wd, kept, spot, total):
    shards = len(xs)
    rows, width = gs[0].shape
    pair, _, hidden = wg.shape
    tile = min(512, hidden)
    steps = hidden // tile
    whole = lambda a: pl.BlockSpec(a.shape, lambda e, j, ids: (0, 0))
    flat = pl.BlockSpec((shards, rows, tile), lambda e, j, ids: (spot, 0, e * steps + j))
    full = pl.BlockSpec((shards, rows, width), lambda e, j, ids: (spot, 0, 0))
    alone = pl.BlockSpec((shards, rows, width), lambda e, j, ids: (0, 0, 0))
    in_specs = [whole(a) for a in xs + gs] + [
        pl.BlockSpec((1, width, tile), lambda e, j, ids: (e, 0, j)),
        pl.BlockSpec((1, width, tile), lambda e, j, ids: (e, 0, j)),
        pl.BlockSpec((1, tile, width), lambda e, j, ids: (e, j, 0)),
    ]
    operands = list(xs) + list(gs) + [wg, wu, wd]
    aliases = {}
    if kept is not None:
        base = 1 + len(operands)
        in_specs += [pl.BlockSpec(memory_space=pl.ANY)] * len(kept)
        operands += list(kept)
        aliases = {base + i: 3 + i for i in range(len(kept))}
    kept_hidden = jax.ShapeDtypeStruct((total, rows, pair * hidden), B16)
    kept_width = jax.ShapeDtypeStruct((total, rows, width), B16)
    out = pl.pallas_call(
        functools.partial(expert_kernel, shards=shards, fresh=kept is None),
        grid_spec=pltpu.PrefetchScalarGridSpec(
            num_scalar_prefetch=1,
            grid=(pair, steps),
            in_specs=in_specs,
            out_specs=[
                alone,
                alone,
                pl.BlockSpec((shards, rows, LANES), lambda e, j, ids: (0, 0, 0)),
                flat,
                flat,
                flat,
                full,
                full,
            ],
            scratch_shapes=[
                pltpu.VMEM((shards * rows, width), F32),
                pltpu.VMEM((shards * rows, width), F32),
            ],
        ),
        out_shape=[
            jax.ShapeDtypeStruct((shards, rows, width), B16),
            jax.ShapeDtypeStruct((shards, rows, width), B16),
            jax.ShapeDtypeStruct((shards, rows, LANES), F32),
            kept_hidden,
            kept_hidden,
            kept_hidden,
            kept_width,
            kept_width,
        ],
        input_output_aliases=aliases,
        compiler_params=pltpu.CompilerParams(vmem_limit_bytes=56 * 2**20),
        cost_estimate=pl.CostEstimate(
            flops=12 * shards * rows * width * hidden * pair,
            bytes_accessed=6 * width * hidden * pair,
            transcendentals=shards * rows * hidden * pair,
        ),
    )(ids, *operands)
    return out[0], out[1], out[2], out[3:]


def split_three(v):
    high = lax.reduce_precision(v, exponent_bits=8, mantissa_bits=7)
    middle = lax.reduce_precision(v - high, exponent_bits=8, mantissa_bits=7)
    return [part.astype(B16) for part in (high, middle, v - high - middle)]


def local_fast(
    tokens,
    doc_starts,
    routes,
    norm_attn,
    norm_query,
    norm_key,
    norm_ffn,
    w_query,
    w_key,
    w_value,
    w_output,
    router,
    expert_gate,
    expert_up,
    expert_down,
    out_grad,
):
    devices = lax.axis_size("ctx")
    rank = lax.axis_index("ctx")
    group = lax.axis_index("dp")
    chips = devices // 2
    chip, core = rank // 2, rank % 2
    rows, width = tokens.shape
    experts = router.shape[1]
    hd = width // HEADS
    scale = hd ** (-0.5)
    half = chips // 2
    order = ring_of(chips)
    right = [(2 * order[p] + c, 2 * order[(p + 1) % chips] + c) for p in range(chips) for c in range(2)]
    left = [(b, a) for a, b in right]
    place_in_ring = jnp.where(chip % 2 == 0, chip // 2, chips - 1 - chip // 2)
    same_core = [[2 * c + p for c in range(chips)] for p in range(2)]

    def to_right(v):
        return lax.ppermute(v, "ctx", right)

    def to_left(v):
        return lax.ppermute(v, "ctx", left)

    def core_swap(v):
        return lax.ppermute(v, "ctx", [(i, i ^ 1) for i in range(devices)])

    def group_swap(v):
        return lax.ppermute(v, "dp", [(0, 1), (1, 0)])

    def chip_at(offset):
        spot = (place_in_ring + offset + chips) % chips
        return jnp.where(spot < half, 2 * spot, 2 * (chips - 1 - spot) + 1)

    offsets = [0] + [s * o for o in range(1, half) for s in (1, -1)] + [half]

    def ring_gather(v):
        cut = v.shape[0] // 2
        got = {0: v}
        for o in range(1, half):
            got[-o] = to_right(got[-(o - 1)])
            got[o] = to_left(got[o - 1])
        first = to_right(got[-(half - 1)][:cut])
        second = to_left(got[half - 1][cut:])
        got[half] = jnp.concatenate([first, second], axis=0)
        return got

    def in_place(got):
        out = jnp.zeros((chips,) + got[0].shape, got[0].dtype)
        for o in offsets:
            out = lax.dynamic_update_index_in_dim(out, got[o], chip_at(o), 0)
        return out

    def ring_sum(part):
        far = part(half)
        cut = far.shape[1] // 2
        there = to_right(far[:, :cut])
        back = to_left(far[:, cut:])
        near, other = part(half - 1), part(1 - half)
        there = jnp.concatenate([near[:, :cut] + there, near[:, cut:]], axis=1)
        back = jnp.concatenate([other[:, :cut], other[:, cut:] + back], axis=1)
        for o in range(half - 2, 0, -1):
            there = to_right(there) + part(o)
            back = to_left(back) + part(-o)
        return to_right(there).astype(F32) + to_left(back).astype(F32) + part(0).astype(F32)

    def sum_chips(v):
        step = 2
        while step < devices:
            v = v + lax.ppermute(v, "ctx", [(i, i ^ step) for i in range(devices)])
            step *= 2
        return v

    def sum_all(v):
        v = v + core_swap(v)
        return sum_chips(v + group_swap(v))

    def by_core(mine, other, axis):
        return jnp.where(core == 0, jnp.stack([mine, other], axis), jnp.stack([other, mine], axis))

    def pick(pair, which):
        return jnp.where(which == 0, pair[0], pair[1])

    wg = jnp.concatenate([expert_gate, core_swap(expert_gate)], axis=0)
    wu = jnp.concatenate([expert_up, core_swap(expert_up)], axis=0)
    wd = jnp.concatenate([expert_down, core_swap(expert_down)], axis=0)

    inputs = tokens.astype(F32)
    n1 = norm_rows(inputs, norm_attn).astype(B16)
    lane = lax.broadcasted_iota(jnp.int32, (rows, LANES), 1)
    flags = jnp.where(lane == 0, doc_starts[:, None], 0).astype(B16)
    n1_got = ring_gather(jnp.concatenate([n1, flags], axis=1))

    slabs = []
    for w in (w_query, w_key, w_value):
        pair = w.reshape(rows, chips, 2, hd)
        slabs.append(jnp.where(group == 0, pair[:, :, 0], pair[:, :, 1]))
    slab = jnp.concatenate(slabs, axis=2).transpose(1, 0, 2)
    own = lax.all_to_all(slab, "ctx", split_axis=0, concat_axis=0, axis_index_groups=same_core, tiled=True)
    other = group_swap(own)
    low_head, high_head = jnp.where(group == 0, own, other), jnp.where(group == 0, other, own)
    columns = []
    for i in range(3):
        columns += [low_head[:, :, i * hd : (i + 1) * hd], high_head[:, :, i * hd : (i + 1) * hd]]
    columns = jnp.concatenate(columns, axis=2)
    wide = 6 * hd
    w_in = by_core(columns, core_swap(columns), 1).reshape(width, wide)
    w_out = by_core(w_output, core_swap(w_output), 0).reshape(2 * hd, width)

    flags = in_place({o: v[:, width].astype(F32) for o, v in n1_got.items()})
    n1_all = in_place({o: v[:, :width] for o, v in n1_got.items()}).reshape(chips * rows, width)
    count = chips * rows
    qkv = dot(n1_all, w_in)
    qp, kp, vp = qkv[:, : 2 * hd], qkv[:, 2 * hd : 4 * hd], qkv[:, 4 * hd :]
    squares = jnp.stack([jnp.sum(qp * qp, axis=1), jnp.sum(kp * kp, axis=1)])
    squares = sum_chips(squares.reshape(2 * chips, rows)).reshape(2, count, 1)
    q_scale = lax.rsqrt(squares[0] / width + EPS)
    k_scale = lax.rsqrt(squares[1] / width + EPS)
    gain_q = lax.dynamic_slice(norm_query, (chip * 2 * hd,), (2 * hd,))
    gain_k = lax.dynamic_slice(norm_key, (chip * 2 * hd,), (2 * hd,))

    place = (2 * lax.broadcasted_iota(jnp.int32, (chips, rows, 1), 0) + core) * rows
    place = place + lax.broadcasted_iota(jnp.int32, (chips, rows, 1), 1)
    freq = THETA ** (-jnp.arange(hd // 2, dtype=F32) * 2.0 / hd)
    angle = place.reshape(count, 1).astype(F32) * freq[None, :]
    cosine, sine = jnp.cos(angle), jnp.sin(angle)
    cosine = jnp.concatenate([cosine] * 4, axis=1)
    sine = jnp.concatenate([-sine, sine] * 2, axis=1)

    def halves(v):
        h = hd // 2
        return jnp.concatenate([v[:, h:hd], v[:, :h], v[:, hd + h :], v[:, hd : hd + h]], axis=1)

    def turn(v):
        return v * cosine + halves(v) * sine

    def turn_back(v):
        return v * cosine + halves(v * sine)

    query = turn(qp * q_scale * gain_q).astype(B16)
    keys = turn(kp * k_scale * gain_k).astype(B16)
    values = vp.astype(B16)

    def to_heads(parts):
        pairs = [(v[:, :hd], v[:, hd:]) for v in parts]
        mine = jnp.concatenate([pick(p, core) for p in pairs], axis=1)
        away = jnp.concatenate([pick(p, 1 - core) for p in pairs], axis=1)
        shape = (chips, rows, mine.shape[1])
        return by_core(mine.reshape(shape), core_swap(away).reshape(shape), 1).reshape(devices * rows, -1)

    def to_tokens(v):
        v = v.reshape(chips, 2, rows, -1)
        mine, away = pick((v[:, 0], v[:, 1]), core), pick((v[:, 0], v[:, 1]), 1 - core)
        mine, other = mine.reshape(count, -1), core_swap(away).reshape(count, -1)
        low_head, high_head = pick((mine, other), core), pick((other, mine), core)
        parts = []
        for i in range(mine.shape[1] // hd):
            parts.append(
                jnp.concatenate([low_head[:, i * hd : (i + 1) * hd], high_head[:, i * hd : (i + 1) * hd]], axis=1)
            )
        return parts

    heads = to_heads([query, keys, values])
    qh, kh, vh = heads[:, :hd], heads[:, hd : 2 * hd], heads[:, 2 * hd :]
    flags = by_core(flags, core_swap(flags), 1).reshape(devices, rows)
    tri = (lax.broadcasted_iota(jnp.int32, (rows, rows), 0) <= lax.broadcasted_iota(jnp.int32, (rows, rows), 1)).astype(F32)
    before = (
        lax.broadcasted_iota(jnp.int32, (devices, devices), 1) < lax.broadcasted_iota(jnp.int32, (devices, devices), 0)
    ).astype(F32)
    seg = jnp.dot(flags, tri) + jnp.dot(before, jnp.broadcast_to(jnp.sum(flags, axis=1, keepdims=True), (devices, rows)))
    seg_row, seg_col = seg.reshape(1, devices * rows), seg.reshape(devices * rows, 1)
    everything = devices * rows
    block = min(256, everything)
    params = pltpu.CompilerParams(vmem_limit_bytes=56 * 2**20)
    attn, lse = pl.pallas_call(
        functools.partial(attention_forward, block=block, scale=scale),
        out_shape=[
            jax.ShapeDtypeStruct((everything, hd), F32),
            jax.ShapeDtypeStruct((1, everything), F32),
        ],
        compiler_params=params,
        cost_estimate=pl.CostEstimate(
            flops=2 * everything * everything * hd, bytes_accessed=8 * everything * hd, transcendentals=everything * everything // 2
        ),
    )(qh, kh, vh, seg_row, seg_col)
    (attn_low,) = to_tokens(attn.astype(B16))
    out_part = dot(attn_low, w_out).astype(B16).reshape(chips, rows, width)
    h1 = inputs + ring_sum(lambda o: lax.dynamic_index_in_dim(out_part, chip_at(o), 0, keepdims=False))

    n2 = norm_rows(h1, norm_ffn).astype(B16)
    probs = jax.nn.softmax(dot(n2, router), axis=-1)
    chosen = jnp.sum(
        (routes[:, :, None] == jnp.arange(experts, dtype=jnp.int32)[None, None, :]).astype(F32), axis=1
    )
    sent = split_three(probs * chosen)
    sent.append(jnp.zeros((rows, LANES - 3 * experts), B16))
    top_got = ring_gather(out_grad)
    n2_got = ring_gather(jnp.concatenate([n2] + sent, axis=1))
    ids = jnp.stack([rank, rank ^ 1, jnp.int32(experts)]).astype(jnp.int32)
    moe_part, dn2_part, dgate_part = {}, {}, {}
    kept = None
    chunks = [([0], 0)] + [([o, -o], o) for o in range(1, half)] + [([half], 1)]
    for which, spot in chunks:
        moe, dn2, dgate, kept = expert_rows(
            ids, [n2_got[o] for o in which], [top_got[o] for o in which], wg, wu, wd, kept, spot, chips
        )
        for i, o in enumerate(which):
            moe_part[o], dn2_part[o], dgate_part[o] = moe[i], dn2[i], dgate[i]
    act_all, dgate_pre_all, dup_pre_all, x_all, top_all = [v.reshape(count, -1) for v in kept]
    n2_sum = ring_sum(lambda o: dn2_part[o])

    dgates = jnp.stack([dgate_part[o][:, :2] for o in offsets])
    there = jnp.stack([chip_at(o) for o in offsets])
    spread_out = (there[None, :] == jnp.arange(chips)[:, None]).astype(F32)
    dgates = jnp.dot(spread_out, dgates.transpose(0, 2, 1).reshape(chips, 2 * rows), precision=HIGH)
    dgates = dgates.reshape(chips, 2, rows)
    dgates = jnp.where(core == 0, dgates, dgates[:, ::-1])
    dgates = lax.all_to_all(dgates, "ctx", split_axis=0, concat_axis=0, axis_index_groups=same_core, tiled=True)
    prob_grad = dgates.reshape(experts, rows).T * chosen
    logit_grad = probs * (prob_grad - jnp.sum(probs * prob_grad, axis=-1, keepdims=True))
    router_term = lax.dot_general(logit_grad, n2.astype(F32), TN, precision=HIGH)
    n2_grad = n2_sum + jnp.dot(logit_grad, router.astype(F32).T, precision=HIGH)
    grad_top = out_grad.astype(F32)
    unused_value, ffn_back = jax.vjp(norm_rows, h1, norm_ffn)
    h1_part, ffn_gain_grad = ffn_back(n2_grad)
    h1_grad = grad_top + h1_part
    h1_low = h1_grad.astype(B16)

    h1_all = in_place(ring_gather(h1_low)).reshape(count, width)
    attn_grad = dot(h1_all, w_out, NT).astype(B16)
    gh = to_heads([attn_grad])
    dq, dk, dv = pl.pallas_call(
        functools.partial(attention_backward, block=block, scale=scale),
        out_shape=[jax.ShapeDtypeStruct((everything, hd), F32)] * 3,
        compiler_params=params,
        cost_estimate=pl.CostEstimate(
            flops=5 * everything * everything * hd, bytes_accessed=24 * everything * hd, transcendentals=everything * everything // 2
        ),
    )(qh, kh, vh, gh, attn, lse, seg_row, seg_col)
    query_grad, key_grad, value_grad = to_tokens(jnp.concatenate([dq, dk, dv], axis=1))
    query_grad, key_grad = turn_back(query_grad), turn_back(key_grad)
    inner = jnp.stack(
        [jnp.sum(query_grad * gain_q * qp, axis=1), jnp.sum(key_grad * gain_k * kp, axis=1)]
    )
    inner = sum_chips(inner.reshape(2 * chips, rows)).reshape(2, count, 1)
    qp_grad = q_scale * (query_grad * gain_q) - qp * (q_scale * q_scale * q_scale * (inner[0] / width))
    kp_grad = k_scale * (key_grad * gain_k) - kp * (k_scale * k_scale * k_scale * (inner[1] / width))
    query_gain = jnp.sum(query_grad * qp * q_scale, axis=0)
    key_gain = jnp.sum(key_grad * kp * k_scale, axis=0)
    qkv_low = jnp.concatenate([qp_grad.astype(B16), kp_grad.astype(B16), value_grad.astype(B16)], axis=1)
    n1_part = dot(qkv_low, w_in, NT).astype(B16).reshape(chips, rows, width)
    n1_grad = ring_sum(lambda o: lax.dynamic_index_in_dim(n1_part, chip_at(o), 0, keepdims=False))
    unused_norm, attn_back = jax.vjp(lambda v: norm_rows(v, norm_attn), inputs)
    (input_part,) = attn_back(n1_grad)
    tokens_grad = (h1_grad + input_part).astype(B16)

    block_out = (h1 + ring_sum(lambda o: moe_part[o])).astype(B16)

    w_part = dot(n1_all, qkv_low, TN)
    attn_gain = jnp.sum(w_part * w_in.astype(F32), axis=1) / norm_attn

    def own_head(v, axis):
        pairs = [lax.slice_in_dim(v, i * hd, (i + 1) * hd, axis=axis) for i in range(v.shape[axis] // hd)]
        pairs = [(pairs[i], pairs[i + 1]) for i in range(0, len(pairs), 2)]
        mine = jnp.concatenate([pick(p, core) for p in pairs], axis=axis)
        away = jnp.concatenate([pick(p, 1 - core) for p in pairs], axis=axis)
        return mine + core_swap(away)

    w_head = own_head(w_part, 1).reshape(2, width // 2, 3 * hd)
    w_mine = pick((w_head[0], w_head[1]), group) + group_swap(
        pick((w_head[0], w_head[1]), 1 - group).astype(B16)
    ).astype(F32)
    w_mine = w_mine.astype(B16).reshape(devices, -1, 3 * hd)
    w_mine = lax.all_to_all(w_mine, "ctx", split_axis=0, concat_axis=0, tiled=True)
    w_mine = w_mine.transpose(1, 0, 2).astype(F32)
    slab_rows = w_mine.shape[0]
    wq_grad, wk_grad, wv_grad = [
        w_mine[:, :, i * hd : (i + 1) * hd].reshape(slab_rows, width) for i in range(3)
    ]
    o_head = own_head(dot(attn_low, h1_all, TN), 0)
    o_head = (o_head + group_swap(o_head.astype(B16)).astype(F32)).astype(B16)
    wo_grad = None
    for i in range(2):
        moves = [
            (g * devices + devices // 2 * g + j, g * devices + 2 * j + i) for g in range(2) for j in range(devices // 2)
        ]
        piece = lax.ppermute(o_head[i * slab_rows : (i + 1) * slab_rows], ("dp", "ctx"), moves)
        wo_grad = piece if wo_grad is None else jnp.where(core == 0, wo_grad, piece)
    wo_grad = wo_grad.astype(F32)

    def expert_grad(left_rows, right_rows, axis):
        hidden = expert_gate.shape[2]
        if axis == 1:
            terms = [dot(left_rows, right_rows[:, i * hidden : (i + 1) * hidden], TN) for i in range(2)]
        else:
            terms = [dot(left_rows[:, i * hidden : (i + 1) * hidden], right_rows, TN) for i in range(2)]
        total = terms[0] + core_swap(terms[1].astype(B16)).astype(F32)
        size = total.shape[axis] // 2
        pieces = (lax.slice_in_dim(total, 0, size, axis=axis), lax.slice_in_dim(total, size, 2 * size, axis=axis))
        away = group_swap(pick(pieces, 1 - group).astype(B16))
        return (pick(pieces, group) + away.astype(F32))[None]

    down_grad_out = expert_grad(act_all, top_all, 0)
    gate_grad_out = expert_grad(x_all, dgate_pre_all, 1)
    up_grad_out = expert_grad(x_all, dup_pre_all, 1)

    def placed(v):
        return lax.dynamic_update_slice(jnp.zeros((width,), F32), v, (chip * 2 * hd,))

    small = sum_all(
        jnp.concatenate(
            [router_term, jnp.stack([ffn_gain_grad, attn_gain, placed(query_gain), placed(key_gain)])], axis=0
        )
    )
    router_sum, gains = small[:experts].T, small[experts:]
    return (
        block_out,
        tokens_grad,
        gains[1],
        gains[2],
        gains[3],
        gains[0],
        wq_grad,
        wk_grad,
        wv_grad,
        wo_grad,
        router_sum,
        gate_grad_out,
        up_grad_out,
        down_grad_out,
    )


def local(*args):
    devices, groups = lax.axis_size("ctx"), lax.axis_size("dp")
    experts, owned = args[11].shape[1], args[12].shape[0]
    fits = devices == HEADS == experts and groups == 2 and owned == 1 and 3 * experts <= LANES
    return (local_fast if fits else local_general)(*args)


def solution(mesh):
    return jax.shard_map(
        local,
        mesh=mesh,
        in_specs=(
            P(("dp", "ctx"), None),
            P(("dp", "ctx")),
            P(("dp", "ctx"), None),
            P(),
            P(),
            P(),
            P(),
            P("ctx", None),
            P("ctx", None),
            P("ctx", None),
            P("ctx", None),
            P(),
            P("ctx", None, None),
            P("ctx", None, None),
            P("ctx", None, None),
            P(("dp", "ctx"), None),
        ),
        out_specs=(
            P(("dp", "ctx"), None),
            P(("dp", "ctx"), None),
            P(),
            P(),
            P(),
            P(),
            P(("dp", "ctx"), None),
            P(("dp", "ctx"), None),
            P(("dp", "ctx"), None),
            P(("dp", "ctx"), None),
            P(),
            P("ctx", None, "dp"),
            P("ctx", None, "dp"),
            P("ctx", "dp", None),
        ),
        check_vma=False,
    )
```

```python
import functools

import jax
import jax.numpy as jnp
from jax import lax
from jax.experimental import pallas as pl
from jax.experimental.pallas import tpu as pltpu
from jax.sharding import PartitionSpec as P

HEADS = 16


EPS = 1e-05
THETA = 10000.0
NEGATIVE = -1e30
HIGH = lax.Precision.HIGHEST


def spread(block, axis, holder):
    block = jnp.where(lax.axis_index(axis) == holder, block, jnp.zeros_like(block))
    return lax.psum(block, axis)


def shifted(shard, axis, by):
    devices = lax.axis_size(axis)
    return lax.ppermute(shard, axis, [(i, (i + by) % devices) for i in range(devices)])


def norm_rows(v, gain):
    return v * lax.rsqrt(jnp.mean(v * v, axis=-1, keepdims=True) + EPS) * gain


def rotate(v, place):
    half = v.shape[-1] // 2
    freq = THETA ** (-jnp.arange(half, dtype=jnp.float32) * 2.0 / v.shape[-1])
    angle = place.astype(jnp.float32)[:, None] * freq[None, :]
    cosine = jnp.cos(angle)[:, None, :]
    sine = jnp.sin(angle)[:, None, :]
    first = v[..., :half]
    second = v[..., half:]
    return jnp.concatenate(
        [first * cosine - second * sine, second * cosine + first * sine], axis=-1
    )


def qk_post(proj, gain, place, heads):
    count, width = proj.shape
    normed = norm_rows(proj, gain).reshape(count, heads, width // heads)
    return rotate(normed, place).reshape(count, width)


def needed(q_place, q_seg, k_place, k_seg):
    return (k_place[0] <= q_place[-1]) & (k_seg[-1] >= q_seg[0])


def pair_mask(q_place, q_seg, k_place, k_seg):
    return (k_place[None, :] <= q_place[:, None]) & (k_seg[None, :] == q_seg[:, None])


def pair_grads(qh, gh, lse, delta, q_place, q_seg, kh, vh, k_place, k_seg, scale, wanted):

    def pair_compute(unused):
        score = jnp.einsum("qhd,khd->hqk", qh, kh, preferred_element_type=jnp.float32) * scale
        mask = pair_mask(q_place, q_seg, k_place, k_seg)
        prob = jnp.where(mask[None], jnp.exp(score - lse[:, :, None]), 0.0)
        dprob = jnp.einsum("qhd,khd->hqk", gh, vh, preferred_element_type=jnp.float32)
        dscore = (prob * (dprob - delta[:, :, None])).astype(jnp.bfloat16)
        prob_low = prob.astype(jnp.bfloat16)
        dq = jnp.einsum("hqk,khd->qhd", dscore, kh, preferred_element_type=jnp.float32) * scale
        dk = jnp.einsum("hqk,qhd->khd", dscore, qh, preferred_element_type=jnp.float32) * scale
        dv = jnp.einsum("hqk,qhd->khd", prob_low, gh, preferred_element_type=jnp.float32)
        return (dq, dk, dv)

    def skip(unused):
        return (
            jnp.zeros(qh.shape, jnp.float32),
            jnp.zeros(kh.shape, jnp.float32),
            jnp.zeros(vh.shape, jnp.float32),
        )

    return lax.cond(wanted, pair_compute, skip, 0)


def local_general(
    tokens,
    doc_starts,
    routes,
    norm_attn,
    norm_query,
    norm_key,
    norm_ffn,
    w_query,
    w_key,
    w_value,
    w_output,
    router,
    expert_gate,
    expert_up,
    expert_down,
    out_grad,
):
    f32 = jnp.float32
    b16 = jnp.bfloat16
    n_ctx = lax.axis_size("ctx")
    rank = lax.axis_index("ctx")
    rows, width = tokens.shape
    heads = HEADS
    head_dim = width // heads
    scale = head_dim ** (-0.5)
    experts = router.shape[1]
    topk = routes.shape[1]
    owned = expert_gate.shape[0]
    cap = max(2, rows * topk * 3 // (2 * experts))
    starts = jnp.sum(doc_starts)
    first_count = spread(starts, "ctx", 0)
    before = jnp.where(rank > 0, first_count, 0)
    seg = before + jnp.cumsum(doc_starts)
    place = rank * rows + jnp.arange(rows, dtype=jnp.int32)
    wq, wk, wv, wo = (
        lax.all_gather(w_query, "ctx", axis=0, tiled=True),
        lax.all_gather(w_key, "ctx", axis=0, tiled=True),
        lax.all_gather(w_value, "ctx", axis=0, tiled=True),
        lax.all_gather(w_output, "ctx", axis=0, tiled=True),
    )
    inputs = tokens.astype(f32)
    n1 = norm_rows(inputs, norm_attn).astype(b16)
    qp = jnp.dot(n1, wq, preferred_element_type=f32)
    kp = jnp.dot(n1, wk, preferred_element_type=f32)
    vp = jnp.dot(n1, wv, preferred_element_type=f32)
    query = qk_post(qp, norm_query, place, heads).astype(b16)
    keys = qk_post(kp, norm_key, place, heads).astype(b16)
    values = vp.astype(b16)
    qh = query.reshape(rows, heads, head_dim)
    start_state = (
        jnp.full((heads, rows), NEGATIVE, f32),
        jnp.zeros((heads, rows), f32),
        jnp.zeros((rows, heads, head_dim), f32),
    )
    k_piece = lax.all_gather(keys, "ctx", axis=0, tiled=True)
    v_piece = lax.all_gather(values, "ctx", axis=0, tiled=True)
    s_piece = lax.all_gather(seg, "ctx", axis=0, tiled=True)
    total_rows = k_piece.shape[0]
    block = min(rows, total_rows)
    count = total_rows // block

    def step(index, state):
        best, total, acc = state
        offset = index * block
        kh = lax.dynamic_slice_in_dim(k_piece, offset, block, 0).reshape(block, heads, head_dim)
        vh = lax.dynamic_slice_in_dim(v_piece, offset, block, 0).reshape(block, heads, head_dim)
        k_seg = lax.dynamic_slice_in_dim(s_piece, offset, block, 0)
        k_place = offset + jnp.arange(block, dtype=jnp.int32)

        def step_compute(unused):
            score = jnp.einsum("qhd,khd->hqk", qh, kh, preferred_element_type=f32) * scale
            mask = pair_mask(place, seg, k_place, k_seg)
            score = jnp.where(mask[None], score, NEGATIVE)
            new_best = jnp.maximum(best, jnp.max(score, axis=-1))
            shrink = jnp.exp(best - new_best)
            prob = jnp.exp(score - new_best[:, :, None])
            new_total = total * shrink + jnp.sum(prob, axis=-1)
            new_acc = acc * shrink.T[:, :, None] + jnp.einsum(
                "hqk,khd->qhd", prob.astype(b16), vh, preferred_element_type=f32
            )
            return (new_best, new_total, new_acc)

        return lax.cond(needed(place, seg, k_place, k_seg), step_compute, lambda unused: state, 0)

    best, total, acc = lax.fori_loop(0, count, step, start_state)
    attn_heads = acc / total.T[:, :, None]
    lse = best + jnp.log(total)
    attn = attn_heads.reshape(rows, width)
    attn_low = attn.astype(b16)
    h1 = inputs + jnp.dot(attn_low, wo, preferred_element_type=f32)
    n2 = norm_rows(h1, norm_ffn).astype(b16)
    probs = jax.nn.softmax(jnp.dot(n2, router, preferred_element_type=f32), axis=-1)
    choice_mask = routes[:, :, None] == jnp.arange(experts, dtype=jnp.int32)[None, None, :]
    gates = jnp.sum(jnp.where(choice_mask, probs[:, None, :], 0.0), axis=-1)
    flat = routes.reshape(-1)
    hits = (flat[:, None] == jnp.arange(experts, dtype=jnp.int32)[None, :]).astype(jnp.int32)
    slot = jnp.sum(jnp.cumsum(hits, axis=0) * hits, axis=1) - 1
    dest = flat * cap + slot
    route_ids = jnp.arange(rows * topk, dtype=jnp.int32)
    source = jnp.zeros((experts * cap,), jnp.int32).at[dest].set(route_ids)
    filled = jnp.zeros((experts * cap,), jnp.bool_).at[dest].set(True)
    send = jnp.where(filled[:, None], n2[source // topk], jnp.zeros((), b16)).reshape(
        experts, cap, width
    )
    received = lax.all_to_all(send, "ctx", split_axis=0, concat_axis=0, tiled=True)
    count = received.shape[1]
    grid = received.reshape(n_ctx, owned, count, width)
    gate_pre = jnp.einsum("secd,edh->sech", grid, expert_gate, preferred_element_type=f32)
    up_pre = jnp.einsum("secd,edh->sech", grid, expert_up, preferred_element_type=f32)
    act = (jax.nn.silu(gate_pre) * up_pre).astype(b16)
    result = jnp.einsum("sech,ehd->secd", act, expert_down, preferred_element_type=f32).astype(b16)
    returned = lax.all_to_all(
        result.reshape(n_ctx * owned, count, width), "ctx", split_axis=0, concat_axis=0, tiled=True
    )
    hidden = gate_pre.shape[-1]
    returned, kept_in, kept_gate, kept_up = (
        returned,
        received,
        gate_pre.reshape(n_ctx * owned, count, hidden),
        up_pre.reshape(n_ctx * owned, count, hidden),
    )
    picked = returned.reshape(experts * cap, width)[dest].reshape(rows, topk, width).astype(f32)
    moe = jnp.einsum("tk,tkd->td", gates, picked, precision=HIGH)
    block_out = (h1 + moe).astype(b16)
    grad_top = out_grad.astype(f32)
    gate_grad = jnp.einsum("td,tkd->tk", grad_top, picked, precision=HIGH)
    down_in = (gates[:, :, None] * grad_top[:, None, :]).astype(b16).reshape(rows * topk, width)
    back_send = jnp.where(filled[:, None], down_in[source], jnp.zeros((), b16)).reshape(
        experts, cap, width
    )
    back_recv = lax.all_to_all(back_send, "ctx", split_axis=0, concat_axis=0, tiled=True)
    hidden = kept_gate.shape[-1]
    grid_dy = back_recv.reshape(n_ctx, owned, cap, width)
    grid_x = kept_in.reshape(n_ctx, owned, cap, width)
    gate_pre = kept_gate.reshape(n_ctx, owned, cap, hidden)
    up_pre = kept_up.reshape(n_ctx, owned, cap, hidden)
    sigma = jax.nn.sigmoid(gate_pre)
    silu = jax.nn.silu(gate_pre)
    act = (silu * up_pre).astype(b16)
    dact = jnp.einsum("secd,ehd->sech", grid_dy, expert_down, preferred_element_type=f32)
    dgate_pre = (dact * up_pre * sigma * (1.0 + gate_pre * (1.0 - sigma))).astype(b16)
    dup_pre = (dact * silu).astype(b16)
    down_term = jnp.einsum("sech,secd->ehd", act, grid_dy, preferred_element_type=f32)
    gate_term = jnp.einsum("secd,sech->edh", grid_x, dgate_pre, preferred_element_type=f32)
    up_term = jnp.einsum("secd,sech->edh", grid_x, dup_pre, preferred_element_type=f32)
    entry_grad = (
        jnp.einsum("sech,edh->secd", dgate_pre, expert_gate, preferred_element_type=f32)
        + jnp.einsum("sech,edh->secd", dup_pre, expert_up, preferred_element_type=f32)
    ).astype(b16)
    entry_back = lax.all_to_all(
        entry_grad.reshape(n_ctx * owned, cap, width),
        "ctx",
        split_axis=0,
        concat_axis=0,
        tiled=True,
    )
    route_grad = jnp.sum(
        entry_back.reshape(experts * cap, width)[dest].reshape(rows, topk, width).astype(f32),
        axis=1,
    )
    gate_grad_out, up_grad_out, down_grad_out = (
        lax.psum_scatter(
            gate_term.astype(jnp.bfloat16), "dp", scatter_dimension=2, tiled=True
        ).astype(jnp.float32),
        lax.psum_scatter(
            up_term.astype(jnp.bfloat16), "dp", scatter_dimension=2, tiled=True
        ).astype(jnp.float32),
        lax.psum_scatter(
            down_term.astype(jnp.bfloat16), "dp", scatter_dimension=1, tiled=True
        ).astype(jnp.float32),
    )
    prob_grad = jnp.sum(jnp.where(choice_mask, gate_grad[:, :, None], 0.0), axis=1)
    logit_grad = probs * (prob_grad - jnp.sum(probs * prob_grad, axis=-1, keepdims=True))
    router_term = jnp.dot(n2.astype(f32).T, logit_grad, precision=HIGH)
    n2_grad = route_grad + jnp.dot(logit_grad, router.astype(f32).T, precision=HIGH)
    unused_value, ffn_back = jax.vjp(norm_rows, h1, norm_ffn)
    h1_part, ffn_gain_grad = ffn_back(n2_grad)
    h1_grad = grad_top + h1_part
    h1_low = h1_grad.astype(b16)
    attn_grad = jnp.dot(h1_low, wo.T, preferred_element_type=f32).astype(b16)
    gh = attn_grad.reshape(rows, heads, head_dim)
    delta = jnp.einsum("qhd,qhd->hq", gh.astype(f32), attn_heads, precision=HIGH)
    local_index = jnp.arange(rows, dtype=jnp.int32)

    def key_step(index, state):
        moving, query_grad = state
        k_move, v_move, s_move, key_acc, value_acc = moving
        anchor = (rank - index + n_ctx) % n_ctx
        k_place = anchor * rows + local_index
        dq, dk, dv = pair_grads(
            qh,
            gh,
            lse,
            delta,
            place,
            seg,
            k_move.astype(b16).reshape(rows, heads, head_dim),
            v_move.astype(b16).reshape(rows, heads, head_dim),
            k_place,
            s_move,
            scale,
            needed(place, seg, k_place, s_move),
        )
        moving = (
            shifted(k_move.astype(jnp.bfloat16), "ctx", 1).astype(k_move.dtype),
            shifted(v_move.astype(jnp.bfloat16), "ctx", 1).astype(v_move.dtype),
            shifted(s_move, "ctx", 1),
            shifted((key_acc + dk.reshape(rows, width)).astype(jnp.bfloat16), "ctx", 1).astype(
                jnp.float32
            ),
            shifted((value_acc + dv.reshape(rows, width)).astype(jnp.bfloat16), "ctx", 1).astype(
                jnp.float32
            ),
        )
        return (moving, query_grad + dq)

    start_keys = (
        (
            keys.astype(f32),
            values.astype(f32),
            seg,
            jnp.zeros((rows, width), f32),
            jnp.zeros((rows, width), f32),
        ),
        jnp.zeros((rows, heads, head_dim), f32),
    )
    (unused_k, unused_v, unused_s, key_grad, value_grad), query_grad = lax.fori_loop(
        0, n_ctx, key_step, start_keys
    )
    query_grad = query_grad.reshape(rows, width)
    unused_query, query_back = jax.vjp(
        lambda proj, gain: qk_post(proj, gain, place, heads), qp, norm_query
    )
    qp_grad, query_gain_grad = query_back(query_grad)
    unused_key, key_back = jax.vjp(
        lambda proj, gain: qk_post(proj, gain, place, heads), kp, norm_key
    )
    kp_grad, key_gain_grad = key_back(key_grad)
    qp_low = qp_grad.astype(b16)
    kp_low = kp_grad.astype(b16)
    vp_low = value_grad.astype(b16)
    n1_grad = (
        jnp.dot(qp_low, wq.T, preferred_element_type=f32)
        + jnp.dot(kp_low, wk.T, preferred_element_type=f32)
        + jnp.dot(vp_low, wv.T, preferred_element_type=f32)
    )
    unused_norm, attn_back = jax.vjp(norm_rows, inputs, norm_attn)
    input_part, attn_gain_grad = attn_back(n1_grad)
    tokens_grad = (h1_grad + input_part).astype(b16)
    contract = (((0,), (0,)), ((), ()))
    stacked = lax.psum_scatter(
        jnp.concatenate(
            [
                lax.dot_general(n1, qp_low, contract, preferred_element_type=f32),
                lax.dot_general(n1, kp_low, contract, preferred_element_type=f32),
                lax.dot_general(n1, vp_low, contract, preferred_element_type=f32),
                lax.dot_general(attn_low, h1_low, contract, preferred_element_type=f32),
            ],
            axis=1,
        ),
        ("dp", "ctx"),
        scatter_dimension=0,
        tiled=True,
    )
    wq_grad = stacked[:, :width]
    wk_grad = stacked[:, width : 2 * width]
    wv_grad = stacked[:, 2 * width : 3 * width]
    wo_grad = stacked[:, 3 * width :]
    attn_gain_sum, query_gain_sum, key_gain_sum, ffn_gain_sum, router_sum = lax.psum(
        (attn_gain_grad, query_gain_grad, key_gain_grad, ffn_gain_grad, router_term), ("dp", "ctx")
    )
    return (
        block_out,
        tokens_grad,
        attn_gain_sum,
        query_gain_sum,
        key_gain_sum,
        ffn_gain_sum,
        wq_grad,
        wk_grad,
        wv_grad,
        wo_grad,
        router_sum,
        gate_grad_out,
        up_grad_out,
        down_grad_out,
    )


B16 = jnp.bfloat16
F32 = jnp.float32
LANES = 128
NT = (((1,), (1,)), ((), ()))
TN = (((0,), (0,)), ((), ()))


def dot(a, b, dims=(((1,), (0,)), ((), ()))):
    return lax.dot_general(a, b, dims, preferred_element_type=F32)


def ring_of(chips):
    return [2 * p if p < chips // 2 else 2 * (chips - 1 - p) + 1 for p in range(chips)]


def rows_of(ids_ref, index, rows, core):
    return pl.ds(pl.multiple_of(ids_ref[1 + index] * (2 * rows) + core * rows, rows), rows)


def column(row):
    return jnp.broadcast_to(row, (row.shape[1], row.shape[1])).T


def rows_sum(v):
    return jnp.sum(v.T, axis=0, keepdims=True)


def joined(refs):
    return jnp.concatenate([r[...] for r in refs], axis=0)


def project_kernel(ids_ref, *refs, first):
    x_refs, (near_own, far_own, near_other, far_other, own_ref, other_ref, square_ref) = refs[:-7], refs[-7:]
    blocks, rows, wide = own_ref.shape
    hd = wide // 3
    x = joined(x_refs)
    half = x.shape[1] // 2
    own = dot(x[:, :half], near_own[...]) + dot(x[:, half:], far_own[...])
    other = dot(x[:, :half], near_other[...]) + dot(x[:, half:], far_other[...])
    own_ref[...] = own.reshape(own_ref.shape)
    other_ref[...] = other.reshape(other_ref.shape)
    square_ref[...] = jnp.zeros_like(square_ref)
    chips = square_ref.shape[0] // 2
    for i in range(blocks):
        at = slice(i * rows, (i + 1) * rows)
        for j in range(2):
            cols = slice(j * hd, (j + 1) * hd)
            total = rows_sum(own[at, cols] * own[at, cols] + other[at, cols] * other[at, cols])
            square_ref[pl.ds(j * chips + ids_ref[1 + first + i], 1)] = total


def turned(v, cosine, sine):
    return v * cosine + pltpu.roll(v, v.shape[1] // 2, 1) * sine


def turned_back(v, cosine, sine):
    return v * cosine + pltpu.roll(v * sine, v.shape[1] // 2, 1)


def head_kernel(ids_ref, *refs, width):
    raw, (total_ref, cos_ref, sin_ref, gain_ref, own_ref, other_ref) = refs[:4], refs[4:]
    chips, rows, wide = own_ref.shape
    hd = wide // 3
    cut = raw[0].shape[0]
    for i in range(chips):
        for h, out in ((0, own_ref), (2, other_ref)):
            src = raw[h][i] if i < cut else raw[h + 1][i - cut]
            for j in range(2):
                scale = column(lax.rsqrt(total_ref[pl.ds(j * chips + ids_ref[1 + i], 1)] / width + EPS))
                v = src[:, j * hd : (j + 1) * hd] * scale * gain_ref[h + j : h + j + 1]
                out[i, :, j * hd : (j + 1) * hd] = turned(v, cos_ref[i], sin_ref[i]).astype(B16)
            out[i, :, 2 * hd :] = src[:, 2 * hd :].astype(B16)


def inner_kernel(ids_ref, grad_own, grad_other, *refs, width):
    raw, (total_ref, cos_ref, sin_ref, gain_ref, inner_ref, out_ref) = refs[:4], refs[4:]
    chips, rows, wide = grad_own.shape
    hd = wide // 3
    cut = raw[0].shape[0]
    out = [jnp.zeros((rows, hd), F32)] * 4
    for i in range(chips):
        for j in range(2):
            cols = slice(j * hd, (j + 1) * hd)
            scale = column(lax.rsqrt(total_ref[pl.ds(j * chips + ids_ref[1 + i], 1)] / width + EPS))
            inner = jnp.zeros((rows, hd), F32)
            for h, grad in ((0, grad_own), (2, grad_other)):
                src = (raw[h][i] if i < cut else raw[h + 1][i - cut])[:, cols]
                v = turned_back(grad[i, :, cols], cos_ref[i], sin_ref[i]) * src
                inner += v * gain_ref[h + j : h + j + 1]
                out[h + j] = out[h + j] + v * scale
            inner_ref[pl.ds(j * chips + ids_ref[1 + i], 1)] = rows_sum(inner)
    out_ref[...] = jnp.concatenate([jnp.sum(v, axis=0, keepdims=True) for v in out] * 2, axis=0)


def finish_kernel(ids_ref, grad_own, grad_other, *refs, width):
    raw, refs = refs[:4], refs[4:]
    total_ref, inner_ref, cos_ref, sin_ref, gain_ref, near_own, far_own, near_other, far_other = refs[:9]
    x_refs, (low_own, low_other, part_ref, sum_ref) = refs[9:-4], refs[-4:]
    chips, rows, wide = grad_own.shape
    hd = wide // 3
    cut = raw[0].shape[0]
    for i in range(chips):
        for j in range(3):
            cols = slice(j * hd, (j + 1) * hd)
            if j < 2:
                at = pl.ds(j * chips + ids_ref[1 + i], 1)
                scale = lax.rsqrt(total_ref[at] / width + EPS)
                inner = column(scale * scale * scale * (inner_ref[at] / width))
                scale = column(scale)
            for h, grad, out in ((0, grad_own, low_own), (2, grad_other, low_other)):
                v = grad[i, :, cols]
                if j < 2:
                    src = (raw[h][i] if i < cut else raw[h + 1][i - cut])[:, cols]
                    v = turned_back(v, cos_ref[i], sin_ref[i])
                    v = scale * (v * gain_ref[h + j : h + j + 1]) - src * inner
                out[i, :, cols] = v.astype(B16)
    x = joined(x_refs)
    half = width // 2
    group = min(4, chips)
    for lo in range(0, chips, group):
        own = low_own[lo : lo + group].reshape(group * rows, wide)
        other = low_other[lo : lo + group].reshape(group * rows, wide)
        for first, w_own, w_other in ((0, near_own, near_other), (half, far_own, far_other)):
            part = dot(own, w_own[...], NT) + dot(other, w_other[...], NT)
            part_ref[lo : lo + group, :, first : first + half] = part.astype(B16).reshape(group, rows, half)
            seen = x[lo * rows : (lo + group) * rows, first : first + half].astype(F32)
            term = jnp.sum((part * seen).reshape(group * rows // 8, 8, half), axis=0)
            if lo == 0:
                sum_ref[:, first : first + half] = term
            else:
                sum_ref[:, first : first + half] += term


def outer_kernel(*refs, count):
    left, x_refs, outs, x_all = refs[:count], refs[count : -count - 1], refs[-count - 1 : -1], refs[-1]
    x_all[...] = joined(x_refs)
    width = x_all.shape[1]
    tile = min(512, width)
    for l_ref, out in zip(left, outs):
        chips, rows, wide = l_ref.shape
        turn = l_ref[...].reshape(chips * rows, wide).astype(F32).T.astype(B16)
        for lo in range(0, width, tile):
            out[:, lo : lo + tile] = dot(turn, x_all[:, lo : lo + tile]).astype(out.dtype)


def head_grad_kernel(*refs):
    x_refs, (w_ref, own_ref, other_ref) = refs[:-3], refs[-3:]
    hd = own_ref.shape[2]
    grad = dot(joined(x_refs), w_ref[...], NT).astype(B16)
    own_ref[...] = grad[:, :hd].reshape(own_ref.shape)
    other_ref[...] = grad[:, hd:].reshape(other_ref.shape)


def on_core(kernel, shapes, operands, flops, scratch=(), light=False):
    scalars = operands[0].dtype == jnp.int32
    memory = [pltpu.SMEM if scalars and i == 0 else pltpu.VMEM for i in range(len(operands))]
    size = sum(v.size * v.dtype.itemsize for v in list(operands) + list(shapes))
    return pl.pallas_call(
        kernel,
        in_specs=[pl.BlockSpec(memory_space=m) for m in memory],
        out_shape=shapes,
        scratch_shapes=scratch,
        compiler_params=pltpu.CompilerParams(vmem_limit_bytes=56 * 2**20),
        cost_estimate=pl.CostEstimate(flops=0 if light else flops, bytes_accessed=0 if light else size, transcendentals=0),
    )(*operands)


def seg_column(row_ref, col_ref, rows):
    for lo in range(0, row_ref.shape[1], rows):
        col_ref[lo : lo + rows] = jnp.concatenate([column(row_ref[:, lo : lo + rows])] * (col_ref.shape[1] // rows), axis=1)


def attention_forward(
    ids_ref, mine_ref, other_ref, seg_row_ref, out_ref, lse_ref, qkv_ref, low_ref, away_ref, seg_col_ref, *, block, scale
):
    chips, rows, hd = mine_ref.shape[0], mine_ref.shape[1], mine_ref.shape[2] // 3
    core = ids_ref[0]
    for i in range(chips):
        qkv_ref[rows_of(ids_ref, i, rows, core)] = mine_ref[i]
        qkv_ref[rows_of(ids_ref, i, rows, 1 - core)] = other_ref[i]
    total = qkv_ref.shape[0]
    seg_column(seg_row_ref, seg_col_ref, rows)
    vt = qkv_ref[:, 2 * hd :].astype(F32).T.astype(B16)
    for index in range(total // block):
        low, high = index * block, (index + 1) * block
        score = dot(qkv_ref[:high, hd : 2 * hd], qkv_ref[low:high, :hd], NT) * scale
        key = lax.broadcasted_iota(jnp.int32, (high, block), 0)
        query = low + lax.broadcasted_iota(jnp.int32, (high, block), 1)
        seen = (key <= query) & (seg_col_ref[:high] == seg_row_ref[:, low:high])
        score = jnp.where(seen, score, NEGATIVE)
        best = jnp.max(score, axis=0, keepdims=True)
        prob = jnp.exp(score - best)
        norm = jnp.sum(prob, axis=0, keepdims=True)
        out = dot(vt[:, :high], prob.astype(B16)) / norm
        out_ref[low:high] = out.T
        lse_ref[:, low:high] = best + jnp.log(norm)
    for i in range(chips):
        low_ref[i] = out_ref[rows_of(ids_ref, i, rows, core)].astype(B16)
        away_ref[i] = out_ref[rows_of(ids_ref, i, rows, 1 - core)].astype(B16)


def attention_backward(
    ids_ref, qkv_ref, *refs, block, scale
):
    out_ref, lse_ref, seg_row_ref, low_ref, away_ref, g_ref, grad_ref, seg_col_ref = refs[4:]
    chips, rows, wide = low_ref.shape
    hd = wide // 3
    core = ids_ref[0]
    cut = refs[0].shape[0]
    for i in range(chips):
        g_ref[rows_of(ids_ref, i, rows, core)] = refs[0][i] if i < cut else refs[1][i - cut]
        g_ref[rows_of(ids_ref, i, rows, 1 - core)] = refs[2][i] if i < cut else refs[3][i - cut]
    total = qkv_ref.shape[0]
    seg_column(seg_row_ref, seg_col_ref, rows)
    kt = qkv_ref[:, hd : 2 * hd].astype(F32).T.astype(B16)
    grad_ref[...] = jnp.zeros_like(grad_ref)
    for index in range(total // block):
        low, high = index * block, (index + 1) * block
        q, g = qkv_ref[low:high, :hd], g_ref[low:high]
        delta = jnp.sum((g.astype(F32) * out_ref[low:high]).T, axis=0, keepdims=True)
        score = dot(qkv_ref[:high, hd : 2 * hd], q, NT) * scale
        key = lax.broadcasted_iota(jnp.int32, (high, block), 0)
        query = low + lax.broadcasted_iota(jnp.int32, (high, block), 1)
        seen = (key <= query) & (seg_col_ref[:high] == seg_row_ref[:, low:high])
        prob = jnp.where(seen, jnp.exp(score - lse_ref[:, low:high]), 0.0)
        dprob = dot(qkv_ref[:high, 2 * hd :], g, NT)
        dscore = (prob * (dprob - delta)).astype(B16)
        grad_ref[:high, hd : 2 * hd] += dot(dscore, q) * scale
        grad_ref[:high, 2 * hd :] += dot(prob.astype(B16), g)
        grad_ref[low:high, :hd] = dot(kt[:, :high], dscore).T * scale
    for i in range(chips):
        low_ref[i] = grad_ref[rows_of(ids_ref, i, rows, core)]
        away_ref[i] = grad_ref[rows_of(ids_ref, i, rows, 1 - core)]


def expert_kernel(ids_ref, *refs, shards, fresh):
    x_refs, refs = refs[:shards], refs[shards:]
    g_refs, refs = refs[:shards], refs[shards:]
    wg_ref, wu_ref, wd_ref = refs[:3]
    refs = refs[3 if fresh else 8 :]
    moe_ref, dx_ref, dgate_ref, ag_ref, dg_ref, du_ref, xs_ref, gs_ref, moe_acc, dx_acc = refs
    expert, step, steps = pl.program_id(0), pl.program_id(1), pl.num_programs(1)
    rows, width = g_refs[0].shape
    first = (expert == 0) & (step == 0)

    @pl.when(first)
    def _():
        for i in range(shards):
            xs_ref[i] = x_refs[i][:, :width]
            gs_ref[i] = g_refs[i][...]
        dgate_ref[...] = jnp.zeros_like(dgate_ref)

    x = xs_ref[...].reshape(shards * rows, width)
    g = gs_ref[...].reshape(shards * rows, width)
    lane = lax.broadcasted_iota(jnp.int32, (rows, LANES), 1)
    mine = (lane < 3 * ids_ref[2]) & (lax.rem(lane, ids_ref[2]) == ids_ref[expert])
    gate = jnp.concatenate(
        [
            jnp.sum(jnp.where(mine, x_refs[i][:, width:].astype(F32), 0.0), axis=1, keepdims=True)
            for i in range(shards)
        ],
        axis=0,
    )
    wg, wu, wd = wg_ref[0], wu_ref[0], wd_ref[0]
    gate_pre = dot(x, wg)
    up_pre = dot(x, wu)
    dact = dot(g, wd, NT)
    sigma = 1.0 / (1.0 + jnp.exp(-gate_pre))
    silu = gate_pre * sigma
    act = silu * up_pre
    part = jnp.sum(act * dact, axis=1, keepdims=True)
    lane = lax.broadcasted_iota(jnp.int32, (shards * rows, LANES), 1)
    dgate_ref[...] += jnp.where(lane == expert, part, 0.0).reshape(dgate_ref.shape)
    act_low = (gate * act).astype(B16)
    dact = gate * dact
    dgate_pre = (dact * up_pre * sigma * (1.0 + gate_pre * (1.0 - sigma))).astype(B16)
    dup_pre = (dact * silu).astype(B16)
    ag_ref[...] = act_low.reshape(ag_ref.shape)
    dg_ref[...] = dgate_pre.reshape(dg_ref.shape)
    du_ref[...] = dup_pre.reshape(du_ref.shape)
    moe = dot(act_low, wd)
    dx = dot(dgate_pre, wg, NT) + dot(dup_pre, wu, NT)

    @pl.when(first)
    def _():
        moe_acc[...] = moe
        dx_acc[...] = dx

    @pl.when(jnp.logical_not(first))
    def _():
        moe_acc[...] += moe
        dx_acc[...] += dx

    @pl.when((expert == pl.num_programs(0) - 1) & (step == steps - 1))
    def _():
        moe_ref[...] = moe_acc[...].astype(B16).reshape(moe_ref.shape)
        dx_ref[...] = dx_acc[...].astype(B16).reshape(dx_ref.shape)


def expert_rows(ids, xs, gs, wg, wu, wd, kept, spot, total):
    shards = len(xs)
    rows, width = gs[0].shape
    pair, _, hidden = wg.shape
    tile = min(512, hidden)
    steps = hidden // tile
    whole = lambda a: pl.BlockSpec(a.shape, lambda e, j, ids: (0, 0))
    flat = pl.BlockSpec((shards, rows, tile), lambda e, j, ids: (spot, 0, e * steps + j))
    full = pl.BlockSpec((shards, rows, width), lambda e, j, ids: (spot, 0, 0))
    alone = pl.BlockSpec((shards, rows, width), lambda e, j, ids: (0, 0, 0))
    in_specs = [whole(a) for a in xs + gs] + [
        pl.BlockSpec((1, width, tile), lambda e, j, ids: (e, 0, j)),
        pl.BlockSpec((1, width, tile), lambda e, j, ids: (e, 0, j)),
        pl.BlockSpec((1, tile, width), lambda e, j, ids: (e, j, 0)),
    ]
    operands = list(xs) + list(gs) + [wg, wu, wd]
    aliases = {}
    if kept is not None:
        base = 1 + len(operands)
        in_specs += [pl.BlockSpec(memory_space=pl.ANY)] * len(kept)
        operands += list(kept)
        aliases = {base + i: 3 + i for i in range(len(kept))}
    kept_hidden = jax.ShapeDtypeStruct((total, rows, pair * hidden), B16)
    kept_width = jax.ShapeDtypeStruct((total, rows, width), B16)
    out = pl.pallas_call(
        functools.partial(expert_kernel, shards=shards, fresh=kept is None),
        grid_spec=pltpu.PrefetchScalarGridSpec(
            num_scalar_prefetch=1,
            grid=(pair, steps),
            in_specs=in_specs,
            out_specs=[
                alone,
                alone,
                pl.BlockSpec((shards, rows, LANES), lambda e, j, ids: (0, 0, 0)),
                flat,
                flat,
                flat,
                full,
                full,
            ],
            scratch_shapes=[
                pltpu.VMEM((shards * rows, width), F32),
                pltpu.VMEM((shards * rows, width), F32),
            ],
        ),
        out_shape=[
            jax.ShapeDtypeStruct((shards, rows, width), B16),
            jax.ShapeDtypeStruct((shards, rows, width), B16),
            jax.ShapeDtypeStruct((shards, rows, LANES), F32),
            kept_hidden,
            kept_hidden,
            kept_hidden,
            kept_width,
            kept_width,
        ],
        input_output_aliases=aliases,
        compiler_params=pltpu.CompilerParams(vmem_limit_bytes=56 * 2**20),
        cost_estimate=pl.CostEstimate(
            flops=12 * shards * rows * width * hidden * pair,
            bytes_accessed=6 * width * hidden * pair,
            transcendentals=shards * rows * hidden * pair,
        ),
    )(ids, *operands)
    return out[0], out[1], out[2], out[3:]


def expert_grad_kernel(left_ref, right_ref, *refs):
    term = dot(left_ref[...], right_ref[...], TN)
    if len(refs) == 2:
        term += refs[0][...].astype(F32)
    refs[-1][...] = term.astype(B16)


def expert_grad_term(left, right, arrived, left_at, right_at, size, across):
    rows = left.shape[0]
    tile = min(512, size)
    high, wide = (size, right.shape[1]) if across else (left.shape[1], size)
    first = left_at // tile
    in_specs = [
        pl.BlockSpec((rows, tile), lambda j: (0, first + j)),
        pl.BlockSpec((rows, wide), lambda j: (0, right_at // size)),
    ]
    block = pl.BlockSpec((tile, wide), lambda j: (j, 0))
    operands = [left, right] + ([] if arrived is None else [arrived])
    return pl.pallas_call(
        expert_grad_kernel,
        grid=(high // tile,),
        in_specs=in_specs + [block] * (len(operands) - 2),
        out_specs=block,
        out_shape=jax.ShapeDtypeStruct((high, wide), B16),
        compiler_params=pltpu.CompilerParams(vmem_limit_bytes=56 * 2**20),
        cost_estimate=pl.CostEstimate(flops=0, bytes_accessed=0, transcendentals=0),
    )(*operands)


def split_three(v):
    high = lax.reduce_precision(v, exponent_bits=8, mantissa_bits=7)
    middle = lax.reduce_precision(v - high, exponent_bits=8, mantissa_bits=7)
    return [part.astype(B16) for part in (high, middle, v - high - middle)]


def local_fast(
    tokens,
    doc_starts,
    routes,
    norm_attn,
    norm_query,
    norm_key,
    norm_ffn,
    w_query,
    w_key,
    w_value,
    w_output,
    router,
    expert_gate,
    expert_up,
    expert_down,
    out_grad,
):
    devices = lax.axis_size("ctx")
    rank = lax.axis_index("ctx")
    group = lax.axis_index("dp")
    chips = devices // 2
    chip, core = rank // 2, rank % 2
    rows, width = tokens.shape
    experts = router.shape[1]
    hd = width // HEADS
    scale = hd ** (-0.5)
    half = chips // 2
    order = ring_of(chips)
    right = [(2 * order[p] + c, 2 * order[(p + 1) % chips] + c) for p in range(chips) for c in range(2)]
    left = [(b, a) for a, b in right]
    place_in_ring = jnp.where(chip % 2 == 0, chip // 2, chips - 1 - chip // 2)
    same_core = [[2 * c + p for c in range(chips)] for p in range(2)]

    def to_right(v):
        return lax.ppermute(v, "ctx", right)

    def to_left(v):
        return lax.ppermute(v, "ctx", left)

    def core_swap(v):
        return lax.ppermute(v, "ctx", [(i, i ^ 1) for i in range(devices)])

    def group_swap(v):
        return lax.ppermute(v, "dp", [(0, 1), (1, 0)])

    def chip_at(offset):
        spot = (place_in_ring + offset + chips) % chips
        return jnp.where(spot < half, 2 * spot, 2 * (chips - 1 - spot) + 1)

    offsets = [0] + [s * o for o in range(1, half) for s in (1, -1)] + [half]

    def after(v, *others):
        return lax.optimization_barrier((v,) + others)[0]

    places = jnp.stack([chip_at(o) for o in offsets])

    def ring_gather(v, ties=(), first=None):
        ties = list(ties) + [()] * half
        cut = v.shape[0] // 32 * 16
        got = {0: v}

        def send(i, one, two):
            if i == 0 and first:
                return first
            one, two = lax.optimization_barrier((one, two) + tuple(ties[i]))[:2]
            return to_right(one), to_left(two)

        for o in range(1, half):
            got[-o], got[o] = send(o - 1, got[-(o - 1)], got[o - 1])
        first, second = send(half - 1, got[-(half - 1)][:cut], got[half - 1][cut:])
        got[half] = jnp.concatenate([first, second], axis=0)
        got["halves"] = (first, second)
        return got

    def in_ring(got):
        return jnp.concatenate([got[o] for o in offsets], axis=0)

    def ring_steps(part, axis):
        far = part(half)
        cut = far.shape[axis] // 2
        a_cut = lambda v: lax.slice_in_dim(v, 0, cut, axis=axis)
        b_cut = lambda v: lax.slice_in_dim(v, cut, v.shape[axis], axis=axis)
        there, back = lax.optimization_barrier((a_cut(far), b_cut(far)))
        there, back = yield to_right(there), to_left(back)
        near, other = part(half - 1), part(1 - half)
        there = jnp.concatenate([a_cut(near) + there, b_cut(near)], axis=axis)
        back = jnp.concatenate([a_cut(other), b_cut(other) + back], axis=axis)
        for o in range(half - 2, 0, -1):
            there, back = lax.optimization_barrier((there, back))
            there, back = yield to_right(there), to_left(back)
            there, back = there + part(o), back + part(-o)
        there, back = lax.optimization_barrier((there, back))
        there, back = yield to_right(there), to_left(back)
        return there.astype(F32) + back.astype(F32) + part(0).astype(F32)

    def tied(values, *others):
        return lax.optimization_barrier(tuple(values) + others)[: len(values)]

    def ring_sum(part, axis, work=()):
        work = list(work) + [()] * half
        ring = ring_steps(part, axis)
        values, token = next(ring), None
        for i in range(half):
            extra = work[i](token) if callable(work[i]) else work[i]
            values = tied(values, *extra)
            token = values[0]
            try:
                values = ring.send(values)
            except StopIteration as end:
                return end.value

    def sum_chips(v):
        step = 2
        while step < devices:
            v = v + lax.ppermute(v, "ctx", [(i, i ^ step) for i in range(devices)])
            step *= 2
        return v

    def by_core(mine, other, axis):
        return jnp.where(core == 0, jnp.stack([mine, other], axis), jnp.stack([other, mine], axis))

    def pick(pair, which):
        return jnp.where(which == 0, pair[0], pair[1])

    def by_parity(v, axis, back=False):
        shape = v.shape
        v = v.reshape(shape[:axis] + ((2, chips, rows) if back else (chips, 2, rows)) + shape[axis + 1 :])
        split = axis if back else axis + 1
        one, two = [lax.index_in_dim(v, i, split, keepdims=False) for i in range(2)]
        one, two = jnp.where(core == 0, one, two), jnp.where(core == 0, two, one)
        return jnp.stack([one, two], axis + 1 if back else axis).reshape(shape)

    wg_pair, wu_pair, wd_pair = [(w, core_swap(w)) for w in (expert_gate, expert_up, expert_down)]

    inputs = tokens.astype(F32)
    n1 = by_parity(norm_rows(inputs, norm_attn).astype(B16), 1)

    slabs = []
    for w in (w_query, w_key, w_value):
        pair = w.reshape(rows, chips, 2, hd)
        slabs.append(jnp.where(group == 0, pair[:, :, 0], pair[:, :, 1]))
    slab = jnp.concatenate(slabs, axis=2).transpose(1, 0, 2)
    first = (to_right(n1), to_left(n1))
    slab = after(slab, *first)
    near_head = lax.all_to_all(slab, "ctx", split_axis=0, concat_axis=0, axis_index_groups=same_core, tiled=True)
    far_head = group_swap(near_head)
    n1_got = {0: n1, -1: first[0], 1: first[1]}
    for o in range(2, half):
        one, two = lax.optimization_barrier((n1_got[1 - o], n1_got[o - 1]) + ((near_head,) if o == 2 else ()))[:2]
        n1_got[-o], n1_got[o] = to_right(one), to_left(two)
    own = jnp.where(core == group, near_head, far_head)
    other = jnp.where(core == group, far_head, near_head)
    w_in = [v.reshape(chips * rows, 3 * hd) for v in (own, core_swap(other), other, core_swap(own))]
    w_out = jnp.concatenate([w_output, core_swap(w_output)], axis=0)

    count = chips * rows
    place = (2 * places[:, None, None] + core) * rows + lax.broadcasted_iota(jnp.int32, (chips, rows, 1), 1)
    freq = THETA ** (-jnp.arange(hd // 2, dtype=F32) * 2.0 / hd)
    angle = place.astype(F32) * freq[None, None, :]
    cosine, sine = jnp.cos(angle), jnp.sin(angle)
    cosine = jnp.concatenate([cosine] * 2, axis=2)
    sine = jnp.concatenate([-sine, sine], axis=2)
    ids = jnp.concatenate([core[None], places]).astype(jnp.int32)
    ranks = (rank, rank ^ 1)
    gains = jnp.stack([lax.dynamic_slice(g, (r * hd,), (hd,)) for r in ranks for g in (norm_query, norm_key)])
    gains = jnp.concatenate([gains, gains], axis=0)
    early, late = offsets[:5], offsets[5:]
    raw, squares = [None] * 4, [None] * 2

    def project(i, shards):
        blocks = (early, late)[i]
        raw[i], raw[i + 2], squares[i] = on_core(
            functools.partial(project_kernel, first=i * len(early)),
            [jax.ShapeDtypeStruct((len(blocks), rows, 3 * hd), F32)] * 2
            + [jax.ShapeDtypeStruct((2 * chips, rows), F32)],
            [ids] + shards + w_in,
            12 * len(blocks) * rows * width * hd,
            light=i == 0,
        )

    project(0, [n1_got[o] for o in early])
    one, two = lax.optimization_barrier((n1_got[1 - half], n1_got[half - 1], squares[0]))[:2]
    cut = rows // 2
    n1_halves = (to_right(one[:cut]), to_left(two[cut:]))
    project(1, [n1_got[o] for o in late if o != half] + list(n1_halves))
    squares = squares[0] + squares[1]
    top = after(out_grad, *n1_halves)
    top_first = (to_right(top), to_left(top))
    flags = lax.dynamic_update_index_in_dim(jnp.zeros((chips, rows), F32), doc_starts.astype(F32), chip, 0)
    total = sum_chips(after(jnp.concatenate([squares, flags], axis=0), *top_first))
    one, two = lax.optimization_barrier(top_first + (total,))[:2]
    top_got = {0: out_grad, -1: top_first[0], 1: top_first[1], -2: to_right(one), 2: to_left(two)}
    heads = on_core(
        functools.partial(head_kernel, width=width),
        [jax.ShapeDtypeStruct((chips, rows, 3 * hd), B16)] * 2,
        [ids] + raw + [total, cosine, sine, gains],
        0,
    )

    flags = total[2 * chips :]
    flags = by_core(flags, core_swap(flags), 1).reshape(devices, rows)
    tri = (lax.broadcasted_iota(jnp.int32, (rows, rows), 0) <= lax.broadcasted_iota(jnp.int32, (rows, rows), 1)).astype(F32)
    before = (
        lax.broadcasted_iota(jnp.int32, (devices, devices), 1) < lax.broadcasted_iota(jnp.int32, (devices, devices), 0)
    ).astype(F32)
    seg = jnp.dot(flags, tri) + jnp.dot(before, jnp.broadcast_to(jnp.sum(flags, axis=1, keepdims=True), (devices, rows)))
    everything = devices * rows
    seg_row = seg.reshape(1, everything)
    block = min(256, everything)
    half_wide = everything * everything // 2
    attn, lse, head_qkv, low_own, low_away = on_core(
        functools.partial(attention_forward, block=block, scale=scale),
        [
            jax.ShapeDtypeStruct((everything, hd), F32),
            jax.ShapeDtypeStruct((1, everything), F32),
            jax.ShapeDtypeStruct((everything, 3 * hd), B16),
            jax.ShapeDtypeStruct((chips, rows, hd), B16),
            jax.ShapeDtypeStruct((chips, rows, hd), B16),
        ],
        [ids, heads[0], core_swap(heads[1]), seg_row],
        8 * half_wide * hd,
        [pltpu.VMEM((everything, block), F32)],
    )
    low_other = after(core_swap(low_away), top_got[2], top_got[-2])
    attn_low = jnp.concatenate([low_own, low_other], axis=2).reshape(count, 2 * hd)
    out_part = dot(attn_low, w_out).astype(B16).reshape(chips, rows, width)
    weights = [jnp.concatenate(pair, axis=0) for pair in (wg_pair, wu_pair, wd_pair)]
    h1 = inputs + ring_sum(
        lambda o: out_part[offsets.index(o)],
        1,
        [(), (weights[0],), (weights[1],), (weights[2],)],
    )

    n2 = norm_rows(h1, norm_ffn).astype(B16)
    probs = jax.nn.softmax(dot(n2, router), axis=-1)
    chosen = jnp.sum(
        (routes[:, :, None] == jnp.arange(experts, dtype=jnp.int32)[None, None, :]).astype(F32), axis=1
    )
    sent = split_three(probs * chosen)
    sent.append(jnp.zeros((rows, LANES - 3 * experts), B16))
    names = jnp.stack([rank, rank ^ 1, jnp.int32(experts)]).astype(jnp.int32)
    moe_part, dn2_part, dgate_part = {}, {}, []
    kept = None

    def run_experts(which, spot):
        moe, dn2, dgate, kept_now = expert_rows(
            names, [n2_got[o] for o in which], [top_got[o] for o in which], *weights, kept, spot, chips
        )
        for i, o in enumerate(which):
            moe_part[o], dn2_part[o] = moe[i], dn2[i]
        dgate_part.append(dgate)
        return kept_now

    n2_got = {0: jnp.concatenate([n2] + sent, axis=1)}
    n2_got[-1], n2_got[1] = to_right(n2_got[0]), to_left(n2_got[0])
    one, two, three, four = lax.optimization_barrier((n2_got[-1], n2_got[1], top_got[-2], top_got[2]))
    n2_got[-2], n2_got[2] = to_right(one), to_left(two)
    top_got[-3], top_got[3] = to_right(three), to_left(four)
    kept = run_experts([0, 1, -1], 0)
    one, two, three, four = lax.optimization_barrier((n2_got[-2], n2_got[2], top_got[-3], top_got[3], kept[0]))[:4]
    n2_got[-3], n2_got[3] = to_right(one), to_left(two)
    top_got[half] = jnp.concatenate([to_right(three[:cut]), to_left(four[cut:])], axis=0)
    kept = run_experts([2, -2], 3)
    one, two = lax.optimization_barrier((n2_got[-3], n2_got[3], kept[0]))[:2]
    n2_got[half] = jnp.concatenate([to_right(one[:cut]), to_left(two[cut:])], axis=0)
    kept = run_experts([3, -3, half], 1)
    kept = [v.reshape(count, -1) for v in kept]
    act_all, dgate_pre_all, dup_pre_all, x_all, top_all = kept

    hidden = expert_gate.shape[2]
    pairs = [(act_all, top_all), (x_all, dgate_pre_all), (x_all, dup_pre_all)]

    def expert_term(i, expert, token, plus):
        left_side, right_side = pairs[i]
        across = i == 0
        at = expert * hidden
        return expert_grad_term(
            after(left_side, token), right_side, plus, at if across else 0, 0 if across else at, hidden, across
        )

    arrived, expert_grads, own_terms = [], [], []

    def own_term(i):
        def run(token):
            own_terms.append(expert_term(i, 0, token, arrived[i]))
            expert_grads.append(
                lax.psum_scatter(own_terms[i], "dp", scatter_dimension=0 if i == 0 else 1, tiled=True)
            )
            return own_terms[-1:]

        return run

    def other_term(i):
        def run(token):
            other = expert_term(i, 1, token, None)
            arrived.append(core_swap(other))
            return (other,)

        return run

    n2_sum = ring_sum(lambda o: dn2_part[o], 1, [(), other_term(0), own_term(0), other_term(1)])

    dgates = jnp.concatenate(dgate_part, axis=0)[:, :, :2].transpose(0, 2, 1)
    spread_out = (places[None, :] == jnp.arange(chips)[:, None]).astype(F32)
    dgates = jnp.dot(spread_out, dgates.reshape(chips, 2 * rows), precision=HIGH)
    dgates = dgates.reshape(chips, 2, rows)
    dgates = jnp.where(core == 0, dgates, dgates[:, ::-1])
    dgates = lax.all_to_all(dgates, "ctx", split_axis=0, concat_axis=0, axis_index_groups=same_core, tiled=True)
    prob_grad = dgates.reshape(experts, rows).T * chosen
    logit_grad = probs * (prob_grad - jnp.sum(probs * prob_grad, axis=-1, keepdims=True))
    router_term = lax.dot_general(logit_grad, n2.astype(F32), TN, precision=HIGH)
    n2_grad = n2_sum + jnp.dot(logit_grad, router.astype(F32).T, precision=HIGH)
    grad_top = out_grad.astype(F32)
    unused_value, ffn_back = jax.vjp(norm_rows, h1, norm_ffn)
    h1_part, ffn_gain_grad = ffn_back(n2_grad)
    h1_grad = grad_top + h1_part
    h1_low = h1_grad.astype(B16)

    grad_parts = [None] * 4

    def head_grad(i, shards):
        blocks = (early, late)[i]
        grad_parts[i], away = on_core(
            head_grad_kernel,
            [jax.ShapeDtypeStruct((len(blocks), rows, hd), B16)] * 2,
            shards + [w_out],
            4 * len(blocks) * rows * width * hd,
        )
        grad_parts[i + 2] = core_swap(away)
        return away

    h1_got = {0: h1_low, -1: to_right(h1_low), 1: to_left(h1_low)}

    def add_step(v, step, token):
        v = after(v, token)
        return v + lax.ppermute(v, "ctx", [(i, i ^ step) for i in range(devices)])

    early_sum = jnp.concatenate([router_term, ffn_gain_grad[None]], axis=0)
    early_sum = early_sum + core_swap(early_sum)
    one, two = tied((h1_got[-1], h1_got[1]), early_sum)
    work = ()
    for o in range(2, half):
        one, two = tied((h1_got[1 - o], h1_got[o - 1]), early_sum, *work)
        h1_got[-o], h1_got[o] = to_right(one), to_left(two)
        early_sum = add_step(early_sum, 2 ** (o - 1), one)
        work = (own_term(1) if o == 2 else other_term(2))(one)
    away = head_grad(0, [h1_got[o] for o in early])
    one, two = tied((h1_got[1 - half], h1_got[half - 1]), early_sum, away, *work)
    cut = rows // 2
    h1_halves = (to_right(one[:cut]), to_left(two[cut:]))
    early_sum = add_step(early_sum, 2 ** (half - 1), one)
    head_grad(1, [h1_got[o] for o in late if o != half] + list(h1_halves))
    moe_ring = ring_steps(lambda o: after(moe_part[o], grad_parts[1]) if o == half else moe_part[o], 1)
    moe_got = next(moe_ring)
    grads_own, grads_away = on_core(
        functools.partial(attention_backward, block=block, scale=scale),
        [jax.ShapeDtypeStruct((chips, rows, 3 * hd), F32)] * 2,
        [ids, head_qkv] + grad_parts + [attn, lse, seg_row],
        20 * half_wide * hd,
        [
            pltpu.VMEM((everything, hd), B16),
            pltpu.VMEM((everything, 3 * hd), F32),
            pltpu.VMEM((everything, block), F32),
        ],
    )
    h1_shards = [h1_got[o] for o in offsets if o != half] + list(h1_halves)
    o_own, o_away = on_core(
        functools.partial(outer_kernel, count=2),
        [jax.ShapeDtypeStruct((hd, width), F32), jax.ShapeDtypeStruct((hd, width), B16)],
        [low_own, after(low_other, grads_own)] + h1_shards,
        4 * count * width * hd,
        [pltpu.VMEM((count, width), B16)],
        True,
    )
    o_head = o_own + core_swap(o_away).astype(F32)
    o_recv = group_swap(o_head.astype(B16))

    moe_got = moe_ring.send(tied(moe_got, grads_own))
    grads = list(tied((grads_own, core_swap(grads_away)), o_own))
    inner, gain_grads = on_core(
        functools.partial(inner_kernel, width=width),
        [jax.ShapeDtypeStruct((2 * chips, rows), F32), jax.ShapeDtypeStruct((8, hd), F32)],
        [ids] + grads + raw + [total, cosine, sine, gains],
        0,
    )
    n1_shards = [n1_got[o] for o in offsets if o != half] + list(n1_halves)
    own_term(2)(inner)
    moe_got = tied(moe_got, gain_grads)
    inner, o_recv, *moe_got = tied((sum_chips(inner), o_recv) + tuple(moe_got))
    o_head = (o_head + o_recv.astype(F32)).astype(B16)
    moe_got = moe_ring.send(tuple(moe_got))
    inner, *moe_got = tied((inner,) + tuple(moe_got), own_terms[2])
    moe_got = moe_ring.send(tuple(moe_got))
    low_grad_own, low_grad_other, n1_part, attn_gain = on_core(
        functools.partial(finish_kernel, width=width),
        [
            jax.ShapeDtypeStruct((chips, rows, 3 * hd), B16),
            jax.ShapeDtypeStruct((chips, rows, 3 * hd), B16),
            jax.ShapeDtypeStruct((chips, rows, width), B16),
            jax.ShapeDtypeStruct((8, width), F32),
        ],
        [ids] + grads + raw + [total, inner, cosine, sine, gains] + w_in + n1_shards,
        12 * count * width * hd,
    )
    attn_gain = by_parity(jnp.sum(attn_gain, axis=0), 0, back=True) / norm_attn

    wo_grad = None
    for i in range(2):
        moves = [
            (g * devices + devices // 2 * g + j, g * devices + 2 * j + i) for g in range(2) for j in range(devices // 2)
        ]
        size = width // (2 * devices)
        piece = lax.ppermute(o_head[i * size : (i + 1) * size], ("dp", "ctx"), moves)
        wo_grad = piece if wo_grad is None else jnp.where(core == 0, wo_grad, piece)
    n1_part, wo_grad, *moe_got = tied((n1_part, wo_grad) + tuple(moe_got))
    try:
        moe_ring.send(tuple(moe_got))
    except StopIteration as end:
        moe_sum = end.value
    wo_grad = wo_grad.astype(F32)

    w_own, w_away = on_core(
        functools.partial(outer_kernel, count=2),
        [jax.ShapeDtypeStruct((3 * hd, width), F32), jax.ShapeDtypeStruct((3 * hd, width), B16)],
        [low_grad_own, after(low_grad_other, n1_part)] + n1_shards,
        12 * count * width * hd,
        [pltpu.VMEM((count, width), B16)],
        True,
    )
    w_away = core_swap(w_away).astype(F32)
    w_head = w_own + jnp.concatenate([w_away[:, width // 2 :], w_away[:, : width // 2]], axis=1)

    def kept_by(which):
        size = width // 4
        return jnp.concatenate(
            [lax.dynamic_slice_in_dim(w_head, i * (width // 2) + which * size, size, 1) for i in range(2)], axis=1
        )

    w_sent = kept_by(1 - group).astype(B16)
    w_mine = kept_by(group) + group_swap(w_sent).astype(F32)
    w_mine = w_mine.T.astype(B16).reshape(2, chips // 2, rows, 3 * hd)
    w_mine = by_core(w_mine[0], w_mine[1], 1).reshape(devices, -1, 3 * hd)
    w_got = lax.all_to_all(w_mine, "ctx", split_axis=0, concat_axis=0, tiled=True)

    def placed(parts):
        out = jnp.zeros((width,), F32)
        for r, v in zip(ranks, parts):
            out = lax.dynamic_update_slice(out, v, (r * hd,))
        return out

    late_sum = jnp.stack([attn_gain, placed(gain_grads[0::2][:2]), placed(gain_grads[1::2][:2])])
    late_sum = [late_sum + core_swap(late_sum)]

    def beside(step, *others):
        def run(token):
            late_sum.append(add_step(late_sum[-1], step, token))
            return (late_sum[-1],) + others

        return run

    n1_grad = ring_sum(
        lambda o: n1_part[offsets.index(o)], 1, [(w_own,)] + [beside(2**i, *([w_sent], [], [w_mine])[i - 1]) for i in range(1, half)]
    )
    late_sum = after(late_sum[-1], n1_grad)
    late_sum = late_sum + group_swap(late_sum)
    early_sum = early_sum + after(group_swap(early_sum), n1_grad)
    expert_grads = lax.optimization_barrier(tuple(expert_grads) + (n1_grad,))[:3]
    down_grad_out, gate_grad_out, up_grad_out = [v.astype(F32)[None] for v in expert_grads]
    w_got = w_got.transpose(1, 0, 2).astype(F32)
    slab_rows = w_got.shape[0]
    wq_grad, wk_grad, wv_grad = [
        w_got[:, :, i * hd : (i + 1) * hd].reshape(slab_rows, width) for i in range(3)
    ]
    n1_grad = by_parity(n1_grad, 1, back=True)
    unused_norm, attn_back = jax.vjp(lambda v: norm_rows(v, norm_attn), inputs)
    (input_part,) = attn_back(n1_grad)
    tokens_grad = (h1_grad + input_part).astype(B16)

    block_out = (h1 + moe_sum).astype(B16)
    router_sum, gain_sums = early_sum[:experts].T, [early_sum[experts]] + [late_sum[i] for i in range(3)]
    return (
        block_out,
        tokens_grad,
        gain_sums[1],
        gain_sums[2],
        gain_sums[3],
        gain_sums[0],
        wq_grad,
        wk_grad,
        wv_grad,
        wo_grad,
        router_sum,
        gate_grad_out,
        up_grad_out,
        down_grad_out,
    )


def local(*args):
    devices, groups = lax.axis_size("ctx"), lax.axis_size("dp")
    experts, owned = args[11].shape[1], args[12].shape[0]
    fits = devices == HEADS == experts and groups == 2 and owned == 1 and 3 * experts <= LANES
    return (local_fast if fits else local_general)(*args)


def solution(mesh):
    return jax.shard_map(
        local,
        mesh=mesh,
        in_specs=(
            P(("dp", "ctx"), None),
            P(("dp", "ctx")),
            P(("dp", "ctx"), None),
            P(),
            P(),
            P(),
            P(),
            P("ctx", None),
            P("ctx", None),
            P("ctx", None),
            P("ctx", None),
            P(),
            P("ctx", None, None),
            P("ctx", None, None),
            P("ctx", None, None),
            P(("dp", "ctx"), None),
        ),
        out_specs=(
            P(("dp", "ctx"), None),
            P(("dp", "ctx"), None),
            P(),
            P(),
            P(),
            P(),
            P(("dp", "ctx"), None),
            P(("dp", "ctx"), None),
            P(("dp", "ctx"), None),
            P(("dp", "ctx"), None),
            P(),
            P("ctx", None, "dp"),
            P("ctx", None, "dp"),
            P("ctx", "dp", None),
        ),
        check_vma=False,
    )
```

```python
import functools

import jax
import jax.numpy as jnp
from jax import lax
from jax.experimental import pallas as pl
from jax.experimental.pallas import tpu as pltpu
from jax.sharding import PartitionSpec as P

HEADS = 16


EPS = 1e-05
THETA = 10000.0
NEGATIVE = -1e30
HIGH = lax.Precision.HIGHEST


def spread(block, axis, holder):
    block = jnp.where(lax.axis_index(axis) == holder, block, jnp.zeros_like(block))
    return lax.psum(block, axis)


def shifted(shard, axis, by):
    devices = lax.axis_size(axis)
    return lax.ppermute(shard, axis, [(i, (i + by) % devices) for i in range(devices)])


def norm_rows(v, gain):
    return v * lax.rsqrt(jnp.mean(v * v, axis=-1, keepdims=True) + EPS) * gain


def rotate(v, place):
    half = v.shape[-1] // 2
    freq = THETA ** (-jnp.arange(half, dtype=jnp.float32) * 2.0 / v.shape[-1])
    angle = place.astype(jnp.float32)[:, None] * freq[None, :]
    cosine = jnp.cos(angle)[:, None, :]
    sine = jnp.sin(angle)[:, None, :]
    first = v[..., :half]
    second = v[..., half:]
    return jnp.concatenate(
        [first * cosine - second * sine, second * cosine + first * sine], axis=-1
    )


def qk_post(proj, gain, place, heads):
    count, width = proj.shape
    normed = norm_rows(proj, gain).reshape(count, heads, width // heads)
    return rotate(normed, place).reshape(count, width)


def needed(q_place, q_seg, k_place, k_seg):
    return (k_place[0] <= q_place[-1]) & (k_seg[-1] >= q_seg[0])


def pair_mask(q_place, q_seg, k_place, k_seg):
    return (k_place[None, :] <= q_place[:, None]) & (k_seg[None, :] == q_seg[:, None])


def pair_grads(qh, gh, lse, delta, q_place, q_seg, kh, vh, k_place, k_seg, scale, wanted):

    def pair_compute(unused):
        score = jnp.einsum("qhd,khd->hqk", qh, kh, preferred_element_type=jnp.float32) * scale
        mask = pair_mask(q_place, q_seg, k_place, k_seg)
        prob = jnp.where(mask[None], jnp.exp(score - lse[:, :, None]), 0.0)
        dprob = jnp.einsum("qhd,khd->hqk", gh, vh, preferred_element_type=jnp.float32)
        dscore = (prob * (dprob - delta[:, :, None])).astype(jnp.bfloat16)
        prob_low = prob.astype(jnp.bfloat16)
        dq = jnp.einsum("hqk,khd->qhd", dscore, kh, preferred_element_type=jnp.float32) * scale
        dk = jnp.einsum("hqk,qhd->khd", dscore, qh, preferred_element_type=jnp.float32) * scale
        dv = jnp.einsum("hqk,qhd->khd", prob_low, gh, preferred_element_type=jnp.float32)
        return (dq, dk, dv)

    def skip(unused):
        return (
            jnp.zeros(qh.shape, jnp.float32),
            jnp.zeros(kh.shape, jnp.float32),
            jnp.zeros(vh.shape, jnp.float32),
        )

    return lax.cond(wanted, pair_compute, skip, 0)


def local_general(
    tokens,
    doc_starts,
    routes,
    norm_attn,
    norm_query,
    norm_key,
    norm_ffn,
    w_query,
    w_key,
    w_value,
    w_output,
    router,
    expert_gate,
    expert_up,
    expert_down,
    out_grad,
):
    f32 = jnp.float32
    b16 = jnp.bfloat16
    n_ctx = lax.axis_size("ctx")
    rank = lax.axis_index("ctx")
    rows, width = tokens.shape
    heads = HEADS
    head_dim = width // heads
    scale = head_dim ** (-0.5)
    experts = router.shape[1]
    topk = routes.shape[1]
    owned = expert_gate.shape[0]
    cap = max(2, rows * topk * 3 // (2 * experts))
    starts = jnp.sum(doc_starts)
    first_count = spread(starts, "ctx", 0)
    before = jnp.where(rank > 0, first_count, 0)
    seg = before + jnp.cumsum(doc_starts)
    place = rank * rows + jnp.arange(rows, dtype=jnp.int32)
    wq, wk, wv, wo = (
        lax.all_gather(w_query, "ctx", axis=0, tiled=True),
        lax.all_gather(w_key, "ctx", axis=0, tiled=True),
        lax.all_gather(w_value, "ctx", axis=0, tiled=True),
        lax.all_gather(w_output, "ctx", axis=0, tiled=True),
    )
    inputs = tokens.astype(f32)
    n1 = norm_rows(inputs, norm_attn).astype(b16)
    qp = jnp.dot(n1, wq, preferred_element_type=f32)
    kp = jnp.dot(n1, wk, preferred_element_type=f32)
    vp = jnp.dot(n1, wv, preferred_element_type=f32)
    query = qk_post(qp, norm_query, place, heads).astype(b16)
    keys = qk_post(kp, norm_key, place, heads).astype(b16)
    values = vp.astype(b16)
    qh = query.reshape(rows, heads, head_dim)
    start_state = (
        jnp.full((heads, rows), NEGATIVE, f32),
        jnp.zeros((heads, rows), f32),
        jnp.zeros((rows, heads, head_dim), f32),
    )
    k_piece = lax.all_gather(keys, "ctx", axis=0, tiled=True)
    v_piece = lax.all_gather(values, "ctx", axis=0, tiled=True)
    s_piece = lax.all_gather(seg, "ctx", axis=0, tiled=True)
    total_rows = k_piece.shape[0]
    block = min(rows, total_rows)
    count = total_rows // block

    def step(index, state):
        best, total, acc = state
        offset = index * block
        kh = lax.dynamic_slice_in_dim(k_piece, offset, block, 0).reshape(block, heads, head_dim)
        vh = lax.dynamic_slice_in_dim(v_piece, offset, block, 0).reshape(block, heads, head_dim)
        k_seg = lax.dynamic_slice_in_dim(s_piece, offset, block, 0)
        k_place = offset + jnp.arange(block, dtype=jnp.int32)

        def step_compute(unused):
            score = jnp.einsum("qhd,khd->hqk", qh, kh, preferred_element_type=f32) * scale
            mask = pair_mask(place, seg, k_place, k_seg)
            score = jnp.where(mask[None], score, NEGATIVE)
            new_best = jnp.maximum(best, jnp.max(score, axis=-1))
            shrink = jnp.exp(best - new_best)
            prob = jnp.exp(score - new_best[:, :, None])
            new_total = total * shrink + jnp.sum(prob, axis=-1)
            new_acc = acc * shrink.T[:, :, None] + jnp.einsum(
                "hqk,khd->qhd", prob.astype(b16), vh, preferred_element_type=f32
            )
            return (new_best, new_total, new_acc)

        return lax.cond(needed(place, seg, k_place, k_seg), step_compute, lambda unused: state, 0)

    best, total, acc = lax.fori_loop(0, count, step, start_state)
    attn_heads = acc / total.T[:, :, None]
    lse = best + jnp.log(total)
    attn = attn_heads.reshape(rows, width)
    attn_low = attn.astype(b16)
    h1 = inputs + jnp.dot(attn_low, wo, preferred_element_type=f32)
    n2 = norm_rows(h1, norm_ffn).astype(b16)
    probs = jax.nn.softmax(jnp.dot(n2, router, preferred_element_type=f32), axis=-1)
    choice_mask = routes[:, :, None] == jnp.arange(experts, dtype=jnp.int32)[None, None, :]
    gates = jnp.sum(jnp.where(choice_mask, probs[:, None, :], 0.0), axis=-1)
    flat = routes.reshape(-1)
    hits = (flat[:, None] == jnp.arange(experts, dtype=jnp.int32)[None, :]).astype(jnp.int32)
    slot = jnp.sum(jnp.cumsum(hits, axis=0) * hits, axis=1) - 1
    dest = flat * cap + slot
    route_ids = jnp.arange(rows * topk, dtype=jnp.int32)
    source = jnp.zeros((experts * cap,), jnp.int32).at[dest].set(route_ids)
    filled = jnp.zeros((experts * cap,), jnp.bool_).at[dest].set(True)
    send = jnp.where(filled[:, None], n2[source // topk], jnp.zeros((), b16)).reshape(
        experts, cap, width
    )
    received = lax.all_to_all(send, "ctx", split_axis=0, concat_axis=0, tiled=True)
    count = received.shape[1]
    grid = received.reshape(n_ctx, owned, count, width)
    gate_pre = jnp.einsum("secd,edh->sech", grid, expert_gate, preferred_element_type=f32)
    up_pre = jnp.einsum("secd,edh->sech", grid, expert_up, preferred_element_type=f32)
    act = (jax.nn.silu(gate_pre) * up_pre).astype(b16)
    result = jnp.einsum("sech,ehd->secd", act, expert_down, preferred_element_type=f32).astype(b16)
    returned = lax.all_to_all(
        result.reshape(n_ctx * owned, count, width), "ctx", split_axis=0, concat_axis=0, tiled=True
    )
    hidden = gate_pre.shape[-1]
    returned, kept_in, kept_gate, kept_up = (
        returned,
        received,
        gate_pre.reshape(n_ctx * owned, count, hidden),
        up_pre.reshape(n_ctx * owned, count, hidden),
    )
    picked = returned.reshape(experts * cap, width)[dest].reshape(rows, topk, width).astype(f32)
    moe = jnp.einsum("tk,tkd->td", gates, picked, precision=HIGH)
    block_out = (h1 + moe).astype(b16)
    grad_top = out_grad.astype(f32)
    gate_grad = jnp.einsum("td,tkd->tk", grad_top, picked, precision=HIGH)
    down_in = (gates[:, :, None] * grad_top[:, None, :]).astype(b16).reshape(rows * topk, width)
    back_send = jnp.where(filled[:, None], down_in[source], jnp.zeros((), b16)).reshape(
        experts, cap, width
    )
    back_recv = lax.all_to_all(back_send, "ctx", split_axis=0, concat_axis=0, tiled=True)
    hidden = kept_gate.shape[-1]
    grid_dy = back_recv.reshape(n_ctx, owned, cap, width)
    grid_x = kept_in.reshape(n_ctx, owned, cap, width)
    gate_pre = kept_gate.reshape(n_ctx, owned, cap, hidden)
    up_pre = kept_up.reshape(n_ctx, owned, cap, hidden)
    sigma = jax.nn.sigmoid(gate_pre)
    silu = jax.nn.silu(gate_pre)
    act = (silu * up_pre).astype(b16)
    dact = jnp.einsum("secd,ehd->sech", grid_dy, expert_down, preferred_element_type=f32)
    dgate_pre = (dact * up_pre * sigma * (1.0 + gate_pre * (1.0 - sigma))).astype(b16)
    dup_pre = (dact * silu).astype(b16)
    down_term = jnp.einsum("sech,secd->ehd", act, grid_dy, preferred_element_type=f32)
    gate_term = jnp.einsum("secd,sech->edh", grid_x, dgate_pre, preferred_element_type=f32)
    up_term = jnp.einsum("secd,sech->edh", grid_x, dup_pre, preferred_element_type=f32)
    entry_grad = (
        jnp.einsum("sech,edh->secd", dgate_pre, expert_gate, preferred_element_type=f32)
        + jnp.einsum("sech,edh->secd", dup_pre, expert_up, preferred_element_type=f32)
    ).astype(b16)
    entry_back = lax.all_to_all(
        entry_grad.reshape(n_ctx * owned, cap, width),
        "ctx",
        split_axis=0,
        concat_axis=0,
        tiled=True,
    )
    route_grad = jnp.sum(
        entry_back.reshape(experts * cap, width)[dest].reshape(rows, topk, width).astype(f32),
        axis=1,
    )
    gate_grad_out, up_grad_out, down_grad_out = (
        lax.psum_scatter(
            gate_term.astype(jnp.bfloat16), "dp", scatter_dimension=2, tiled=True
        ).astype(jnp.float32),
        lax.psum_scatter(
            up_term.astype(jnp.bfloat16), "dp", scatter_dimension=2, tiled=True
        ).astype(jnp.float32),
        lax.psum_scatter(
            down_term.astype(jnp.bfloat16), "dp", scatter_dimension=1, tiled=True
        ).astype(jnp.float32),
    )
    prob_grad = jnp.sum(jnp.where(choice_mask, gate_grad[:, :, None], 0.0), axis=1)
    logit_grad = probs * (prob_grad - jnp.sum(probs * prob_grad, axis=-1, keepdims=True))
    router_term = jnp.dot(n2.astype(f32).T, logit_grad, precision=HIGH)
    n2_grad = route_grad + jnp.dot(logit_grad, router.astype(f32).T, precision=HIGH)
    unused_value, ffn_back = jax.vjp(norm_rows, h1, norm_ffn)
    h1_part, ffn_gain_grad = ffn_back(n2_grad)
    h1_grad = grad_top + h1_part
    h1_low = h1_grad.astype(b16)
    attn_grad = jnp.dot(h1_low, wo.T, preferred_element_type=f32).astype(b16)
    gh = attn_grad.reshape(rows, heads, head_dim)
    delta = jnp.einsum("qhd,qhd->hq", gh.astype(f32), attn_heads, precision=HIGH)
    local_index = jnp.arange(rows, dtype=jnp.int32)

    def key_step(index, state):
        moving, query_grad = state
        k_move, v_move, s_move, key_acc, value_acc = moving
        anchor = (rank - index + n_ctx) % n_ctx
        k_place = anchor * rows + local_index
        dq, dk, dv = pair_grads(
            qh,
            gh,
            lse,
            delta,
            place,
            seg,
            k_move.astype(b16).reshape(rows, heads, head_dim),
            v_move.astype(b16).reshape(rows, heads, head_dim),
            k_place,
            s_move,
            scale,
            needed(place, seg, k_place, s_move),
        )
        moving = (
            shifted(k_move.astype(jnp.bfloat16), "ctx", 1).astype(k_move.dtype),
            shifted(v_move.astype(jnp.bfloat16), "ctx", 1).astype(v_move.dtype),
            shifted(s_move, "ctx", 1),
            shifted((key_acc + dk.reshape(rows, width)).astype(jnp.bfloat16), "ctx", 1).astype(
                jnp.float32
            ),
            shifted((value_acc + dv.reshape(rows, width)).astype(jnp.bfloat16), "ctx", 1).astype(
                jnp.float32
            ),
        )
        return (moving, query_grad + dq)

    start_keys = (
        (
            keys.astype(f32),
            values.astype(f32),
            seg,
            jnp.zeros((rows, width), f32),
            jnp.zeros((rows, width), f32),
        ),
        jnp.zeros((rows, heads, head_dim), f32),
    )
    (unused_k, unused_v, unused_s, key_grad, value_grad), query_grad = lax.fori_loop(
        0, n_ctx, key_step, start_keys
    )
    query_grad = query_grad.reshape(rows, width)
    unused_query, query_back = jax.vjp(
        lambda proj, gain: qk_post(proj, gain, place, heads), qp, norm_query
    )
    qp_grad, query_gain_grad = query_back(query_grad)
    unused_key, key_back = jax.vjp(
        lambda proj, gain: qk_post(proj, gain, place, heads), kp, norm_key
    )
    kp_grad, key_gain_grad = key_back(key_grad)
    qp_low = qp_grad.astype(b16)
    kp_low = kp_grad.astype(b16)
    vp_low = value_grad.astype(b16)
    n1_grad = (
        jnp.dot(qp_low, wq.T, preferred_element_type=f32)
        + jnp.dot(kp_low, wk.T, preferred_element_type=f32)
        + jnp.dot(vp_low, wv.T, preferred_element_type=f32)
    )
    unused_norm, attn_back = jax.vjp(norm_rows, inputs, norm_attn)
    input_part, attn_gain_grad = attn_back(n1_grad)
    tokens_grad = (h1_grad + input_part).astype(b16)
    contract = (((0,), (0,)), ((), ()))
    stacked = lax.psum_scatter(
        jnp.concatenate(
            [
                lax.dot_general(n1, qp_low, contract, preferred_element_type=f32),
                lax.dot_general(n1, kp_low, contract, preferred_element_type=f32),
                lax.dot_general(n1, vp_low, contract, preferred_element_type=f32),
                lax.dot_general(attn_low, h1_low, contract, preferred_element_type=f32),
            ],
            axis=1,
        ),
        ("dp", "ctx"),
        scatter_dimension=0,
        tiled=True,
    )
    wq_grad = stacked[:, :width]
    wk_grad = stacked[:, width : 2 * width]
    wv_grad = stacked[:, 2 * width : 3 * width]
    wo_grad = stacked[:, 3 * width :]
    attn_gain_sum, query_gain_sum, key_gain_sum, ffn_gain_sum, router_sum = lax.psum(
        (attn_gain_grad, query_gain_grad, key_gain_grad, ffn_gain_grad, router_term), ("dp", "ctx")
    )
    return (
        block_out,
        tokens_grad,
        attn_gain_sum,
        query_gain_sum,
        key_gain_sum,
        ffn_gain_sum,
        wq_grad,
        wk_grad,
        wv_grad,
        wo_grad,
        router_sum,
        gate_grad_out,
        up_grad_out,
        down_grad_out,
    )


B16 = jnp.bfloat16
F32 = jnp.float32
LANES = 128
NT = (((1,), (1,)), ((), ()))
TN = (((0,), (0,)), ((), ()))


def dot(a, b, dims=(((1,), (0,)), ((), ()))):
    return lax.dot_general(a, b, dims, preferred_element_type=F32)


def ring_of(chips):
    return [2 * p if p < chips // 2 else 2 * (chips - 1 - p) + 1 for p in range(chips)]


def rows_of(ids_ref, index, rows, core):
    return pl.ds(pl.multiple_of(ids_ref[1 + index] * (2 * rows) + core * rows, rows), rows)


def column(row):
    return jnp.broadcast_to(row, (row.shape[1], row.shape[1])).T


def rows_sum(v):
    return jnp.sum(v.T, axis=0, keepdims=True)


def joined(refs):
    return jnp.concatenate([r[...] for r in refs], axis=0)


def project_kernel(ids_ref, *refs, first):
    x_refs, (near_own, far_own, near_other, far_other, own_ref, other_ref, square_ref) = refs[:-7], refs[-7:]
    blocks, rows, wide = own_ref.shape
    hd = wide // 3
    x = joined(x_refs)
    half = x.shape[1] // 2
    own = dot(x[:, :half], near_own[...]) + dot(x[:, half:], far_own[...])
    other = dot(x[:, :half], near_other[...]) + dot(x[:, half:], far_other[...])
    own_ref[...] = own.reshape(own_ref.shape)
    other_ref[...] = other.reshape(other_ref.shape)
    square_ref[...] = jnp.zeros_like(square_ref)
    chips = square_ref.shape[0] // 2
    for i in range(blocks):
        at = slice(i * rows, (i + 1) * rows)
        for j in range(2):
            cols = slice(j * hd, (j + 1) * hd)
            total = rows_sum(own[at, cols] * own[at, cols] + other[at, cols] * other[at, cols])
            square_ref[pl.ds(j * chips + ids_ref[1 + first + i], 1)] = total


def turned(v, cosine, sine):
    return v * cosine + pltpu.roll(v, v.shape[1] // 2, 1) * sine


def turned_back(v, cosine, sine):
    return v * cosine + pltpu.roll(v * sine, v.shape[1] // 2, 1)


def head_kernel(ids_ref, *refs, width):
    raw, (total_ref, cos_ref, sin_ref, gain_ref, own_ref, other_ref) = refs[:4], refs[4:]
    chips, rows, wide = own_ref.shape
    hd = wide // 3
    cut = raw[0].shape[0]
    for i in range(chips):
        for h, out in ((0, own_ref), (2, other_ref)):
            src = raw[h][i] if i < cut else raw[h + 1][i - cut]
            for j in range(2):
                scale = column(lax.rsqrt(total_ref[pl.ds(j * chips + ids_ref[1 + i], 1)] / width + EPS))
                v = src[:, j * hd : (j + 1) * hd] * scale * gain_ref[h + j : h + j + 1]
                out[i, :, j * hd : (j + 1) * hd] = turned(v, cos_ref[i], sin_ref[i]).astype(B16)
            out[i, :, 2 * hd :] = src[:, 2 * hd :].astype(B16)


def inner_kernel(ids_ref, grad_own, grad_other, *refs, width):
    raw, (total_ref, cos_ref, sin_ref, gain_ref, inner_ref, out_ref) = refs[:4], refs[4:]
    chips, rows, wide = grad_own.shape
    hd = wide // 3
    cut = raw[0].shape[0]
    out = [jnp.zeros((rows, hd), F32)] * 4
    for i in range(chips):
        for j in range(2):
            cols = slice(j * hd, (j + 1) * hd)
            scale = column(lax.rsqrt(total_ref[pl.ds(j * chips + ids_ref[1 + i], 1)] / width + EPS))
            inner = jnp.zeros((rows, hd), F32)
            for h, grad in ((0, grad_own), (2, grad_other)):
                src = (raw[h][i] if i < cut else raw[h + 1][i - cut])[:, cols]
                v = turned_back(grad[i, :, cols].astype(F32), cos_ref[i], sin_ref[i]) * src
                inner += v * gain_ref[h + j : h + j + 1]
                out[h + j] = out[h + j] + v * scale
            inner_ref[pl.ds(j * chips + ids_ref[1 + i], 1)] = rows_sum(inner)
    out_ref[...] = jnp.concatenate([jnp.sum(v, axis=0, keepdims=True) for v in out] * 2, axis=0)


def finish_kernel(ids_ref, grad_own, grad_other, *refs, width):
    raw, refs = refs[:4], refs[4:]
    total_ref, inner_ref, cos_ref, sin_ref, gain_ref, near_own, far_own, near_other, far_other = refs[:9]
    x_refs, (low_own, low_other, part_ref, sum_ref) = refs[9:-4], refs[-4:]
    chips, rows, wide = grad_own.shape
    hd = wide // 3
    cut = raw[0].shape[0]
    for i in range(chips):
        for j in range(3):
            cols = slice(j * hd, (j + 1) * hd)
            if j < 2:
                at = pl.ds(j * chips + ids_ref[1 + i], 1)
                scale = lax.rsqrt(total_ref[at] / width + EPS)
                inner = column(scale * scale * scale * (inner_ref[at] / width))
                scale = column(scale)
            for h, grad, out in ((0, grad_own, low_own), (2, grad_other, low_other)):
                v = grad[i, :, cols].astype(F32)
                if j < 2:
                    src = (raw[h][i] if i < cut else raw[h + 1][i - cut])[:, cols]
                    v = turned_back(v, cos_ref[i], sin_ref[i])
                    v = scale * (v * gain_ref[h + j : h + j + 1]) - src * inner
                out[i, :, cols] = v.astype(B16)
    x = joined(x_refs)
    half = width // 2
    group = min(4, chips)
    for lo in range(0, chips, group):
        own = low_own[lo : lo + group].reshape(group * rows, wide)
        other = low_other[lo : lo + group].reshape(group * rows, wide)
        for first, w_own, w_other in ((0, near_own, near_other), (half, far_own, far_other)):
            part = dot(own, w_own[...], NT) + dot(other, w_other[...], NT)
            part_ref[lo : lo + group, :, first : first + half] = part.astype(B16).reshape(group, rows, half)
            seen = x[lo * rows : (lo + group) * rows, first : first + half].astype(F32)
            term = jnp.sum((part * seen).reshape(group * rows // 8, 8, half), axis=0)
            if lo == 0:
                sum_ref[:, first : first + half] = term
            else:
                sum_ref[:, first : first + half] += term


def outer_kernel(*refs, count):
    outs = refs[-count - 4 : -5] + (refs[-5:-1],)
    left, x_refs, x_all = refs[:count], refs[count : -count - 4], refs[-1]
    x_all[...] = joined(x_refs)
    width = x_all.shape[1]
    tile = min(512, width)
    for l_ref, out in zip(left, outs):
        chips, rows, wide = l_ref.shape
        turn = l_ref[...].reshape(chips * rows, wide).astype(F32).T.astype(B16)
        parts = out if isinstance(out, tuple) else (out,)
        size = parts[0].shape[1]
        for lo in range(0, width, tile):
            parts[lo // size][:, lo % size : lo % size + tile] = dot(turn, x_all[:, lo : lo + tile]).astype(B16 if len(parts) > 1 else out.dtype)


def head_grad_kernel(*refs):
    x_refs, (w_ref, own_ref, other_ref) = refs[:-3], refs[-3:]
    hd = own_ref.shape[2]
    grad = dot(joined(x_refs), w_ref[...], NT).astype(B16)
    own_ref[...] = grad[:, :hd].reshape(own_ref.shape)
    other_ref[...] = grad[:, hd:].reshape(other_ref.shape)


def on_core(kernel, shapes, operands, flops, scratch=()):
    scalars = operands[0].dtype == jnp.int32
    memory = [pltpu.SMEM if scalars and i == 0 else pltpu.VMEM for i in range(len(operands))]
    size = sum(v.size * v.dtype.itemsize for v in list(operands) + jax.tree.leaves(shapes))
    return pl.pallas_call(
        kernel,
        in_specs=[pl.BlockSpec(memory_space=m) for m in memory],
        out_shape=shapes,
        scratch_shapes=scratch,
        compiler_params=pltpu.CompilerParams(vmem_limit_bytes=56 * 2**20),
        cost_estimate=pl.CostEstimate(flops=flops, bytes_accessed=size, transcendentals=0),
    )(*operands)


def seg_column(row_ref, col_ref, rows):
    for lo in range(0, row_ref.shape[1], rows):
        col_ref[lo : lo + rows] = jnp.concatenate([column(row_ref[:, lo : lo + rows])] * (col_ref.shape[1] // rows), axis=1)


def attention_forward(
    ids_ref, mine_ref, other_ref, seg_row_ref, out_ref, lse_ref, qkv_ref, low_ref, away_ref, seg_col_ref, *, block, scale
):
    chips, rows, hd = mine_ref.shape[0], mine_ref.shape[1], mine_ref.shape[2] // 3
    core = ids_ref[0]
    for i in range(chips):
        qkv_ref[rows_of(ids_ref, i, rows, core)] = mine_ref[i]
        qkv_ref[rows_of(ids_ref, i, rows, 1 - core)] = other_ref[i]
    total = qkv_ref.shape[0]
    seg_column(seg_row_ref, seg_col_ref, rows)
    vt = qkv_ref[:, 2 * hd :].astype(F32).T.astype(B16)
    for index in range(total // block):
        low, high = index * block, (index + 1) * block
        score = dot(qkv_ref[:high, hd : 2 * hd], qkv_ref[low:high, :hd], NT) * scale
        key = lax.broadcasted_iota(jnp.int32, (high, block), 0)
        query = low + lax.broadcasted_iota(jnp.int32, (high, block), 1)
        seen = (key <= query) & (seg_col_ref[:high] == seg_row_ref[:, low:high])
        score = jnp.where(seen, score, NEGATIVE)
        best = jnp.max(score, axis=0, keepdims=True)
        prob = jnp.exp(score - best)
        norm = jnp.sum(prob, axis=0, keepdims=True)
        out = dot(vt[:, :high], prob.astype(B16)) / norm
        out_ref[low:high] = out.T
        lse_ref[:, low:high] = best + jnp.log(norm)
    for i in range(chips):
        low_ref[i] = out_ref[rows_of(ids_ref, i, rows, core)].astype(B16)
        away_ref[i] = out_ref[rows_of(ids_ref, i, rows, 1 - core)].astype(B16)


def attention_backward(
    ids_ref, qkv_ref, *refs, block, scale
):
    out_ref, lse_ref, seg_row_ref, low_ref, away_ref, g_ref, grad_ref, seg_col_ref = refs[4:]
    chips, rows, wide = low_ref.shape
    hd = wide // 3
    core = ids_ref[0]
    cut = refs[0].shape[0]
    for i in range(chips):
        g_ref[rows_of(ids_ref, i, rows, core)] = refs[0][i] if i < cut else refs[1][i - cut]
        g_ref[rows_of(ids_ref, i, rows, 1 - core)] = refs[2][i] if i < cut else refs[3][i - cut]
    total = qkv_ref.shape[0]
    seg_column(seg_row_ref, seg_col_ref, rows)
    kt = qkv_ref[:, hd : 2 * hd].astype(F32).T.astype(B16)
    grad_ref[...] = jnp.zeros_like(grad_ref)
    for index in range(total // block):
        low, high = index * block, (index + 1) * block
        q, g = qkv_ref[low:high, :hd], g_ref[low:high]
        delta = jnp.sum((g.astype(F32) * out_ref[low:high]).T, axis=0, keepdims=True)
        score = dot(qkv_ref[:high, hd : 2 * hd], q, NT) * scale
        key = lax.broadcasted_iota(jnp.int32, (high, block), 0)
        query = low + lax.broadcasted_iota(jnp.int32, (high, block), 1)
        seen = (key <= query) & (seg_col_ref[:high] == seg_row_ref[:, low:high])
        prob = jnp.where(seen, jnp.exp(score - lse_ref[:, low:high]), 0.0)
        dprob = dot(qkv_ref[:high, 2 * hd :], g, NT)
        dscore = (prob * (dprob - delta)).astype(B16)
        grad_ref[:high, hd : 2 * hd] += dot(dscore, q) * scale
        grad_ref[:high, 2 * hd :] += dot(prob.astype(B16), g)
        grad_ref[low:high, :hd] = dot(kt[:, :high], dscore).T * scale
    for i in range(chips):
        low_ref[i] = grad_ref[rows_of(ids_ref, i, rows, core)]
        away_ref[i] = grad_ref[rows_of(ids_ref, i, rows, 1 - core)].astype(B16)


def expert_kernel(ids_ref, *refs, shards, experts, fresh):
    x_refs, refs = refs[:shards], refs[shards:]
    g_refs, refs = refs[:shards], refs[shards:]
    wg_ref, wu_ref, wd_ref = refs[:3]
    refs = refs[3 if fresh else 8 :]
    moe_ref, dx_ref, ag_ref, dg_ref, du_ref, xs_ref, gs_ref, moe_acc, dx_acc, dgate_acc = refs
    expert, step, steps = pl.program_id(0), pl.program_id(1), pl.num_programs(1)
    rows, width = g_refs[0].shape
    first = (expert == 0) & (step == 0)

    @pl.when(first)
    def _():
        for i in range(shards):
            xs_ref[i] = x_refs[i][:, :width]
            gs_ref[i] = g_refs[i][...]
        dgate_acc[...] = jnp.zeros_like(dgate_acc)

    x = xs_ref[...].reshape(shards * rows, width)
    g = gs_ref[...].reshape(shards * rows, width)
    lane = lax.broadcasted_iota(jnp.int32, (rows, LANES), 1)
    mine = (lane < 3 * experts) & (lax.rem(lane, experts) == ids_ref[expert])
    gate = jnp.concatenate(
        [
            jnp.sum(jnp.where(mine, x_refs[i][:, width:].astype(F32), 0.0), axis=1, keepdims=True)
            for i in range(shards)
        ],
        axis=0,
    )
    wg, wu, wd = wg_ref[0], wu_ref[0], wd_ref[0]
    gate_pre = dot(x, wg)
    up_pre = dot(x, wu)
    dact = dot(g, wd, NT)
    sigma = 1.0 / (1.0 + jnp.exp(-gate_pre))
    silu = gate_pre * sigma
    act = silu * up_pre
    part = jnp.sum(act * dact, axis=1, keepdims=True)
    lane = lax.broadcasted_iota(jnp.int32, (shards * rows, LANES), 1)
    dgate_acc[...] += jnp.where(lane == ids_ref[expert], part, 0.0)
    act_low = (gate * act).astype(B16)
    dact = gate * dact
    dgate_pre = (dact * up_pre * sigma * (1.0 + gate_pre * (1.0 - sigma))).astype(B16)
    dup_pre = (dact * silu).astype(B16)
    ag_ref[...] = act_low.reshape(ag_ref.shape)
    dg_ref[...] = dgate_pre.reshape(dg_ref.shape)
    du_ref[...] = dup_pre.reshape(du_ref.shape)
    moe = dot(act_low, wd)
    dx = dot(dgate_pre, wg, NT) + dot(dup_pre, wu, NT)

    @pl.when(first)
    def _():
        moe_acc[...] = moe
        dx_acc[...] = dx

    @pl.when(jnp.logical_not(first))
    def _():
        moe_acc[...] += moe
        dx_acc[...] += dx

    @pl.when((expert == pl.num_programs(0) - 1) & (step == steps - 1))
    def _():
        moe_ref[...] = moe_acc[...].astype(B16).reshape(moe_ref.shape)
        dx_ref[:, :, :width] = dx_acc[...].astype(B16).reshape(shards, rows, width)
        rest = dgate_acc[...]
        sent = jnp.zeros_like(rest)
        for i in range(3):
            piece = rest.astype(B16).astype(F32)
            rest -= piece
            sent += pltpu.roll(piece, i * experts, 1) if i else piece
        dx_ref[:, :, width:] = sent.astype(B16).reshape(shards, rows, LANES)


def expert_rows(ids, xs, gs, wg, wu, wd, kept, spot, total, experts):
    shards = len(xs)
    rows, width = gs[0].shape
    pair, _, hidden = wg.shape
    tile = min(512, hidden)
    steps = hidden // tile
    whole = lambda a: pl.BlockSpec(a.shape, lambda e, j, ids: (0, 0))
    flat = pl.BlockSpec((shards, rows, tile), lambda e, j, ids: (spot, 0, e * steps + j))
    full = pl.BlockSpec((shards, rows, width), lambda e, j, ids: (spot, 0, 0))
    alone = pl.BlockSpec((shards, rows, width), lambda e, j, ids: (0, 0, 0))
    in_specs = [whole(a) for a in xs + gs] + [
        pl.BlockSpec((1, width, tile), lambda e, j, ids: (e, 0, j)),
        pl.BlockSpec((1, width, tile), lambda e, j, ids: (e, 0, j)),
        pl.BlockSpec((1, tile, width), lambda e, j, ids: (e, j, 0)),
    ]
    operands = list(xs) + list(gs) + [wg, wu, wd]
    aliases = {}
    if kept is not None:
        base = 1 + len(operands)
        in_specs += [pl.BlockSpec(memory_space=pl.ANY)] * len(kept)
        operands += list(kept)
        aliases = {base + i: 2 + i for i in range(len(kept))}
    kept_hidden = jax.ShapeDtypeStruct((total, rows, pair * hidden), B16)
    kept_width = jax.ShapeDtypeStruct((total, rows, width), B16)
    out = pl.pallas_call(
        functools.partial(expert_kernel, shards=shards, experts=experts, fresh=kept is None),
        grid_spec=pltpu.PrefetchScalarGridSpec(
            num_scalar_prefetch=1,
            grid=(pair, steps),
            in_specs=in_specs,
            out_specs=[
                alone,
                pl.BlockSpec((shards, rows, width + LANES), lambda e, j, ids: (0, 0, 0)),
                flat,
                flat,
                flat,
                full,
                full,
            ],
            scratch_shapes=[
                pltpu.VMEM((shards * rows, width), F32),
                pltpu.VMEM((shards * rows, width), F32),
                pltpu.VMEM((shards * rows, LANES), F32),
            ],
        ),
        out_shape=[
            jax.ShapeDtypeStruct((shards, rows, width), B16),
            jax.ShapeDtypeStruct((shards, rows, width + LANES), B16),
            kept_hidden,
            kept_hidden,
            kept_hidden,
            kept_width,
            kept_width,
        ],
        input_output_aliases=aliases,
        compiler_params=pltpu.CompilerParams(vmem_limit_bytes=56 * 2**20),
        cost_estimate=pl.CostEstimate(
            flops=12 * shards * rows * width * hidden * pair,
            bytes_accessed=6 * width * hidden * pair,
            transcendentals=shards * rows * hidden * pair,
        ),
    )(ids, *operands)
    return out[0], out[1], out[2:]


def rows_grad_kernel(ids_ref, there_ref, back_ref, own_ref, grad_ref, rows_ref, gain_ref, out_ref):
    rows, width = grad_ref.shape
    core, blocks = ids_ref[0], width // rows
    spots, parts = [], []
    total, inner = jnp.zeros((rows, rows), F32), jnp.zeros((rows, rows), F32)
    for i in range(blocks):
        at = slice(i * rows, (i + 1) * rows)
        chip, parity = i % (blocks // 2), core if i < blocks // 2 else 1 - core
        spot = pl.ds(pl.multiple_of((2 * chip + parity) * rows, rows), rows)
        part = there_ref[:, at].astype(F32) + back_ref[:, at].astype(F32) + own_ref[:, at].astype(F32)
        part = part * gain_ref[:, spot]
        v = rows_ref[:, spot].astype(F32)
        total += v * v
        inner += v * part
        spots.append(spot)
        parts.append(part)
    scale = lax.rsqrt(jnp.sum(total, axis=1, keepdims=True) / width + EPS)
    inner = scale * scale * scale * (jnp.sum(inner, axis=1, keepdims=True) / width)
    for spot, part in zip(spots, parts):
        out_ref[:, spot] = (grad_ref[:, spot] + part * scale - rows_ref[:, spot].astype(F32) * inner).astype(B16)


def expert_grad_kernel(left_ref, right_ref, *refs, pieces, whole):
    step = pl.program_id(0)
    term = dot(left_ref[...], right_ref[...], TN)
    for i in range(pieces):

        @pl.when(step == i)
        def _():
            if whole:
                refs[-1][...] = (term + refs[i][...].astype(F32)).astype(B16)
            else:
                refs[i][...] = term.astype(B16)


def expert_grad_term(left, right, arrived, left_at, right_at, size, across):
    rows = left.shape[0]
    high, wide = (size, right.shape[1]) if across else (left.shape[1], size)
    pieces = 4
    tile = high // pieces
    first = left_at // tile
    in_specs = [
        pl.BlockSpec((rows, tile), lambda j: (0, first + j)),
        pl.BlockSpec((rows, wide), lambda j: (0, right_at // size)),
    ]
    fixed = pl.BlockSpec((tile, wide), lambda j: (0, 0))
    whole = arrived is not None
    return pl.pallas_call(
        functools.partial(expert_grad_kernel, pieces=pieces, whole=whole),
        grid=(pieces,),
        in_specs=in_specs + ([fixed] * pieces if whole else []),
        out_specs=pl.BlockSpec((tile, wide), lambda j: (j, 0)) if whole else [fixed] * pieces,
        out_shape=jax.ShapeDtypeStruct((high, wide), B16) if whole else [jax.ShapeDtypeStruct((tile, wide), B16)] * pieces,
        compiler_params=pltpu.CompilerParams(vmem_limit_bytes=56 * 2**20),
        cost_estimate=pl.CostEstimate(
            flops=2 * rows * high * wide, bytes_accessed=2 * (rows * (high + wide) + high * wide), transcendentals=0
        ),
    )(left, right, *(arrived if whole else []))


def split_three(v):
    high = lax.reduce_precision(v, exponent_bits=8, mantissa_bits=7)
    middle = lax.reduce_precision(v - high, exponent_bits=8, mantissa_bits=7)
    return [part.astype(B16) for part in (high, middle, v - high - middle)]


def local_fast(
    tokens,
    doc_starts,
    routes,
    norm_attn,
    norm_query,
    norm_key,
    norm_ffn,
    w_query,
    w_key,
    w_value,
    w_output,
    router,
    expert_gate,
    expert_up,
    expert_down,
    out_grad,
):
    devices = lax.axis_size("ctx")
    rank = lax.axis_index("ctx")
    group = lax.axis_index("dp")
    chips = devices // 2
    chip, core = rank // 2, rank % 2
    rows, width = tokens.shape
    experts = router.shape[1]
    hd = width // HEADS
    scale = hd ** (-0.5)
    half = chips // 2
    order = ring_of(chips)
    right = [(2 * order[p] + c, 2 * order[(p + 1) % chips] + c) for p in range(chips) for c in range(2)]
    left = [(b, a) for a, b in right]
    place_in_ring = jnp.where(chip % 2 == 0, chip // 2, chips - 1 - chip // 2)
    same_core = [[2 * c + p for c in range(chips)] for p in range(2)]

    def to_right(v):
        return lax.ppermute(v, "ctx", right)

    def to_left(v):
        return lax.ppermute(v, "ctx", left)

    def core_swap(v):
        return lax.ppermute(v, "ctx", [(i, i ^ 1) for i in range(devices)])

    def group_swap(v):
        return lax.ppermute(v, "dp", [(0, 1), (1, 0)])

    def chip_at(offset):
        spot = (place_in_ring + offset + chips) % chips
        return jnp.where(spot < half, 2 * spot, 2 * (chips - 1 - spot) + 1)

    offsets = [0] + [s * o for o in range(1, half) for s in (1, -1)] + [half]

    def after(v, *others):
        return lax.optimization_barrier((v,) + others)[0]

    places = jnp.stack([chip_at(o) for o in offsets])

    def ring_gather(v, ties=(), first=None):
        ties = list(ties) + [()] * half
        cut = v.shape[0] // 32 * 16
        got = {0: v}

        def send(i, one, two):
            if i == 0 and first:
                return first
            one, two = lax.optimization_barrier((one, two) + tuple(ties[i]))[:2]
            return to_right(one), to_left(two)

        for o in range(1, half):
            got[-o], got[o] = send(o - 1, got[-(o - 1)], got[o - 1])
        first, second = send(half - 1, got[-(half - 1)][:cut], got[half - 1][cut:])
        got[half] = jnp.concatenate([first, second], axis=0)
        got["halves"] = (first, second)
        return got

    def in_ring(got):
        return jnp.concatenate([got[o] for o in offsets], axis=0)

    def ring_steps(part, axis):
        far = part(half)
        cut = far.shape[axis] // 2 // LANES * LANES
        a_cut = lambda v: lax.slice_in_dim(v, 0, cut, axis=axis)
        b_cut = lambda v: lax.slice_in_dim(v, cut, v.shape[axis], axis=axis)
        there, back = lax.optimization_barrier((a_cut(far), b_cut(far)))
        there, back = yield to_right(there), to_left(back)
        near, other = part(half - 1), part(1 - half)
        there = jnp.concatenate([a_cut(near) + there, b_cut(near)], axis=axis)
        back = jnp.concatenate([a_cut(other), b_cut(other) + back], axis=axis)
        for o in range(half - 2, 0, -1):
            there, back = lax.optimization_barrier((there, back))
            there, back = yield to_right(there), to_left(back)
            there, back = there + part(o), back + part(-o)
        there, back = lax.optimization_barrier((there, back))
        there, back = yield to_right(there), to_left(back)
        return there, back, part(0)

    def tied(values, *others, all_of=False):
        return lax.optimization_barrier(tuple(values) + others)[: None if all_of else len(values)]

    def ring_sum(part, axis, work=()):
        work = list(work) + [None] * half
        ring = ring_steps(part, axis)
        values, token = next(ring), None
        for i in range(half):
            arrays, then = work[i](token) if work[i] else ((), None)
            values = tied(values, *arrays, all_of=True)
            if then:
                then(*values[2:])
            values = values[:2]
            token = values[0]
            try:
                values = ring.send(values)
            except StopIteration as end:
                return end.value

    def total_of(terms):
        return sum(v.astype(F32) for v in terms)

    def sum_chips(v):
        step = 2
        while step < devices:
            v = v + lax.ppermute(v, "ctx", [(i, i ^ step) for i in range(devices)])
            step *= 2
        return v

    def by_core(mine, other, axis):
        return jnp.where(core == 0, jnp.stack([mine, other], axis), jnp.stack([other, mine], axis))

    def pick(pair, which):
        return jnp.where(which == 0, pair[0], pair[1])

    def by_parity(v, axis, back=False):
        shape = v.shape
        v = v.reshape(shape[:axis] + ((2, chips, rows) if back else (chips, 2, rows)) + shape[axis + 1 :])
        split = axis if back else axis + 1
        one, two = [lax.index_in_dim(v, i, split, keepdims=False) for i in range(2)]
        one, two = jnp.where(core == 0, one, two), jnp.where(core == 0, two, one)
        return jnp.stack([one, two], axis + 1 if back else axis).reshape(shape)

    wg_pair, wu_pair, wd_pair = [(w, core_swap(w)) for w in (expert_gate, expert_up, expert_down)]

    inputs = tokens.astype(F32)
    n1 = by_parity(norm_rows(inputs, norm_attn).astype(B16), 1)

    slabs = []
    for w in (w_query, w_key, w_value):
        pair = w.reshape(rows, chips, 2, hd)
        slabs.append(jnp.where(group == 0, pair[:, :, 0], pair[:, :, 1]))
    slab = jnp.concatenate(slabs, axis=2).transpose(1, 0, 2)
    first = (to_right(n1), to_left(n1))
    near_head = lax.all_to_all(slab, "ctx", split_axis=0, concat_axis=0, axis_index_groups=same_core, tiled=True)
    far_head = group_swap(near_head)
    near_head, *first = tied((near_head,) + first)
    n1_got = {0: n1, -1: first[0], 1: first[1]}
    for o in range(2, half):
        one, two = lax.optimization_barrier((n1_got[1 - o], n1_got[o - 1]) + ((near_head,) if o == 2 else ()))[:2]
        n1_got[-o], n1_got[o] = to_right(one), to_left(two)
    own = jnp.where(core == group, near_head, far_head)
    other = jnp.where(core == group, far_head, near_head)
    w_in = [v.reshape(chips * rows, 3 * hd) for v in (own, core_swap(other), other, core_swap(own))]
    w_out = jnp.concatenate([w_output, core_swap(w_output)], axis=0)

    count = chips * rows
    place = (2 * places[:, None, None] + core) * rows + lax.broadcasted_iota(jnp.int32, (chips, rows, 1), 1)
    freq = THETA ** (-jnp.arange(hd // 2, dtype=F32) * 2.0 / hd)
    angle = place.astype(F32) * freq[None, None, :]
    cosine, sine = jnp.cos(angle), jnp.sin(angle)
    cosine = jnp.concatenate([cosine] * 2, axis=2)
    sine = jnp.concatenate([-sine, sine], axis=2)
    ids = jnp.concatenate([core[None], places]).astype(jnp.int32)
    ranks = (rank, rank ^ 1)
    gains = jnp.stack([lax.dynamic_slice(g, (r * hd,), (hd,)) for r in ranks for g in (norm_query, norm_key)])
    gains = jnp.concatenate([gains, gains], axis=0)
    early, late = offsets[:5], offsets[5:]
    raw, squares = [None] * 4, [None] * 2

    def project(i, shards):
        blocks = (early, late)[i]
        raw[i], raw[i + 2], squares[i] = on_core(
            functools.partial(project_kernel, first=i * len(early)),
            [jax.ShapeDtypeStruct((len(blocks), rows, 3 * hd), F32)] * 2
            + [jax.ShapeDtypeStruct((2 * chips, rows), F32)],
            [ids] + shards + w_in,
            12 * len(blocks) * rows * width * hd,
        )

    project(0, [n1_got[o] for o in early])
    one, two = lax.optimization_barrier((n1_got[1 - half], n1_got[half - 1], squares[0]))[:2]
    cut = rows // 2
    n1_halves = (to_right(one[:cut]), to_left(two[cut:]))
    project(1, [n1_got[o] for o in late if o != half] + list(n1_halves))
    squares = squares[0] + squares[1]
    top = after(out_grad, *n1_halves)
    top_first = (to_right(top), to_left(top))
    flags = lax.dynamic_update_index_in_dim(jnp.zeros((chips, rows), F32), doc_starts.astype(F32), chip, 0)
    total = sum_chips(after(jnp.concatenate([squares, flags], axis=0), *top_first))
    one, two = lax.optimization_barrier(top_first + (total,))[:2]
    top_got = {0: out_grad, -1: top_first[0], 1: top_first[1], -2: to_right(one), 2: to_left(two)}
    heads = on_core(
        functools.partial(head_kernel, width=width),
        [jax.ShapeDtypeStruct((chips, rows, 3 * hd), B16)] * 2,
        [ids] + raw + [total, cosine, sine, gains],
        0,
    )

    flags = total[2 * chips :]
    flags = by_core(flags, core_swap(flags), 1).reshape(devices, rows)
    tri = (lax.broadcasted_iota(jnp.int32, (rows, rows), 0) <= lax.broadcasted_iota(jnp.int32, (rows, rows), 1)).astype(F32)
    before = (
        lax.broadcasted_iota(jnp.int32, (devices, devices), 1) < lax.broadcasted_iota(jnp.int32, (devices, devices), 0)
    ).astype(F32)
    seg = jnp.dot(flags, tri) + jnp.dot(before, jnp.broadcast_to(jnp.sum(flags, axis=1, keepdims=True), (devices, rows)))
    everything = devices * rows
    seg_row = seg.reshape(1, everything)
    block = min(256, everything)
    half_wide = everything * everything // 2
    attn, lse, head_qkv, low_own, low_away = on_core(
        functools.partial(attention_forward, block=block, scale=scale),
        [
            jax.ShapeDtypeStruct((everything, hd), F32),
            jax.ShapeDtypeStruct((1, everything), F32),
            jax.ShapeDtypeStruct((everything, 3 * hd), B16),
            jax.ShapeDtypeStruct((chips, rows, hd), B16),
            jax.ShapeDtypeStruct((chips, rows, hd), B16),
        ],
        [ids, heads[0], core_swap(heads[1]), seg_row],
        8 * half_wide * hd,
        [pltpu.VMEM((everything, block), F32)],
    )
    low_other = after(core_swap(low_away), top_got[2], top_got[-2])
    attn_low = jnp.concatenate([low_own, low_other], axis=2).reshape(count, 2 * hd)
    out_part = dot(attn_low, w_out).astype(B16).reshape(chips, rows, width)
    weights = [jnp.concatenate(pair, axis=0) for pair in (wg_pair, wu_pair, wd_pair)]
    h1 = inputs + total_of(
        ring_sum(
            lambda o: out_part[offsets.index(o)], 1, [None] + [lambda token, w=w: ((w,), None) for w in weights]
        )
    )

    n2 = norm_rows(h1, norm_ffn).astype(B16)
    probs = jax.nn.softmax(dot(n2, router), axis=-1)
    chosen = jnp.sum(
        (routes[:, :, None] == jnp.arange(experts, dtype=jnp.int32)[None, None, :]).astype(F32), axis=1
    )
    sent = split_three(probs * chosen)
    sent.append(jnp.zeros((rows, LANES - 3 * experts), B16))
    names = jnp.stack(ranks).astype(jnp.int32)
    moe_part, dn2_part = {}, {}
    kept = None

    def run_experts(which, spot):
        moe, dn2, kept_now = expert_rows(
            names, [n2_got[o] for o in which], [top_got[o] for o in which], *weights, kept, spot, chips, experts
        )
        for i, o in enumerate(which):
            moe_part[o], dn2_part[o] = moe[i], dn2[i]
        return kept_now

    n2_got = {0: jnp.concatenate([n2] + sent, axis=1)}
    n2_got[-1], n2_got[1] = to_right(n2_got[0]), to_left(n2_got[0])
    one, two, three, four = lax.optimization_barrier((n2_got[-1], n2_got[1], top_got[-2], top_got[2]))
    n2_got[-2], n2_got[2] = to_right(one), to_left(two)
    top_got[-3], top_got[3] = to_right(three), to_left(four)
    kept = run_experts([0, 1, -1], 0)
    one, two, three, four = lax.optimization_barrier((n2_got[-2], n2_got[2], top_got[-3], top_got[3], kept[0]))[:4]
    n2_got[-3], n2_got[3] = to_right(one), to_left(two)
    top_got[half] = jnp.concatenate([to_right(three[:cut]), to_left(four[cut:])], axis=0)
    kept = run_experts([2, -2], 3)
    one, two = lax.optimization_barrier((n2_got[-3], n2_got[3], kept[0]))[:2]
    n2_got[half] = jnp.concatenate([to_right(one[:cut]), to_left(two[cut:])], axis=0)
    kept = run_experts([3, -3, half], 1)
    kept = [v.reshape(count, -1) for v in kept]
    act_all, dgate_pre_all, dup_pre_all, x_all, top_all = kept

    hidden = expert_gate.shape[2]
    pairs = [(act_all, top_all), (x_all, dgate_pre_all), (x_all, dup_pre_all)]

    def expert_term(i, expert, token, plus):
        left_side, right_side = pairs[i]
        across = i == 0
        at = expert * hidden
        return expert_grad_term(
            left_side if token is None else after(left_side, token), right_side, plus, at if across else 0, 0 if across else at, hidden, across
        )

    arrived, expert_grads = [], []

    def own_term(i):
        def run(token):
            return (expert_term(i, 0, token, arrived[i]),), then

        def then(mine):
            expert_grads.append(lax.psum_scatter(mine, "dp", scatter_dimension=0 if i == 0 else 1, tiled=True))

        return run

    def other_term(i):
        def run(token):
            return tuple(expert_term(i, 1, token, None)), then

        def then(*other):
            arrived.append([core_swap(v) for v in other])

        return run

    n2_sum = total_of(
        ring_sum(lambda o: dn2_part[o], 1, [other_term(0), other_term(1), own_term(0), other_term(2)])
    )
    dgates = n2_sum[:, width : width + 3 * experts].reshape(rows, 3, experts)
    n2_sum = n2_sum[:, :width]
    prob_grad = (dgates[:, 0] + dgates[:, 1] + dgates[:, 2]) * chosen
    logit_grad = probs * (prob_grad - jnp.sum(probs * prob_grad, axis=-1, keepdims=True))
    router_term = lax.dot_general(logit_grad, n2.astype(F32), TN, precision=HIGH)
    n2_grad = n2_sum + jnp.dot(logit_grad, router.astype(F32).T, precision=HIGH)
    grad_top = out_grad.astype(F32)
    unused_value, ffn_back = jax.vjp(norm_rows, h1, norm_ffn)
    h1_part, ffn_gain_grad = ffn_back(n2_grad)
    h1_grad = grad_top + h1_part
    h1_low = h1_grad.astype(B16)

    grad_parts = [None] * 4

    def head_grad(i, shards):
        blocks = (early, late)[i]
        grad_parts[i], away = on_core(
            head_grad_kernel,
            [jax.ShapeDtypeStruct((len(blocks), rows, hd), B16)] * 2,
            shards + [w_out],
            4 * len(blocks) * rows * width * hd,
        )
        grad_parts[i + 2] = core_swap(away)
        return away

    h1_got = {0: h1_low, -1: to_right(h1_low), 1: to_left(h1_low)}

    def from_across(v, step, token):
        return lax.ppermute(after(v, token), "ctx", [(i, i ^ step) for i in range(devices)])

    early_sum = jnp.concatenate([router_term, ffn_gain_grad[None]], axis=0)
    early_sum = early_sum + core_swap(early_sum)
    one, two = h1_got[-1], h1_got[1]
    for o in range(1, half):
        mine, then = own_term(o)(h1_low if o == 1 else one) if o < 3 else ((), lambda: None)
        h1_got[-o], h1_got[o], *mine = tied((h1_got[-o], h1_got[o]), *mine, all_of=True)
        then(*mine)
        one, two = h1_got[-o], h1_got[o]
        if o < half - 1:
            h1_got[-o - 1], h1_got[o + 1] = to_right(one), to_left(two)
    cut = rows // 2
    h1_halves = (to_right(one[:cut]), to_left(two[cut:]))
    away = head_grad(0, [after(h1_got[0], one)] + [h1_got[o] for o in early[1:]])
    h1_halves = tied(h1_halves, away)
    away = head_grad(1, [h1_got[o] for o in late if o != half] + list(h1_halves))
    moe_ring = ring_steps(lambda o: after(moe_part[o], *h1_halves) if o == half else moe_part[o], 1)
    moe_got = next(moe_ring)
    attn = after(attn, *moe_got)
    moe_got = moe_ring.send(moe_got)
    early_recv = from_across(early_sum, 2, away)
    grads_own, grads_away = on_core(
        functools.partial(attention_backward, block=block, scale=scale),
        [jax.ShapeDtypeStruct((chips, rows, 3 * hd), t) for t in (F32, B16)],
        [ids, head_qkv] + grad_parts + [attn, lse, seg_row],
        20 * half_wide * hd,
        [
            pltpu.VMEM((everything, hd), B16),
            pltpu.VMEM((everything, 3 * hd), F32),
            pltpu.VMEM((everything, block), F32),
        ],
    )
    grads = [grads_own, core_swap(grads_away)]
    inner, gain_grads = on_core(
        functools.partial(inner_kernel, width=width),
        [jax.ShapeDtypeStruct((2 * chips, rows), F32), jax.ShapeDtypeStruct((8, hd), F32)],
        [ids] + grads + raw + [total, cosine, sine, gains],
        0,
    )
    n1_shards = [n1_got[o] for o in offsets if o != half] + list(n1_halves)
    h1_shards = [h1_got[o] for o in offsets if o != half] + list(h1_halves)
    o_own, *o_away = on_core(
        functools.partial(outer_kernel, count=2),
        [jax.ShapeDtypeStruct((hd, width), F32)] + [jax.ShapeDtypeStruct((hd, width // 4), B16)] * 4,
        [low_own, after(low_other, gain_grads)] + h1_shards,
        4 * count * width * hd,
        [pltpu.VMEM((count, width), B16)],
    )
    o_head = o_own + jnp.concatenate([core_swap(v) for v in o_away], axis=1).astype(F32)
    o_recv = group_swap(o_head.astype(B16))

    early_recv, *moe_got = tied((early_recv,) + tuple(moe_got), grads_own)
    moe_got = moe_ring.send(tuple(moe_got))
    early_sum = early_sum + early_recv
    early_recv = from_across(early_sum, 4, grads_own)
    inner, *moe_got = tied((inner,) + tuple(moe_got), o_own)
    inner = sum_chips(inner)
    moe_got = moe_ring.send(tied(moe_got, inner))
    early_sum = early_sum + after(early_recv, inner)
    early_recv = from_across(early_sum, 8, inner)
    low_grad_own, low_grad_other, n1_part, attn_gain = on_core(
        functools.partial(finish_kernel, width=width),
        [
            jax.ShapeDtypeStruct((chips, rows, 3 * hd), B16),
            jax.ShapeDtypeStruct((chips, rows, 3 * hd), B16),
            jax.ShapeDtypeStruct((chips, rows, width), B16),
            jax.ShapeDtypeStruct((8, width), F32),
        ],
        [ids] + grads + raw + [total, inner, cosine, sine, gains] + w_in + n1_shards,
        12 * count * width * hd,
    )
    attn_gain = by_parity(jnp.sum(attn_gain, axis=0), 0, back=True) / norm_attn

    n1_part, *moe_got = tied((n1_part,) + tuple(moe_got))
    try:
        moe_ring.send(tuple(moe_got))
    except StopIteration as end:
        moe_sum = total_of(end.value)

    def heads_grads(token):
        return on_core(
            functools.partial(outer_kernel, count=2),
            [jax.ShapeDtypeStruct((3 * hd, width), F32)] + [jax.ShapeDtypeStruct((3 * hd, width // 4), B16)] * 4,
            [low_grad_own, after(low_grad_other, token)] + n1_shards,
            12 * count * width * hd,
            [pltpu.VMEM((count, width), B16)],
        )

    def placed(parts):
        out = jnp.zeros((width,), F32)
        for r, v in zip(ranks, parts):
            out = lax.dynamic_update_slice(out, v, (r * hd,))
        return out

    gain_grads = after(gain_grads, n1_part)
    late_sum = jnp.stack([attn_gain, placed(gain_grads[0::2][:2]), placed(gain_grads[1::2][:2])])
    late_sum = [late_sum + core_swap(late_sum)]
    w_got, grads_out = [], []

    def kept_by(which):
        size = width // 4
        return jnp.concatenate(
            [lax.dynamic_slice_in_dim(w_got[0], i * (width // 2) + which * size, size, 1) for i in range(2)], axis=1
        )

    early = []

    def swap_heads(early_recv, w_own, *w_away):
        early.append(group_swap(early_sum + early_recv))
        early.append(early_sum + early_recv)
        w_away = [core_swap(v) for v in w_away]
        w_got.append(w_own + jnp.concatenate(w_away[2:] + w_away[:2], axis=1).astype(F32))
        w_got.append(group_swap(kept_by(1 - group).astype(B16)))

    def in_slabs(w_mine):
        w_mine = w_mine.T.astype(B16).reshape(2, chips // 2, rows, 3 * hd)
        return by_core(w_mine[0], w_mine[1], 1).reshape(devices, -1, 3 * hd)

    def join(w_mine):
        w_got.append(lax.all_to_all(w_mine, "ctx", split_axis=0, concat_axis=0, tiled=True))

    def small_step(step, others=lambda token: (), then=None):
        def run(token):
            return (from_across(late_sum[-1], step, token),) + tuple(others(token)), finish

        def finish(v, *rest):
            late_sum.append(late_sum[-1] + v)
            if then:
                then(*rest)

        return run

    n1_grad = ring_sum(
        lambda o: n1_part[offsets.index(o)],
        1,
        [
            None,
            small_step(2, lambda token: [early_recv] + list(heads_grads(token)), swap_heads),
            small_step(4, lambda token: [in_slabs(kept_by(group) + after(w_got[1], token).astype(F32))], join),
            small_step(
                8,
                lambda token: w_got[2:] + [v.astype(F32)[None] for v in tied(expert_grads, token)],
                lambda w, *v: grads_out.extend((w,) + v),
            ),
        ],
    )
    w_got, down_grad_out, gate_grad_out, up_grad_out = grads_out
    o_head = (o_head + after(o_recv, n1_grad[0]).astype(F32)).astype(B16)
    wo_grad = None
    for i in range(2):
        moves = [
            (g * devices + devices // 2 * g + j, g * devices + 2 * j + i) for g in range(2) for j in range(devices // 2)
        ]
        size = width // (2 * devices)
        piece = lax.ppermute(o_head[i * size : (i + 1) * size], ("dp", "ctx"), moves)
        wo_grad = piece if wo_grad is None else jnp.where(core == 0, wo_grad, piece)
    wo_grad = wo_grad.astype(F32)
    late_sum = after(late_sum[-1], n1_grad[0])
    late_sum = late_sum + group_swap(late_sum)
    early_sum = early[1] + after(early[0], n1_grad[0])
    w_got = w_got.transpose(1, 0, 2).astype(F32)
    slab_rows = w_got.shape[0]
    wq_grad, wk_grad, wv_grad = [
        w_got[:, :, i * hd : (i + 1) * hd].reshape(slab_rows, width) for i in range(3)
    ]
    tokens_grad = on_core(
        rows_grad_kernel,
        jax.ShapeDtypeStruct((rows, width), B16),
        [ids, *n1_grad, h1_grad, tokens, norm_attn.reshape(1, width)],
        0,
    )

    block_out = (h1 + moe_sum).astype(B16)
    router_sum, gain_sums = early_sum[:experts].T, [early_sum[experts]] + [late_sum[i] for i in range(3)]
    return (
        block_out,
        tokens_grad,
        gain_sums[1],
        gain_sums[2],
        gain_sums[3],
        gain_sums[0],
        wq_grad,
        wk_grad,
        wv_grad,
        wo_grad,
        router_sum,
        gate_grad_out,
        up_grad_out,
        down_grad_out,
    )


def local(*args):
    devices, groups = lax.axis_size("ctx"), lax.axis_size("dp")
    experts, owned = args[11].shape[1], args[12].shape[0]
    fits = devices == HEADS == experts and groups == 2 and owned == 1 and 3 * experts <= LANES
    return (local_fast if fits else local_general)(*args)


def solution(mesh):
    return jax.shard_map(
        local,
        mesh=mesh,
        in_specs=(
            P(("dp", "ctx"), None),
            P(("dp", "ctx")),
            P(("dp", "ctx"), None),
            P(),
            P(),
            P(),
            P(),
            P("ctx", None),
            P("ctx", None),
            P("ctx", None),
            P("ctx", None),
            P(),
            P("ctx", None, None),
            P("ctx", None, None),
            P("ctx", None, None),
            P(("dp", "ctx"), None),
        ),
        out_specs=(
            P(("dp", "ctx"), None),
            P(("dp", "ctx"), None),
            P(),
            P(),
            P(),
            P(),
            P(("dp", "ctx"), None),
            P(("dp", "ctx"), None),
            P(("dp", "ctx"), None),
            P(("dp", "ctx"), None),
            P(),
            P("ctx", None, "dp"),
            P("ctx", None, "dp"),
            P("ctx", "dp", None),
        ),
        check_vma=False,
    )
```

```python
import functools

import jax
import jax.numpy as jnp
from jax import lax
from jax.experimental import pallas as pl
from jax.experimental.pallas import tpu as pltpu
from jax.sharding import PartitionSpec as P

HEADS = 16


EPS = 1e-05
THETA = 10000.0
NEGATIVE = -1e30
HIGH = lax.Precision.HIGHEST


def spread(block, axis, holder):
    block = jnp.where(lax.axis_index(axis) == holder, block, jnp.zeros_like(block))
    return lax.psum(block, axis)


def shifted(shard, axis, by):
    devices = lax.axis_size(axis)
    return lax.ppermute(shard, axis, [(i, (i + by) % devices) for i in range(devices)])


def norm_rows(v, gain):
    return v * lax.rsqrt(jnp.mean(v * v, axis=-1, keepdims=True) + EPS) * gain


def rotate(v, place):
    half = v.shape[-1] // 2
    freq = THETA ** (-jnp.arange(half, dtype=jnp.float32) * 2.0 / v.shape[-1])
    angle = place.astype(jnp.float32)[:, None] * freq[None, :]
    cosine = jnp.cos(angle)[:, None, :]
    sine = jnp.sin(angle)[:, None, :]
    first = v[..., :half]
    second = v[..., half:]
    return jnp.concatenate(
        [first * cosine - second * sine, second * cosine + first * sine], axis=-1
    )


def qk_post(proj, gain, place, heads):
    count, width = proj.shape
    normed = norm_rows(proj, gain).reshape(count, heads, width // heads)
    return rotate(normed, place).reshape(count, width)


def needed(q_place, q_seg, k_place, k_seg):
    return (k_place[0] <= q_place[-1]) & (k_seg[-1] >= q_seg[0])


def pair_mask(q_place, q_seg, k_place, k_seg):
    return (k_place[None, :] <= q_place[:, None]) & (k_seg[None, :] == q_seg[:, None])


def pair_grads(qh, gh, lse, delta, q_place, q_seg, kh, vh, k_place, k_seg, scale, wanted):

    def pair_compute(unused):
        score = jnp.einsum("qhd,khd->hqk", qh, kh, preferred_element_type=jnp.float32) * scale
        mask = pair_mask(q_place, q_seg, k_place, k_seg)
        prob = jnp.where(mask[None], jnp.exp(score - lse[:, :, None]), 0.0)
        dprob = jnp.einsum("qhd,khd->hqk", gh, vh, preferred_element_type=jnp.float32)
        dscore = (prob * (dprob - delta[:, :, None])).astype(jnp.bfloat16)
        prob_low = prob.astype(jnp.bfloat16)
        dq = jnp.einsum("hqk,khd->qhd", dscore, kh, preferred_element_type=jnp.float32) * scale
        dk = jnp.einsum("hqk,qhd->khd", dscore, qh, preferred_element_type=jnp.float32) * scale
        dv = jnp.einsum("hqk,qhd->khd", prob_low, gh, preferred_element_type=jnp.float32)
        return (dq, dk, dv)

    def skip(unused):
        return (
            jnp.zeros(qh.shape, jnp.float32),
            jnp.zeros(kh.shape, jnp.float32),
            jnp.zeros(vh.shape, jnp.float32),
        )

    return lax.cond(wanted, pair_compute, skip, 0)


def local_general(
    tokens,
    doc_starts,
    routes,
    norm_attn,
    norm_query,
    norm_key,
    norm_ffn,
    w_query,
    w_key,
    w_value,
    w_output,
    router,
    expert_gate,
    expert_up,
    expert_down,
    out_grad,
):
    f32 = jnp.float32
    b16 = jnp.bfloat16
    n_ctx = lax.axis_size("ctx")
    rank = lax.axis_index("ctx")
    rows, width = tokens.shape
    heads = HEADS
    head_dim = width // heads
    scale = head_dim ** (-0.5)
    experts = router.shape[1]
    topk = routes.shape[1]
    owned = expert_gate.shape[0]
    cap = max(2, rows * topk * 3 // (2 * experts))
    starts = jnp.sum(doc_starts)
    first_count = spread(starts, "ctx", 0)
    before = jnp.where(rank > 0, first_count, 0)
    seg = before + jnp.cumsum(doc_starts)
    place = rank * rows + jnp.arange(rows, dtype=jnp.int32)
    wq, wk, wv, wo = (
        lax.all_gather(w_query, "ctx", axis=0, tiled=True),
        lax.all_gather(w_key, "ctx", axis=0, tiled=True),
        lax.all_gather(w_value, "ctx", axis=0, tiled=True),
        lax.all_gather(w_output, "ctx", axis=0, tiled=True),
    )
    inputs = tokens.astype(f32)
    n1 = norm_rows(inputs, norm_attn).astype(b16)
    qp = jnp.dot(n1, wq, preferred_element_type=f32)
    kp = jnp.dot(n1, wk, preferred_element_type=f32)
    vp = jnp.dot(n1, wv, preferred_element_type=f32)
    query = qk_post(qp, norm_query, place, heads).astype(b16)
    keys = qk_post(kp, norm_key, place, heads).astype(b16)
    values = vp.astype(b16)
    qh = query.reshape(rows, heads, head_dim)
    start_state = (
        jnp.full((heads, rows), NEGATIVE, f32),
        jnp.zeros((heads, rows), f32),
        jnp.zeros((rows, heads, head_dim), f32),
    )
    k_piece = lax.all_gather(keys, "ctx", axis=0, tiled=True)
    v_piece = lax.all_gather(values, "ctx", axis=0, tiled=True)
    s_piece = lax.all_gather(seg, "ctx", axis=0, tiled=True)
    total_rows = k_piece.shape[0]
    block = min(rows, total_rows)
    count = total_rows // block

    def step(index, state):
        best, total, acc = state
        offset = index * block
        kh = lax.dynamic_slice_in_dim(k_piece, offset, block, 0).reshape(block, heads, head_dim)
        vh = lax.dynamic_slice_in_dim(v_piece, offset, block, 0).reshape(block, heads, head_dim)
        k_seg = lax.dynamic_slice_in_dim(s_piece, offset, block, 0)
        k_place = offset + jnp.arange(block, dtype=jnp.int32)

        def step_compute(unused):
            score = jnp.einsum("qhd,khd->hqk", qh, kh, preferred_element_type=f32) * scale
            mask = pair_mask(place, seg, k_place, k_seg)
            score = jnp.where(mask[None], score, NEGATIVE)
            new_best = jnp.maximum(best, jnp.max(score, axis=-1))
            shrink = jnp.exp(best - new_best)
            prob = jnp.exp(score - new_best[:, :, None])
            new_total = total * shrink + jnp.sum(prob, axis=-1)
            new_acc = acc * shrink.T[:, :, None] + jnp.einsum(
                "hqk,khd->qhd", prob.astype(b16), vh, preferred_element_type=f32
            )
            return (new_best, new_total, new_acc)

        return lax.cond(needed(place, seg, k_place, k_seg), step_compute, lambda unused: state, 0)

    best, total, acc = lax.fori_loop(0, count, step, start_state)
    attn_heads = acc / total.T[:, :, None]
    lse = best + jnp.log(total)
    attn = attn_heads.reshape(rows, width)
    attn_low = attn.astype(b16)
    h1 = inputs + jnp.dot(attn_low, wo, preferred_element_type=f32)
    n2 = norm_rows(h1, norm_ffn).astype(b16)
    probs = jax.nn.softmax(jnp.dot(n2, router, preferred_element_type=f32), axis=-1)
    choice_mask = routes[:, :, None] == jnp.arange(experts, dtype=jnp.int32)[None, None, :]
    gates = jnp.sum(jnp.where(choice_mask, probs[:, None, :], 0.0), axis=-1)
    flat = routes.reshape(-1)
    hits = (flat[:, None] == jnp.arange(experts, dtype=jnp.int32)[None, :]).astype(jnp.int32)
    slot = jnp.sum(jnp.cumsum(hits, axis=0) * hits, axis=1) - 1
    dest = flat * cap + slot
    route_ids = jnp.arange(rows * topk, dtype=jnp.int32)
    source = jnp.zeros((experts * cap,), jnp.int32).at[dest].set(route_ids)
    filled = jnp.zeros((experts * cap,), jnp.bool_).at[dest].set(True)
    send = jnp.where(filled[:, None], n2[source // topk], jnp.zeros((), b16)).reshape(
        experts, cap, width
    )
    received = lax.all_to_all(send, "ctx", split_axis=0, concat_axis=0, tiled=True)
    count = received.shape[1]
    grid = received.reshape(n_ctx, owned, count, width)
    gate_pre = jnp.einsum("secd,edh->sech", grid, expert_gate, preferred_element_type=f32)
    up_pre = jnp.einsum("secd,edh->sech", grid, expert_up, preferred_element_type=f32)
    act = (jax.nn.silu(gate_pre) * up_pre).astype(b16)
    result = jnp.einsum("sech,ehd->secd", act, expert_down, preferred_element_type=f32).astype(b16)
    returned = lax.all_to_all(
        result.reshape(n_ctx * owned, count, width), "ctx", split_axis=0, concat_axis=0, tiled=True
    )
    hidden = gate_pre.shape[-1]
    returned, kept_in, kept_gate, kept_up = (
        returned,
        received,
        gate_pre.reshape(n_ctx * owned, count, hidden),
        up_pre.reshape(n_ctx * owned, count, hidden),
    )
    picked = returned.reshape(experts * cap, width)[dest].reshape(rows, topk, width).astype(f32)
    moe = jnp.einsum("tk,tkd->td", gates, picked, precision=HIGH)
    block_out = (h1 + moe).astype(b16)
    grad_top = out_grad.astype(f32)
    gate_grad = jnp.einsum("td,tkd->tk", grad_top, picked, precision=HIGH)
    down_in = (gates[:, :, None] * grad_top[:, None, :]).astype(b16).reshape(rows * topk, width)
    back_send = jnp.where(filled[:, None], down_in[source], jnp.zeros((), b16)).reshape(
        experts, cap, width
    )
    back_recv = lax.all_to_all(back_send, "ctx", split_axis=0, concat_axis=0, tiled=True)
    hidden = kept_gate.shape[-1]
    grid_dy = back_recv.reshape(n_ctx, owned, cap, width)
    grid_x = kept_in.reshape(n_ctx, owned, cap, width)
    gate_pre = kept_gate.reshape(n_ctx, owned, cap, hidden)
    up_pre = kept_up.reshape(n_ctx, owned, cap, hidden)
    sigma = jax.nn.sigmoid(gate_pre)
    silu = jax.nn.silu(gate_pre)
    act = (silu * up_pre).astype(b16)
    dact = jnp.einsum("secd,ehd->sech", grid_dy, expert_down, preferred_element_type=f32)
    dgate_pre = (dact * up_pre * sigma * (1.0 + gate_pre * (1.0 - sigma))).astype(b16)
    dup_pre = (dact * silu).astype(b16)
    down_term = jnp.einsum("sech,secd->ehd", act, grid_dy, preferred_element_type=f32)
    gate_term = jnp.einsum("secd,sech->edh", grid_x, dgate_pre, preferred_element_type=f32)
    up_term = jnp.einsum("secd,sech->edh", grid_x, dup_pre, preferred_element_type=f32)
    entry_grad = (
        jnp.einsum("sech,edh->secd", dgate_pre, expert_gate, preferred_element_type=f32)
        + jnp.einsum("sech,edh->secd", dup_pre, expert_up, preferred_element_type=f32)
    ).astype(b16)
    entry_back = lax.all_to_all(
        entry_grad.reshape(n_ctx * owned, cap, width),
        "ctx",
        split_axis=0,
        concat_axis=0,
        tiled=True,
    )
    route_grad = jnp.sum(
        entry_back.reshape(experts * cap, width)[dest].reshape(rows, topk, width).astype(f32),
        axis=1,
    )
    gate_grad_out, up_grad_out, down_grad_out = (
        lax.psum_scatter(
            gate_term.astype(jnp.bfloat16), "dp", scatter_dimension=2, tiled=True
        ).astype(jnp.float32),
        lax.psum_scatter(
            up_term.astype(jnp.bfloat16), "dp", scatter_dimension=2, tiled=True
        ).astype(jnp.float32),
        lax.psum_scatter(
            down_term.astype(jnp.bfloat16), "dp", scatter_dimension=1, tiled=True
        ).astype(jnp.float32),
    )
    prob_grad = jnp.sum(jnp.where(choice_mask, gate_grad[:, :, None], 0.0), axis=1)
    logit_grad = probs * (prob_grad - jnp.sum(probs * prob_grad, axis=-1, keepdims=True))
    router_term = jnp.dot(n2.astype(f32).T, logit_grad, precision=HIGH)
    n2_grad = route_grad + jnp.dot(logit_grad, router.astype(f32).T, precision=HIGH)
    unused_value, ffn_back = jax.vjp(norm_rows, h1, norm_ffn)
    h1_part, ffn_gain_grad = ffn_back(n2_grad)
    h1_grad = grad_top + h1_part
    h1_low = h1_grad.astype(b16)
    attn_grad = jnp.dot(h1_low, wo.T, preferred_element_type=f32).astype(b16)
    gh = attn_grad.reshape(rows, heads, head_dim)
    delta = jnp.einsum("qhd,qhd->hq", gh.astype(f32), attn_heads, precision=HIGH)
    local_index = jnp.arange(rows, dtype=jnp.int32)

    def key_step(index, state):
        moving, query_grad = state
        k_move, v_move, s_move, key_acc, value_acc = moving
        anchor = (rank - index + n_ctx) % n_ctx
        k_place = anchor * rows + local_index
        dq, dk, dv = pair_grads(
            qh,
            gh,
            lse,
            delta,
            place,
            seg,
            k_move.astype(b16).reshape(rows, heads, head_dim),
            v_move.astype(b16).reshape(rows, heads, head_dim),
            k_place,
            s_move,
            scale,
            needed(place, seg, k_place, s_move),
        )
        moving = (
            shifted(k_move.astype(jnp.bfloat16), "ctx", 1).astype(k_move.dtype),
            shifted(v_move.astype(jnp.bfloat16), "ctx", 1).astype(v_move.dtype),
            shifted(s_move, "ctx", 1),
            shifted((key_acc + dk.reshape(rows, width)).astype(jnp.bfloat16), "ctx", 1).astype(
                jnp.float32
            ),
            shifted((value_acc + dv.reshape(rows, width)).astype(jnp.bfloat16), "ctx", 1).astype(
                jnp.float32
            ),
        )
        return (moving, query_grad + dq)

    start_keys = (
        (
            keys.astype(f32),
            values.astype(f32),
            seg,
            jnp.zeros((rows, width), f32),
            jnp.zeros((rows, width), f32),
        ),
        jnp.zeros((rows, heads, head_dim), f32),
    )
    (unused_k, unused_v, unused_s, key_grad, value_grad), query_grad = lax.fori_loop(
        0, n_ctx, key_step, start_keys
    )
    query_grad = query_grad.reshape(rows, width)
    unused_query, query_back = jax.vjp(
        lambda proj, gain: qk_post(proj, gain, place, heads), qp, norm_query
    )
    qp_grad, query_gain_grad = query_back(query_grad)
    unused_key, key_back = jax.vjp(
        lambda proj, gain: qk_post(proj, gain, place, heads), kp, norm_key
    )
    kp_grad, key_gain_grad = key_back(key_grad)
    qp_low = qp_grad.astype(b16)
    kp_low = kp_grad.astype(b16)
    vp_low = value_grad.astype(b16)
    n1_grad = (
        jnp.dot(qp_low, wq.T, preferred_element_type=f32)
        + jnp.dot(kp_low, wk.T, preferred_element_type=f32)
        + jnp.dot(vp_low, wv.T, preferred_element_type=f32)
    )
    unused_norm, attn_back = jax.vjp(norm_rows, inputs, norm_attn)
    input_part, attn_gain_grad = attn_back(n1_grad)
    tokens_grad = (h1_grad + input_part).astype(b16)
    contract = (((0,), (0,)), ((), ()))
    stacked = lax.psum_scatter(
        jnp.concatenate(
            [
                lax.dot_general(n1, qp_low, contract, preferred_element_type=f32),
                lax.dot_general(n1, kp_low, contract, preferred_element_type=f32),
                lax.dot_general(n1, vp_low, contract, preferred_element_type=f32),
                lax.dot_general(attn_low, h1_low, contract, preferred_element_type=f32),
            ],
            axis=1,
        ),
        ("dp", "ctx"),
        scatter_dimension=0,
        tiled=True,
    )
    wq_grad = stacked[:, :width]
    wk_grad = stacked[:, width : 2 * width]
    wv_grad = stacked[:, 2 * width : 3 * width]
    wo_grad = stacked[:, 3 * width :]
    attn_gain_sum, query_gain_sum, key_gain_sum, ffn_gain_sum, router_sum = lax.psum(
        (attn_gain_grad, query_gain_grad, key_gain_grad, ffn_gain_grad, router_term), ("dp", "ctx")
    )
    return (
        block_out,
        tokens_grad,
        attn_gain_sum,
        query_gain_sum,
        key_gain_sum,
        ffn_gain_sum,
        wq_grad,
        wk_grad,
        wv_grad,
        wo_grad,
        router_sum,
        gate_grad_out,
        up_grad_out,
        down_grad_out,
    )


B16 = jnp.bfloat16
F32 = jnp.float32
LANES = 128
NT = (((1,), (1,)), ((), ()))
TN = (((0,), (0,)), ((), ()))


def dot(a, b, dims=(((1,), (0,)), ((), ()))):
    return lax.dot_general(a, b, dims, preferred_element_type=F32)


def ring_of(chips):
    return [2 * p if p < chips // 2 else 2 * (chips - 1 - p) + 1 for p in range(chips)]


def rows_of(ids_ref, index, rows, core):
    return pl.ds(pl.multiple_of(ids_ref[1 + index] * (2 * rows) + core * rows, rows), rows)


def column(row):
    return jnp.broadcast_to(row, (row.shape[1], row.shape[1])).T


def rows_sum(v):
    return jnp.sum(v.T, axis=0, keepdims=True)


def joined(refs):
    return jnp.concatenate([r[...] for r in refs], axis=0)


def project_kernel(ids_ref, *refs, first):
    x_refs, (near_own, far_own, near_other, far_other, own_ref, other_ref, square_ref) = refs[:-7], refs[-7:]
    blocks, rows, wide = own_ref.shape
    hd = wide // 3
    x = joined(x_refs)
    half = x.shape[1] // 2
    own = dot(x[:, :half], near_own[...]) + dot(x[:, half:], far_own[...])
    other = dot(x[:, :half], near_other[...]) + dot(x[:, half:], far_other[...])
    own_ref[...] = own.reshape(own_ref.shape)
    other_ref[...] = other.reshape(other_ref.shape)
    square_ref[...] = jnp.zeros_like(square_ref)
    chips = square_ref.shape[0] // 2
    for i in range(blocks):
        at = slice(i * rows, (i + 1) * rows)
        for j in range(2):
            cols = slice(j * hd, (j + 1) * hd)
            total = rows_sum(own[at, cols] * own[at, cols] + other[at, cols] * other[at, cols])
            square_ref[pl.ds(j * chips + ids_ref[1 + first + i], 1)] = total


def turned(v, cosine, sine):
    return v * cosine + pltpu.roll(v, v.shape[1] // 2, 1) * sine


def turned_back(v, cosine, sine):
    return v * cosine + pltpu.roll(v * sine, v.shape[1] // 2, 1)


def head_kernel(ids_ref, *refs, width):
    raw, (total_ref, cos_ref, sin_ref, gain_ref, own_ref, other_ref) = refs[:4], refs[4:]
    chips, rows, wide = own_ref.shape
    hd = wide // 3
    cut = raw[0].shape[0]
    for i in range(chips):
        for h, out in ((0, own_ref), (2, other_ref)):
            src = raw[h][i] if i < cut else raw[h + 1][i - cut]
            for j in range(2):
                scale = column(lax.rsqrt(total_ref[pl.ds(j * chips + ids_ref[1 + i], 1)] / width + EPS))
                v = src[:, j * hd : (j + 1) * hd] * scale * gain_ref[h + j : h + j + 1]
                out[i, :, j * hd : (j + 1) * hd] = turned(v, cos_ref[i], sin_ref[i]).astype(B16)
            out[i, :, 2 * hd :] = src[:, 2 * hd :].astype(B16)


def inner_kernel(ids_ref, grad_own, grad_other, *refs, width):
    raw, (total_ref, cos_ref, sin_ref, gain_ref, inner_ref, out_ref) = refs[:4], refs[4:]
    chips, rows, wide = grad_own.shape
    hd = wide // 3
    cut = raw[0].shape[0]
    out = [jnp.zeros((rows, hd), F32)] * 4
    for i in range(chips):
        for j in range(2):
            cols = slice(j * hd, (j + 1) * hd)
            scale = column(lax.rsqrt(total_ref[pl.ds(j * chips + ids_ref[1 + i], 1)] / width + EPS))
            inner = jnp.zeros((rows, hd), F32)
            for h, grad in ((0, grad_own), (2, grad_other)):
                src = (raw[h][i] if i < cut else raw[h + 1][i - cut])[:, cols]
                v = turned_back(grad[i, :, cols].astype(F32), cos_ref[i], sin_ref[i]) * src
                inner += v * gain_ref[h + j : h + j + 1]
                out[h + j] = out[h + j] + v * scale
            inner_ref[pl.ds(j * chips + ids_ref[1 + i], 1)] = rows_sum(inner)
    out_ref[...] = jnp.concatenate([jnp.sum(v, axis=0, keepdims=True) for v in out] * 2, axis=0)


def finish_kernel(ids_ref, grad_own, grad_other, *refs, width):
    raw, refs = refs[:4], refs[4:]
    total_ref, inner_ref, cos_ref, sin_ref, gain_ref, near_own, far_own, near_other, far_other = refs[:9]
    x_refs, (low_own, low_other, part_ref, sum_ref) = refs[9:-4], refs[-4:]
    chips, rows, wide = grad_own.shape
    hd = wide // 3
    cut = raw[0].shape[0]
    for i in range(chips):
        for j in range(3):
            cols = slice(j * hd, (j + 1) * hd)
            if j < 2:
                at = pl.ds(j * chips + ids_ref[1 + i], 1)
                scale = lax.rsqrt(total_ref[at] / width + EPS)
                inner = column(scale * scale * scale * (inner_ref[at] / width))
                scale = column(scale)
            for h, grad, out in ((0, grad_own, low_own), (2, grad_other, low_other)):
                v = grad[i, :, cols].astype(F32)
                if j < 2:
                    src = (raw[h][i] if i < cut else raw[h + 1][i - cut])[:, cols]
                    v = turned_back(v, cos_ref[i], sin_ref[i])
                    v = scale * (v * gain_ref[h + j : h + j + 1]) - src * inner
                out[i, :, cols] = v.astype(B16)
    x = joined(x_refs)
    half = width // 2
    group = min(4, chips)
    for lo in range(0, chips, group):
        own = low_own[lo : lo + group].reshape(group * rows, wide)
        other = low_other[lo : lo + group].reshape(group * rows, wide)
        for first, w_own, w_other in ((0, near_own, near_other), (half, far_own, far_other)):
            part = dot(own, w_own[...], NT) + dot(other, w_other[...], NT)
            part_ref[lo : lo + group, :, first : first + half] = part.astype(B16).reshape(group, rows, half)
            seen = x[lo * rows : (lo + group) * rows, first : first + half].astype(F32)
            term = jnp.sum((part * seen).reshape(group * rows // 8, 8, half), axis=0)
            if lo == 0:
                sum_ref[:, first : first + half] = term
            else:
                sum_ref[:, first : first + half] += term


def outer_kernel(*refs, count):
    outs = refs[-count - 4 : -5] + (refs[-5:-1],)
    left, x_refs, x_all = refs[:count], refs[count : -count - 4], refs[-1]
    x_all[...] = joined(x_refs)
    width = x_all.shape[1]
    tile = min(512, width)
    for l_ref, out in zip(left, outs):
        chips, rows, wide = l_ref.shape
        turn = l_ref[...].reshape(chips * rows, wide).astype(F32).T.astype(B16)
        parts = out if isinstance(out, tuple) else (out,)
        size = parts[0].shape[1]
        for lo in range(0, width, tile):
            parts[lo // size][:, lo % size : lo % size + tile] = dot(turn, x_all[:, lo : lo + tile]).astype(B16 if len(parts) > 1 else out.dtype)


def head_grad_kernel(*refs):
    x_refs, (w_ref, own_ref, other_ref) = refs[:-3], refs[-3:]
    hd = own_ref.shape[2]
    grad = dot(joined(x_refs), w_ref[...], NT).astype(B16)
    own_ref[...] = grad[:, :hd].reshape(own_ref.shape)
    other_ref[...] = grad[:, hd:].reshape(other_ref.shape)


def slab_kernel(ids_ref, *refs):
    w_refs, out_ref = refs[:-1], refs[-1]
    chips, rows, wide = out_ref.shape
    hd = wide // len(w_refs)
    for c in range(chips):
        spot = pl.ds(pl.multiple_of((2 * c + ids_ref[0]) * hd, hd), hd)
        for i, w_ref in enumerate(w_refs):
            out_ref[c, :, i * hd : (i + 1) * hd] = w_ref[:, spot]


def on_core(kernel, shapes, operands, flops, scratch=()):
    scalars = operands[0].dtype == jnp.int32
    memory = [pltpu.SMEM if scalars and i == 0 else pltpu.VMEM for i in range(len(operands))]
    size = sum(v.size * v.dtype.itemsize for v in list(operands) + jax.tree.leaves(shapes))
    return pl.pallas_call(
        kernel,
        in_specs=[pl.BlockSpec(memory_space=m) for m in memory],
        out_shape=shapes,
        scratch_shapes=scratch,
        compiler_params=pltpu.CompilerParams(vmem_limit_bytes=56 * 2**20),
        cost_estimate=pl.CostEstimate(flops=flops, bytes_accessed=size, transcendentals=0),
    )(*operands)


def seg_column(row_ref, col_ref, rows):
    for lo in range(0, row_ref.shape[1], rows):
        col_ref[lo : lo + rows] = jnp.concatenate([column(row_ref[:, lo : lo + rows])] * (col_ref.shape[1] // rows), axis=1)


def attention_forward(
    ids_ref, mine_ref, other_ref, seg_row_ref, out_ref, lse_ref, qkv_ref, low_ref, away_ref, seg_col_ref, *, block, scale
):
    chips, rows, hd = mine_ref.shape[0], mine_ref.shape[1], mine_ref.shape[2] // 3
    core = ids_ref[0]
    for i in range(chips):
        qkv_ref[rows_of(ids_ref, i, rows, core)] = mine_ref[i]
        qkv_ref[rows_of(ids_ref, i, rows, 1 - core)] = other_ref[i]
    total = qkv_ref.shape[0]
    seg_column(seg_row_ref, seg_col_ref, rows)
    vt = qkv_ref[:, 2 * hd :].astype(F32).T.astype(B16)
    for index in range(total // block):
        low, high = index * block, (index + 1) * block
        score = dot(qkv_ref[:high, hd : 2 * hd], qkv_ref[low:high, :hd], NT) * scale
        key = lax.broadcasted_iota(jnp.int32, (high, block), 0)
        query = low + lax.broadcasted_iota(jnp.int32, (high, block), 1)
        seen = (key <= query) & (seg_col_ref[:high] == seg_row_ref[:, low:high])
        score = jnp.where(seen, score, NEGATIVE)
        best = jnp.max(score, axis=0, keepdims=True)
        prob = jnp.exp(score - best)
        norm = jnp.sum(prob, axis=0, keepdims=True)
        out = dot(vt[:, :high], prob.astype(B16)) / norm
        out_ref[low:high] = out.T
        lse_ref[:, low:high] = best + jnp.log(norm)
    for i in range(chips):
        low_ref[i] = out_ref[rows_of(ids_ref, i, rows, core)].astype(B16)
        away_ref[i] = out_ref[rows_of(ids_ref, i, rows, 1 - core)].astype(B16)


def attention_backward(
    ids_ref, qkv_ref, *refs, block, scale
):
    out_ref, lse_ref, seg_row_ref, low_ref, away_ref, g_ref, grad_ref, seg_col_ref = refs[4:]
    chips, rows, wide = low_ref.shape
    hd = wide // 3
    core = ids_ref[0]
    cut = refs[0].shape[0]
    for i in range(chips):
        g_ref[rows_of(ids_ref, i, rows, core)] = refs[0][i] if i < cut else refs[1][i - cut]
        g_ref[rows_of(ids_ref, i, rows, 1 - core)] = refs[2][i] if i < cut else refs[3][i - cut]
    total = qkv_ref.shape[0]
    seg_column(seg_row_ref, seg_col_ref, rows)
    kt = qkv_ref[:, hd : 2 * hd].astype(F32).T.astype(B16)
    grad_ref[...] = jnp.zeros_like(grad_ref)
    for index in range(total // block):
        low, high = index * block, (index + 1) * block
        q, g = qkv_ref[low:high, :hd], g_ref[low:high]
        delta = jnp.sum((g.astype(F32) * out_ref[low:high]).T, axis=0, keepdims=True)
        score = dot(qkv_ref[:high, hd : 2 * hd], q, NT) * scale
        key = lax.broadcasted_iota(jnp.int32, (high, block), 0)
        query = low + lax.broadcasted_iota(jnp.int32, (high, block), 1)
        seen = (key <= query) & (seg_col_ref[:high] == seg_row_ref[:, low:high])
        prob = jnp.where(seen, jnp.exp(score - lse_ref[:, low:high]), 0.0)
        dprob = dot(qkv_ref[:high, 2 * hd :], g, NT)
        dscore = (prob * (dprob - delta)).astype(B16)
        grad_ref[:high, hd : 2 * hd] += dot(dscore, q) * scale
        grad_ref[:high, 2 * hd :] += dot(prob.astype(B16), g)
        grad_ref[low:high, :hd] = dot(kt[:, :high], dscore).T * scale
    for i in range(chips):
        low_ref[i] = grad_ref[rows_of(ids_ref, i, rows, core)]
        away_ref[i] = grad_ref[rows_of(ids_ref, i, rows, 1 - core)].astype(B16)


def expert_kernel(ids_ref, *refs, shards, experts, fresh):
    x_refs, refs = refs[:shards], refs[shards:]
    g_refs, refs = refs[:shards], refs[shards:]
    wg_ref, wu_ref, wd_ref = refs[:3]
    refs = refs[3 if fresh else 8 :]
    moe_ref, dx_ref, ag_ref, dg_ref, du_ref, xs_ref, gs_ref, moe_acc, dx_acc, dgate_acc = refs
    expert, step, steps = pl.program_id(0), pl.program_id(1), pl.num_programs(1)
    rows, width = g_refs[0].shape
    first = (expert == 0) & (step == 0)

    @pl.when(first)
    def _():
        for i in range(shards):
            xs_ref[i] = x_refs[i][:, :width]
            gs_ref[i] = g_refs[i][...]
        dgate_acc[...] = jnp.zeros_like(dgate_acc)

    x = xs_ref[...].reshape(shards * rows, width)
    g = gs_ref[...].reshape(shards * rows, width)
    lane = lax.broadcasted_iota(jnp.int32, (rows, LANES), 1)
    mine = (lane < 3 * experts) & (lax.rem(lane, experts) == ids_ref[expert])
    gate = jnp.concatenate(
        [
            jnp.sum(jnp.where(mine, x_refs[i][:, width:].astype(F32), 0.0), axis=1, keepdims=True)
            for i in range(shards)
        ],
        axis=0,
    )
    wg, wu, wd = wg_ref[0], wu_ref[0], wd_ref[0]
    gate_pre = dot(x, wg)
    up_pre = dot(x, wu)
    dact = dot(g, wd, NT)
    sigma = 1.0 / (1.0 + jnp.exp(-gate_pre))
    silu = gate_pre * sigma
    act = silu * up_pre
    part = jnp.sum(act * dact, axis=1, keepdims=True)
    lane = lax.broadcasted_iota(jnp.int32, (shards * rows, LANES), 1)
    dgate_acc[...] += jnp.where(lane == ids_ref[expert], part, 0.0)
    act_low = (gate * act).astype(B16)
    dact = gate * dact
    dgate_pre = (dact * up_pre * sigma * (1.0 + gate_pre * (1.0 - sigma))).astype(B16)
    dup_pre = (dact * silu).astype(B16)
    ag_ref[...] = act_low.reshape(ag_ref.shape)
    dg_ref[...] = dgate_pre.reshape(dg_ref.shape)
    du_ref[...] = dup_pre.reshape(du_ref.shape)
    moe = dot(act_low, wd)
    dx = dot(dgate_pre, wg, NT) + dot(dup_pre, wu, NT)

    @pl.when(first)
    def _():
        moe_acc[...] = moe
        dx_acc[...] = dx

    @pl.when(jnp.logical_not(first))
    def _():
        moe_acc[...] += moe
        dx_acc[...] += dx

    @pl.when((expert == pl.num_programs(0) - 1) & (step == steps - 1))
    def _():
        moe_ref[...] = moe_acc[...].astype(B16).reshape(moe_ref.shape)
        dx_ref[:, :, :width] = dx_acc[...].astype(B16).reshape(shards, rows, width)
        rest = dgate_acc[...]
        sent = jnp.zeros_like(rest)
        for i in range(3):
            piece = rest.astype(B16).astype(F32)
            rest -= piece
            sent += pltpu.roll(piece, i * experts, 1) if i else piece
        dx_ref[:, :, width:] = sent.astype(B16).reshape(shards, rows, LANES)


def expert_rows(ids, xs, gs, wg, wu, wd, kept, spot, total, experts):
    shards = len(xs)
    rows, width = gs[0].shape
    pair, _, hidden = wg.shape
    tile = min(512, hidden)
    steps = hidden // tile
    whole = lambda a: pl.BlockSpec(a.shape, lambda e, j, ids: (0, 0))
    flat = pl.BlockSpec((shards, rows, tile), lambda e, j, ids: (spot, 0, e * steps + j))
    full = pl.BlockSpec((shards, rows, width), lambda e, j, ids: (spot, 0, 0))
    alone = pl.BlockSpec((shards, rows, width), lambda e, j, ids: (0, 0, 0))
    in_specs = [whole(a) for a in xs + gs] + [
        pl.BlockSpec((1, width, tile), lambda e, j, ids: (e, 0, j)),
        pl.BlockSpec((1, width, tile), lambda e, j, ids: (e, 0, j)),
        pl.BlockSpec((1, tile, width), lambda e, j, ids: (e, j, 0)),
    ]
    operands = list(xs) + list(gs) + [wg, wu, wd]
    aliases = {}
    if kept is not None:
        base = 1 + len(operands)
        in_specs += [pl.BlockSpec(memory_space=pl.ANY)] * len(kept)
        operands += list(kept)
        aliases = {base + i: 2 + i for i in range(len(kept))}
    kept_hidden = jax.ShapeDtypeStruct((total, rows, pair * hidden), B16)
    kept_width = jax.ShapeDtypeStruct((total, rows, width), B16)
    out = pl.pallas_call(
        functools.partial(expert_kernel, shards=shards, experts=experts, fresh=kept is None),
        grid_spec=pltpu.PrefetchScalarGridSpec(
            num_scalar_prefetch=1,
            grid=(pair, steps),
            in_specs=in_specs,
            out_specs=[
                alone,
                pl.BlockSpec((shards, rows, width + LANES), lambda e, j, ids: (0, 0, 0)),
                flat,
                flat,
                flat,
                full,
                full,
            ],
            scratch_shapes=[
                pltpu.VMEM((shards * rows, width), F32),
                pltpu.VMEM((shards * rows, width), F32),
                pltpu.VMEM((shards * rows, LANES), F32),
            ],
        ),
        out_shape=[
            jax.ShapeDtypeStruct((shards, rows, width), B16),
            jax.ShapeDtypeStruct((shards, rows, width + LANES), B16),
            kept_hidden,
            kept_hidden,
            kept_hidden,
            kept_width,
            kept_width,
        ],
        input_output_aliases=aliases,
        compiler_params=pltpu.CompilerParams(vmem_limit_bytes=56 * 2**20),
        cost_estimate=pl.CostEstimate(
            flops=12 * shards * rows * width * hidden * pair,
            bytes_accessed=6 * width * hidden * pair,
            transcendentals=shards * rows * hidden * pair,
        ),
    )(ids, *operands)
    return out[0], out[1], out[2:]


def rows_grad_kernel(ids_ref, there_ref, back_ref, own_ref, grad_ref, rows_ref, gain_ref, out_ref):
    rows, width = grad_ref.shape
    core, blocks = ids_ref[0], width // rows
    spots, parts = [], []
    total, inner = jnp.zeros((rows, rows), F32), jnp.zeros((rows, rows), F32)
    for i in range(blocks):
        at = slice(i * rows, (i + 1) * rows)
        chip, parity = i % (blocks // 2), core if i < blocks // 2 else 1 - core
        spot = pl.ds(pl.multiple_of((2 * chip + parity) * rows, rows), rows)
        part = there_ref[:, at].astype(F32) + back_ref[:, at].astype(F32) + own_ref[:, at].astype(F32)
        part = part * gain_ref[:, spot]
        v = rows_ref[:, spot].astype(F32)
        total += v * v
        inner += v * part
        spots.append(spot)
        parts.append(part)
    scale = lax.rsqrt(jnp.sum(total, axis=1, keepdims=True) / width + EPS)
    inner = scale * scale * scale * (jnp.sum(inner, axis=1, keepdims=True) / width)
    for spot, part in zip(spots, parts):
        out_ref[:, spot] = (grad_ref[:, spot] + part * scale - rows_ref[:, spot].astype(F32) * inner).astype(B16)


def expert_grad_kernel(left_ref, right_ref, *refs, pieces, whole):
    step = pl.program_id(0)
    term = dot(left_ref[...], right_ref[...], TN)
    for i in range(pieces):

        @pl.when(step == i)
        def _():
            if whole:
                refs[-1][...] = (term + refs[i][...].astype(F32)).astype(B16)
            else:
                refs[i][...] = term.astype(B16)


def expert_grad_term(left, right, arrived, left_at, right_at, size, across):
    rows = left.shape[0]
    high, wide = (size, right.shape[1]) if across else (left.shape[1], size)
    pieces = 4
    tile = high // pieces
    first = left_at // tile
    in_specs = [
        pl.BlockSpec((rows, tile), lambda j: (0, first + j)),
        pl.BlockSpec((rows, wide), lambda j: (0, right_at // size)),
    ]
    fixed = pl.BlockSpec((tile, wide), lambda j: (0, 0))
    whole = arrived is not None
    return pl.pallas_call(
        functools.partial(expert_grad_kernel, pieces=pieces, whole=whole),
        grid=(pieces,),
        in_specs=in_specs + ([fixed] * pieces if whole else []),
        out_specs=pl.BlockSpec((tile, wide), lambda j: (j, 0)) if whole else [fixed] * pieces,
        out_shape=jax.ShapeDtypeStruct((high, wide), B16) if whole else [jax.ShapeDtypeStruct((tile, wide), B16)] * pieces,
        compiler_params=pltpu.CompilerParams(vmem_limit_bytes=56 * 2**20),
        cost_estimate=pl.CostEstimate(
            flops=2 * rows * high * wide, bytes_accessed=2 * (rows * (high + wide) + high * wide), transcendentals=0
        ),
    )(left, right, *(arrived if whole else []))


def split_three(v):
    high = lax.reduce_precision(v, exponent_bits=8, mantissa_bits=7)
    middle = lax.reduce_precision(v - high, exponent_bits=8, mantissa_bits=7)
    return [part.astype(B16) for part in (high, middle, v - high - middle)]


def local_fast(
    tokens,
    doc_starts,
    routes,
    norm_attn,
    norm_query,
    norm_key,
    norm_ffn,
    w_query,
    w_key,
    w_value,
    w_output,
    router,
    expert_gate,
    expert_up,
    expert_down,
    out_grad,
):
    devices = lax.axis_size("ctx")
    rank = lax.axis_index("ctx")
    group = lax.axis_index("dp")
    chips = devices // 2
    chip, core = rank // 2, rank % 2
    rows, width = tokens.shape
    experts = router.shape[1]
    hd = width // HEADS
    scale = hd ** (-0.5)
    half = chips // 2
    order = ring_of(chips)
    right = [(2 * order[p] + c, 2 * order[(p + 1) % chips] + c) for p in range(chips) for c in range(2)]
    left = [(b, a) for a, b in right]
    place_in_ring = jnp.where(chip % 2 == 0, chip // 2, chips - 1 - chip // 2)
    same_core = [[2 * c + p for c in range(chips)] for p in range(2)]

    def to_right(v):
        return lax.ppermute(v, "ctx", right)

    def to_left(v):
        return lax.ppermute(v, "ctx", left)

    def core_swap(v):
        return lax.ppermute(v, "ctx", [(i, i ^ 1) for i in range(devices)])

    def group_swap(v):
        return lax.ppermute(v, "dp", [(0, 1), (1, 0)])

    def chip_at(offset):
        spot = (place_in_ring + offset + chips) % chips
        return jnp.where(spot < half, 2 * spot, 2 * (chips - 1 - spot) + 1)

    offsets = [0] + [s * o for o in range(1, half) for s in (1, -1)] + [half]

    def after(v, *others):
        return lax.optimization_barrier((v,) + others)[0]

    places = jnp.stack([chip_at(o) for o in offsets])

    def ring_gather(v, ties=(), first=None):
        ties = list(ties) + [()] * half
        cut = v.shape[0] // 32 * 16
        got = {0: v}

        def send(i, one, two):
            if i == 0 and first:
                return first
            one, two = lax.optimization_barrier((one, two) + tuple(ties[i]))[:2]
            return to_right(one), to_left(two)

        for o in range(1, half):
            got[-o], got[o] = send(o - 1, got[-(o - 1)], got[o - 1])
        first, second = send(half - 1, got[-(half - 1)][:cut], got[half - 1][cut:])
        got[half] = jnp.concatenate([first, second], axis=0)
        got["halves"] = (first, second)
        return got

    def in_ring(got):
        return jnp.concatenate([got[o] for o in offsets], axis=0)

    def ring_steps(part, axis):
        far = part(half)
        cut = far.shape[axis] // 2 // LANES * LANES
        a_cut = lambda v: lax.slice_in_dim(v, 0, cut, axis=axis)
        b_cut = lambda v: lax.slice_in_dim(v, cut, v.shape[axis], axis=axis)
        there, back = lax.optimization_barrier((a_cut(far), b_cut(far)))
        there, back = yield to_right(there), to_left(back)
        near, other = part(half - 1), part(1 - half)
        there = jnp.concatenate([a_cut(near) + there, b_cut(near)], axis=axis)
        back = jnp.concatenate([a_cut(other), b_cut(other) + back], axis=axis)
        for o in range(half - 2, 0, -1):
            there, back = lax.optimization_barrier((there, back))
            there, back = yield to_right(there), to_left(back)
            there, back = there + part(o), back + part(-o)
        there, back = lax.optimization_barrier((there, back))
        there, back = yield to_right(there), to_left(back)
        return there, back, part(0)

    def tied(values, *others, all_of=False):
        return lax.optimization_barrier(tuple(values) + others)[: None if all_of else len(values)]

    def ring_sum(part, axis, work=()):
        work = list(work) + [None] * half
        ring = ring_steps(part, axis)
        values, token = next(ring), None
        for i in range(half):
            arrays, then = work[i](token) if work[i] else ((), None)
            values = tied(values, *arrays, all_of=True)
            if then:
                then(*values[2:])
            values = values[:2]
            token = values[0]
            try:
                values = ring.send(values)
            except StopIteration as end:
                return end.value

    def total_of(terms):
        return sum(v.astype(F32) for v in terms)

    def sum_chips(v):
        step = 2
        while step < devices:
            v = v + lax.ppermute(v, "ctx", [(i, i ^ step) for i in range(devices)])
            step *= 2
        return v

    def by_core(mine, other, axis):
        return jnp.where(core == 0, jnp.stack([mine, other], axis), jnp.stack([other, mine], axis))

    def pick(pair, which):
        return jnp.where(which == 0, pair[0], pair[1])

    def by_parity(v, axis, back=False):
        shape = v.shape
        v = v.reshape(shape[:axis] + ((2, chips, rows) if back else (chips, 2, rows)) + shape[axis + 1 :])
        split = axis if back else axis + 1
        one, two = [lax.index_in_dim(v, i, split, keepdims=False) for i in range(2)]
        one, two = jnp.where(core == 0, one, two), jnp.where(core == 0, two, one)
        return jnp.stack([one, two], axis + 1 if back else axis).reshape(shape)

    wg_pair, wu_pair, wd_pair = [(w, core_swap(w)) for w in (expert_gate, expert_up, expert_down)]

    inputs = tokens.astype(F32)
    n1 = by_parity(norm_rows(inputs, norm_attn).astype(B16), 1)

    slab = on_core(
        slab_kernel,
        jax.ShapeDtypeStruct((chips, rows, 3 * hd), B16),
        [group[None].astype(jnp.int32), w_query, w_key, w_value],
        0,
    )
    first = (to_right(n1), to_left(n1))
    near_head = lax.all_to_all(slab, "ctx", split_axis=0, concat_axis=0, axis_index_groups=same_core, tiled=True)
    far_head = group_swap(near_head)
    near_head, *first = tied((near_head,) + first)
    n1_got = {0: n1, -1: first[0], 1: first[1]}
    for o in range(2, half):
        one, two = lax.optimization_barrier((n1_got[1 - o], n1_got[o - 1]) + ((near_head,) if o == 2 else ()))[:2]
        n1_got[-o], n1_got[o] = to_right(one), to_left(two)
    own = jnp.where(core == group, near_head, far_head)
    other = jnp.where(core == group, far_head, near_head)
    w_in = [v.reshape(chips * rows, 3 * hd) for v in (own, core_swap(other), other, core_swap(own))]
    w_out = jnp.concatenate([w_output, core_swap(w_output)], axis=0)

    count = chips * rows
    place = (2 * places[:, None, None] + core) * rows + lax.broadcasted_iota(jnp.int32, (chips, rows, 1), 1)
    freq = THETA ** (-jnp.arange(hd // 2, dtype=F32) * 2.0 / hd)
    angle = place.astype(F32) * freq[None, None, :]
    cosine, sine = jnp.cos(angle), jnp.sin(angle)
    cosine = jnp.concatenate([cosine] * 2, axis=2)
    sine = jnp.concatenate([-sine, sine], axis=2)
    ids = jnp.concatenate([core[None], places]).astype(jnp.int32)
    ranks = (rank, rank ^ 1)
    gains = jnp.stack([lax.dynamic_slice(g, (r * hd,), (hd,)) for r in ranks for g in (norm_query, norm_key)])
    gains = jnp.concatenate([gains, gains], axis=0)
    early, late = offsets[:5], offsets[5:]
    raw, squares = [None] * 4, [None] * 2

    def project(i, shards):
        blocks = (early, late)[i]
        raw[i], raw[i + 2], squares[i] = on_core(
            functools.partial(project_kernel, first=i * len(early)),
            [jax.ShapeDtypeStruct((len(blocks), rows, 3 * hd), F32)] * 2
            + [jax.ShapeDtypeStruct((2 * chips, rows), F32)],
            [ids] + shards + w_in,
            12 * len(blocks) * rows * width * hd,
        )

    project(0, [n1_got[o] for o in early])
    one, two = lax.optimization_barrier((n1_got[1 - half], n1_got[half - 1], squares[0]))[:2]
    cut = rows // 2
    n1_halves = (to_right(one[:cut]), to_left(two[cut:]))
    project(1, [n1_got[o] for o in late if o != half] + list(n1_halves))
    squares = squares[0] + squares[1]
    top = after(out_grad, *n1_halves)
    top_first = (to_right(top), to_left(top))
    flags = lax.dynamic_update_index_in_dim(jnp.zeros((chips, rows), F32), doc_starts.astype(F32), chip, 0)
    total = sum_chips(after(jnp.concatenate([squares, flags], axis=0), *top_first))
    one, two = lax.optimization_barrier(top_first + (total,))[:2]
    top_got = {0: out_grad, -1: top_first[0], 1: top_first[1], -2: to_right(one), 2: to_left(two)}
    heads = on_core(
        functools.partial(head_kernel, width=width),
        [jax.ShapeDtypeStruct((chips, rows, 3 * hd), B16)] * 2,
        [ids] + raw + [total, cosine, sine, gains],
        0,
    )

    flags = total[2 * chips :]
    flags = by_core(flags, core_swap(flags), 1).reshape(devices, rows)
    tri = (lax.broadcasted_iota(jnp.int32, (rows, rows), 0) <= lax.broadcasted_iota(jnp.int32, (rows, rows), 1)).astype(F32)
    before = (
        lax.broadcasted_iota(jnp.int32, (devices, devices), 1) < lax.broadcasted_iota(jnp.int32, (devices, devices), 0)
    ).astype(F32)
    seg = jnp.dot(flags, tri) + jnp.dot(before, jnp.broadcast_to(jnp.sum(flags, axis=1, keepdims=True), (devices, rows)))
    everything = devices * rows
    seg_row = seg.reshape(1, everything)
    block = min(256, everything)
    half_wide = everything * everything // 2
    attn, lse, head_qkv, low_own, low_away = on_core(
        functools.partial(attention_forward, block=block, scale=scale),
        [
            jax.ShapeDtypeStruct((everything, hd), F32),
            jax.ShapeDtypeStruct((1, everything), F32),
            jax.ShapeDtypeStruct((everything, 3 * hd), B16),
            jax.ShapeDtypeStruct((chips, rows, hd), B16),
            jax.ShapeDtypeStruct((chips, rows, hd), B16),
        ],
        [ids, heads[0], core_swap(heads[1]), seg_row],
        8 * half_wide * hd,
        [pltpu.VMEM((everything, block), F32)],
    )
    low_other = after(core_swap(low_away), top_got[2], top_got[-2])
    attn_low = jnp.concatenate([low_own, low_other], axis=2).reshape(count, 2 * hd)
    out_part = dot(attn_low, w_out).astype(B16).reshape(chips, rows, width)
    weights = [jnp.concatenate(pair, axis=0) for pair in (wg_pair, wu_pair, wd_pair)]
    h1 = inputs + total_of(
        ring_sum(
            lambda o: out_part[offsets.index(o)], 1, [None] + [lambda token, w=w: ((w,), None) for w in weights]
        )
    )

    n2 = norm_rows(h1, norm_ffn).astype(B16)
    probs = jax.nn.softmax(dot(n2, router), axis=-1)
    chosen = jnp.sum(
        (routes[:, :, None] == jnp.arange(experts, dtype=jnp.int32)[None, None, :]).astype(F32), axis=1
    )
    sent = split_three(probs * chosen)
    sent.append(jnp.zeros((rows, LANES - 3 * experts), B16))
    names = jnp.stack(ranks).astype(jnp.int32)
    moe_part, dn2_part = {}, {}
    kept = None

    def run_experts(which, spot):
        moe, dn2, kept_now = expert_rows(
            names, [n2_got[o] for o in which], [top_got[o] for o in which], *weights, kept, spot, chips, experts
        )
        for i, o in enumerate(which):
            moe_part[o], dn2_part[o] = moe[i], dn2[i]
        return kept_now

    n2_got = {0: jnp.concatenate([n2] + sent, axis=1)}
    n2_got[-1], n2_got[1] = to_right(n2_got[0]), to_left(n2_got[0])
    one, two, three, four = lax.optimization_barrier((n2_got[-1], n2_got[1], top_got[-2], top_got[2]))
    n2_got[-2], n2_got[2] = to_right(one), to_left(two)
    top_got[-3], top_got[3] = to_right(three), to_left(four)
    kept = run_experts([0, 1, -1], 0)
    one, two, three, four = lax.optimization_barrier((n2_got[-2], n2_got[2], top_got[-3], top_got[3], kept[0]))[:4]
    n2_got[-3], n2_got[3] = to_right(one), to_left(two)
    top_got[half] = jnp.concatenate([to_right(three[:cut]), to_left(four[cut:])], axis=0)
    kept = run_experts([2, -2], 3)
    one, two = lax.optimization_barrier((n2_got[-3], n2_got[3], kept[0]))[:2]
    n2_got[half] = jnp.concatenate([to_right(one[:cut]), to_left(two[cut:])], axis=0)
    kept = run_experts([3, -3, half], 1)
    kept = [v.reshape(count, -1) for v in kept]
    act_all, dgate_pre_all, dup_pre_all, x_all, top_all = kept

    hidden = expert_gate.shape[2]
    pairs = [(act_all, top_all), (x_all, dgate_pre_all), (x_all, dup_pre_all)]

    def expert_term(i, expert, token, plus):
        left_side, right_side = pairs[i]
        across = i == 0
        at = expert * hidden
        return expert_grad_term(
            left_side if token is None else after(left_side, token), right_side, plus, at if across else 0, 0 if across else at, hidden, across
        )

    arrived, expert_grads = [], []

    def own_term(i):
        def run(token):
            return (expert_term(i, 0, token, arrived[i]),), then

        def then(mine):
            expert_grads.append(lax.psum_scatter(mine, "dp", scatter_dimension=0 if i == 0 else 1, tiled=True))

        return run

    def other_term(i):
        def run(token):
            return tuple(expert_term(i, 1, token, None)), then

        def then(*other):
            arrived.append([core_swap(v) for v in other])

        return run

    n2_sum = total_of(
        ring_sum(lambda o: dn2_part[o], 1, [other_term(0), own_term(0), other_term(1), other_term(2)])
    )
    dgates = n2_sum[:, width : width + 3 * experts].reshape(rows, 3, experts)
    n2_sum = n2_sum[:, :width]
    prob_grad = (dgates[:, 0] + dgates[:, 1] + dgates[:, 2]) * chosen
    logit_grad = probs * (prob_grad - jnp.sum(probs * prob_grad, axis=-1, keepdims=True))
    router_term = lax.dot_general(logit_grad, n2.astype(F32), TN, precision=HIGH)
    n2_grad = n2_sum + jnp.dot(logit_grad, router.astype(F32).T, precision=HIGH)
    grad_top = out_grad.astype(F32)
    unused_value, ffn_back = jax.vjp(norm_rows, h1, norm_ffn)
    h1_part, ffn_gain_grad = ffn_back(n2_grad)
    h1_grad = grad_top + h1_part
    h1_low = h1_grad.astype(B16)

    grad_parts = [None] * 4

    def head_grad(i, shards):
        blocks = (early, late)[i]
        grad_parts[i], away = on_core(
            head_grad_kernel,
            [jax.ShapeDtypeStruct((len(blocks), rows, hd), B16)] * 2,
            shards + [w_out],
            4 * len(blocks) * rows * width * hd,
        )
        grad_parts[i + 2] = core_swap(away)
        return away

    h1_got = {0: h1_low, -1: to_right(h1_low), 1: to_left(h1_low)}

    def from_across(v, step, token):
        return lax.ppermute(after(v, token), "ctx", [(i, i ^ step) for i in range(devices)])

    early_sum = jnp.concatenate([router_term, ffn_gain_grad[None]], axis=0)
    early_sum = early_sum + core_swap(early_sum)
    one, two = h1_got[-1], h1_got[1]
    for o in range(1, half):
        mine, then = own_term(o)(h1_low if o == 1 else one) if o < 3 else ((), lambda: None)
        h1_got[-o], h1_got[o], *mine = tied((h1_got[-o], h1_got[o]), *mine, all_of=True)
        then(*mine)
        one, two = h1_got[-o], h1_got[o]
        if o < half - 1:
            h1_got[-o - 1], h1_got[o + 1] = to_right(one), to_left(two)
    cut = rows // 2
    h1_halves = (to_right(one[:cut]), to_left(two[cut:]))
    away = head_grad(0, [after(h1_got[0], one)] + [h1_got[o] for o in early[1:]])
    h1_halves = tied(h1_halves, away)
    away = head_grad(1, [h1_got[o] for o in late if o != half] + list(h1_halves))
    moe_ring = ring_steps(lambda o: after(moe_part[o], *h1_halves) if o == half else moe_part[o], 1)
    moe_got = next(moe_ring)
    attn = after(attn, *moe_got)
    moe_got = moe_ring.send(moe_got)
    early_recv = from_across(early_sum, 2, away)
    grads_own, grads_away = on_core(
        functools.partial(attention_backward, block=block, scale=scale),
        [jax.ShapeDtypeStruct((chips, rows, 3 * hd), t) for t in (F32, B16)],
        [ids, head_qkv] + grad_parts + [attn, lse, seg_row],
        20 * half_wide * hd,
        [
            pltpu.VMEM((everything, hd), B16),
            pltpu.VMEM((everything, 3 * hd), F32),
            pltpu.VMEM((everything, block), F32),
        ],
    )
    grads = [grads_own, core_swap(grads_away)]
    inner, gain_grads = on_core(
        functools.partial(inner_kernel, width=width),
        [jax.ShapeDtypeStruct((2 * chips, rows), F32), jax.ShapeDtypeStruct((8, hd), F32)],
        [ids] + grads + raw + [total, cosine, sine, gains],
        0,
    )
    n1_shards = [n1_got[o] for o in offsets if o != half] + list(n1_halves)
    h1_shards = [h1_got[o] for o in offsets if o != half] + list(h1_halves)
    o_own, *o_away = on_core(
        functools.partial(outer_kernel, count=2),
        [jax.ShapeDtypeStruct((hd, width), F32)] + [jax.ShapeDtypeStruct((hd, width // 4), B16)] * 4,
        [low_own, after(low_other, gain_grads)] + h1_shards,
        4 * count * width * hd,
        [pltpu.VMEM((count, width), B16)],
    )
    o_head = o_own + jnp.concatenate([core_swap(v) for v in o_away], axis=1).astype(F32)
    o_recv = group_swap(o_head.astype(B16))

    early_recv, *moe_got = tied((early_recv,) + tuple(moe_got), grads_own)
    moe_got = moe_ring.send(tuple(moe_got))
    early_sum = early_sum + early_recv
    early_recv = from_across(early_sum, 4, grads_own)
    inner, *moe_got = tied((inner,) + tuple(moe_got), o_own)
    inner = sum_chips(inner)
    moe_got = moe_ring.send(tied(moe_got, inner))
    early_sum = early_sum + after(early_recv, inner)
    early_recv = from_across(early_sum, 8, inner)
    low_grad_own, low_grad_other, n1_part, attn_gain = on_core(
        functools.partial(finish_kernel, width=width),
        [
            jax.ShapeDtypeStruct((chips, rows, 3 * hd), B16),
            jax.ShapeDtypeStruct((chips, rows, 3 * hd), B16),
            jax.ShapeDtypeStruct((chips, rows, width), B16),
            jax.ShapeDtypeStruct((8, width), F32),
        ],
        [ids] + grads + raw + [total, inner, cosine, sine, gains] + w_in + n1_shards,
        12 * count * width * hd,
    )
    attn_gain = by_parity(jnp.sum(attn_gain, axis=0), 0, back=True) / norm_attn

    n1_part, *moe_got = tied((n1_part,) + tuple(moe_got))
    try:
        moe_ring.send(tuple(moe_got))
    except StopIteration as end:
        moe_sum = total_of(end.value)

    def heads_grads(token):
        return on_core(
            functools.partial(outer_kernel, count=2),
            [jax.ShapeDtypeStruct((3 * hd, width), F32)] + [jax.ShapeDtypeStruct((3 * hd, width // 4), B16)] * 4,
            [low_grad_own, after(low_grad_other, token)] + n1_shards,
            12 * count * width * hd,
            [pltpu.VMEM((count, width), B16)],
        )

    def placed(parts):
        out = jnp.zeros((width,), F32)
        for r, v in zip(ranks, parts):
            out = lax.dynamic_update_slice(out, v, (r * hd,))
        return out

    gain_grads = after(gain_grads, n1_part)
    late_sum = jnp.stack([attn_gain, placed(gain_grads[0::2][:2]), placed(gain_grads[1::2][:2])])
    late_sum = [late_sum + core_swap(late_sum)]
    w_got, grads_out = [], []

    def kept_by(which):
        size = width // 4
        return jnp.concatenate(
            [lax.dynamic_slice_in_dim(w_got[0], i * (width // 2) + which * size, size, 1) for i in range(2)], axis=1
        )

    early = []

    expert_done = []

    def swap_heads(early_recv, w_own, *w_away):
        expert_done.extend(w_away[4:])
        w_away = w_away[:4]
        early.append(group_swap(early_sum + early_recv))
        early.append(early_sum + early_recv)
        w_away = [core_swap(v) for v in w_away]
        w_got.append(w_own + jnp.concatenate(w_away[2:] + w_away[:2], axis=1).astype(F32))
        w_got.append(group_swap(kept_by(1 - group).astype(B16)))

    def in_slabs(w_mine):
        w_mine = w_mine.T.astype(B16).reshape(2, chips // 2, rows, 3 * hd)
        return by_core(w_mine[0], w_mine[1], 1).reshape(devices, -1, 3 * hd)

    def join(w_mine):
        w_got.append(lax.all_to_all(w_mine, "ctx", split_axis=0, concat_axis=0, tiled=True))

    def small_step(step, others=lambda token: (), then=None):
        def run(token):
            return (from_across(late_sum[-1], step, token),) + tuple(others(token)), finish

        def finish(v, *rest):
            late_sum.append(late_sum[-1] + v)
            if then:
                then(*rest)

        return run

    n1_grad = ring_sum(
        lambda o: n1_part[offsets.index(o)],
        1,
        [
            lambda token: ([early_recv] + list(heads_grads(n1_part)) + expert_grads, swap_heads),
            small_step(2, lambda token: [in_slabs(kept_by(group) + after(w_got[1], token).astype(F32))], join),
            small_step(4),
            small_step(
                8,
                lambda token: [after(v, token).astype(F32)[None] for v in expert_done] + w_got[2:],
                lambda *v: grads_out.extend(v),
            ),
        ],
    )
    down_grad_out, gate_grad_out, up_grad_out, w_got = grads_out
    o_head = (o_head + after(o_recv, n1_grad[0]).astype(F32)).astype(B16)
    wo_grad = None
    for i in range(2):
        moves = [
            (g * devices + devices // 2 * g + j, g * devices + 2 * j + i) for g in range(2) for j in range(devices // 2)
        ]
        size = width // (2 * devices)
        piece = lax.ppermute(o_head[i * size : (i + 1) * size], ("dp", "ctx"), moves)
        wo_grad = piece if wo_grad is None else jnp.where(core == 0, wo_grad, piece)
    wo_grad = wo_grad.astype(F32)
    late_sum = after(late_sum[-1], n1_grad[0])
    late_sum = late_sum + group_swap(late_sum)
    early_sum = early[1] + after(early[0], n1_grad[0])
    w_got = w_got.transpose(1, 0, 2).astype(F32)
    slab_rows = w_got.shape[0]
    wq_grad, wk_grad, wv_grad = [
        w_got[:, :, i * hd : (i + 1) * hd].reshape(slab_rows, width) for i in range(3)
    ]
    tokens_grad = on_core(
        rows_grad_kernel,
        jax.ShapeDtypeStruct((rows, width), B16),
        [ids, *n1_grad, h1_grad, tokens, norm_attn.reshape(1, width)],
        0,
    )

    block_out = (h1 + moe_sum).astype(B16)
    router_sum, gain_sums = early_sum[:experts].T, [early_sum[experts]] + [late_sum[i] for i in range(3)]
    return (
        block_out,
        tokens_grad,
        gain_sums[1],
        gain_sums[2],
        gain_sums[3],
        gain_sums[0],
        wq_grad,
        wk_grad,
        wv_grad,
        wo_grad,
        router_sum,
        gate_grad_out,
        up_grad_out,
        down_grad_out,
    )


def local(*args):
    devices, groups = lax.axis_size("ctx"), lax.axis_size("dp")
    experts, owned = args[11].shape[1], args[12].shape[0]
    fits = devices == HEADS == experts and groups == 2 and owned == 1 and 3 * experts <= LANES
    return (local_fast if fits else local_general)(*args)


def solution(mesh):
    return jax.shard_map(
        local,
        mesh=mesh,
        in_specs=(
            P(("dp", "ctx"), None),
            P(("dp", "ctx")),
            P(("dp", "ctx"), None),
            P(),
            P(),
            P(),
            P(),
            P("ctx", None),
            P("ctx", None),
            P("ctx", None),
            P("ctx", None),
            P(),
            P("ctx", None, None),
            P("ctx", None, None),
            P("ctx", None, None),
            P(("dp", "ctx"), None),
        ),
        out_specs=(
            P(("dp", "ctx"), None),
            P(("dp", "ctx"), None),
            P(),
            P(),
            P(),
            P(),
            P(("dp", "ctx"), None),
            P(("dp", "ctx"), None),
            P(("dp", "ctx"), None),
            P(("dp", "ctx"), None),
            P(),
            P("ctx", None, "dp"),
            P("ctx", None, "dp"),
            P("ctx", "dp", None),
        ),
        check_vma=False,
    )
```

```python
import functools

import jax
import jax.numpy as jnp
from jax import lax
from jax.experimental import pallas as pl
from jax.experimental.pallas import tpu as pltpu
from jax.sharding import PartitionSpec as P

HEADS = 16


EPS = 1e-05
THETA = 10000.0
NEGATIVE = -1e30
HIGH = lax.Precision.HIGHEST


def spread(block, axis, holder):
    block = jnp.where(lax.axis_index(axis) == holder, block, jnp.zeros_like(block))
    return lax.psum(block, axis)


def shifted(shard, axis, by):
    devices = lax.axis_size(axis)
    return lax.ppermute(shard, axis, [(i, (i + by) % devices) for i in range(devices)])


def norm_rows(v, gain):
    return v * lax.rsqrt(jnp.mean(v * v, axis=-1, keepdims=True) + EPS) * gain


def rotate(v, place):
    half = v.shape[-1] // 2
    freq = THETA ** (-jnp.arange(half, dtype=jnp.float32) * 2.0 / v.shape[-1])
    angle = place.astype(jnp.float32)[:, None] * freq[None, :]
    cosine = jnp.cos(angle)[:, None, :]
    sine = jnp.sin(angle)[:, None, :]
    first = v[..., :half]
    second = v[..., half:]
    return jnp.concatenate(
        [first * cosine - second * sine, second * cosine + first * sine], axis=-1
    )


def qk_post(proj, gain, place, heads):
    count, width = proj.shape
    normed = norm_rows(proj, gain).reshape(count, heads, width // heads)
    return rotate(normed, place).reshape(count, width)


def needed(q_place, q_seg, k_place, k_seg):
    return (k_place[0] <= q_place[-1]) & (k_seg[-1] >= q_seg[0])


def pair_mask(q_place, q_seg, k_place, k_seg):
    return (k_place[None, :] <= q_place[:, None]) & (k_seg[None, :] == q_seg[:, None])


def pair_grads(qh, gh, lse, delta, q_place, q_seg, kh, vh, k_place, k_seg, scale, wanted):

    def pair_compute(unused):
        score = jnp.einsum("qhd,khd->hqk", qh, kh, preferred_element_type=jnp.float32) * scale
        mask = pair_mask(q_place, q_seg, k_place, k_seg)
        prob = jnp.where(mask[None], jnp.exp(score - lse[:, :, None]), 0.0)
        dprob = jnp.einsum("qhd,khd->hqk", gh, vh, preferred_element_type=jnp.float32)
        dscore = (prob * (dprob - delta[:, :, None])).astype(jnp.bfloat16)
        prob_low = prob.astype(jnp.bfloat16)
        dq = jnp.einsum("hqk,khd->qhd", dscore, kh, preferred_element_type=jnp.float32) * scale
        dk = jnp.einsum("hqk,qhd->khd", dscore, qh, preferred_element_type=jnp.float32) * scale
        dv = jnp.einsum("hqk,qhd->khd", prob_low, gh, preferred_element_type=jnp.float32)
        return (dq, dk, dv)

    def skip(unused):
        return (
            jnp.zeros(qh.shape, jnp.float32),
            jnp.zeros(kh.shape, jnp.float32),
            jnp.zeros(vh.shape, jnp.float32),
        )

    return lax.cond(wanted, pair_compute, skip, 0)


def local_general(
    tokens,
    doc_starts,
    routes,
    norm_attn,
    norm_query,
    norm_key,
    norm_ffn,
    w_query,
    w_key,
    w_value,
    w_output,
    router,
    expert_gate,
    expert_up,
    expert_down,
    out_grad,
):
    f32 = jnp.float32
    b16 = jnp.bfloat16
    n_ctx = lax.axis_size("ctx")
    rank = lax.axis_index("ctx")
    rows, width = tokens.shape
    heads = HEADS
    head_dim = width // heads
    scale = head_dim ** (-0.5)
    experts = router.shape[1]
    topk = routes.shape[1]
    owned = expert_gate.shape[0]
    cap = max(2, rows * topk * 3 // (2 * experts))
    starts = jnp.sum(doc_starts)
    first_count = spread(starts, "ctx", 0)
    before = jnp.where(rank > 0, first_count, 0)
    seg = before + jnp.cumsum(doc_starts)
    place = rank * rows + jnp.arange(rows, dtype=jnp.int32)
    wq, wk, wv, wo = (
        lax.all_gather(w_query, "ctx", axis=0, tiled=True),
        lax.all_gather(w_key, "ctx", axis=0, tiled=True),
        lax.all_gather(w_value, "ctx", axis=0, tiled=True),
        lax.all_gather(w_output, "ctx", axis=0, tiled=True),
    )
    inputs = tokens.astype(f32)
    n1 = norm_rows(inputs, norm_attn).astype(b16)
    qp = jnp.dot(n1, wq, preferred_element_type=f32)
    kp = jnp.dot(n1, wk, preferred_element_type=f32)
    vp = jnp.dot(n1, wv, preferred_element_type=f32)
    query = qk_post(qp, norm_query, place, heads).astype(b16)
    keys = qk_post(kp, norm_key, place, heads).astype(b16)
    values = vp.astype(b16)
    qh = query.reshape(rows, heads, head_dim)
    start_state = (
        jnp.full((heads, rows), NEGATIVE, f32),
        jnp.zeros((heads, rows), f32),
        jnp.zeros((rows, heads, head_dim), f32),
    )
    k_piece = lax.all_gather(keys, "ctx", axis=0, tiled=True)
    v_piece = lax.all_gather(values, "ctx", axis=0, tiled=True)
    s_piece = lax.all_gather(seg, "ctx", axis=0, tiled=True)
    total_rows = k_piece.shape[0]
    block = min(rows, total_rows)
    count = total_rows // block

    def step(index, state):
        best, total, acc = state
        offset = index * block
        kh = lax.dynamic_slice_in_dim(k_piece, offset, block, 0).reshape(block, heads, head_dim)
        vh = lax.dynamic_slice_in_dim(v_piece, offset, block, 0).reshape(block, heads, head_dim)
        k_seg = lax.dynamic_slice_in_dim(s_piece, offset, block, 0)
        k_place = offset + jnp.arange(block, dtype=jnp.int32)

        def step_compute(unused):
            score = jnp.einsum("qhd,khd->hqk", qh, kh, preferred_element_type=f32) * scale
            mask = pair_mask(place, seg, k_place, k_seg)
            score = jnp.where(mask[None], score, NEGATIVE)
            new_best = jnp.maximum(best, jnp.max(score, axis=-1))
            shrink = jnp.exp(best - new_best)
            prob = jnp.exp(score - new_best[:, :, None])
            new_total = total * shrink + jnp.sum(prob, axis=-1)
            new_acc = acc * shrink.T[:, :, None] + jnp.einsum(
                "hqk,khd->qhd", prob.astype(b16), vh, preferred_element_type=f32
            )
            return (new_best, new_total, new_acc)

        return lax.cond(needed(place, seg, k_place, k_seg), step_compute, lambda unused: state, 0)

    best, total, acc = lax.fori_loop(0, count, step, start_state)
    attn_heads = acc / total.T[:, :, None]
    lse = best + jnp.log(total)
    attn = attn_heads.reshape(rows, width)
    attn_low = attn.astype(b16)
    h1 = inputs + jnp.dot(attn_low, wo, preferred_element_type=f32)
    n2 = norm_rows(h1, norm_ffn).astype(b16)
    probs = jax.nn.softmax(jnp.dot(n2, router, preferred_element_type=f32), axis=-1)
    choice_mask = routes[:, :, None] == jnp.arange(experts, dtype=jnp.int32)[None, None, :]
    gates = jnp.sum(jnp.where(choice_mask, probs[:, None, :], 0.0), axis=-1)
    flat = routes.reshape(-1)
    hits = (flat[:, None] == jnp.arange(experts, dtype=jnp.int32)[None, :]).astype(jnp.int32)
    slot = jnp.sum(jnp.cumsum(hits, axis=0) * hits, axis=1) - 1
    dest = flat * cap + slot
    route_ids = jnp.arange(rows * topk, dtype=jnp.int32)
    source = jnp.zeros((experts * cap,), jnp.int32).at[dest].set(route_ids)
    filled = jnp.zeros((experts * cap,), jnp.bool_).at[dest].set(True)
    send = jnp.where(filled[:, None], n2[source // topk], jnp.zeros((), b16)).reshape(
        experts, cap, width
    )
    received = lax.all_to_all(send, "ctx", split_axis=0, concat_axis=0, tiled=True)
    count = received.shape[1]
    grid = received.reshape(n_ctx, owned, count, width)
    gate_pre = jnp.einsum("secd,edh->sech", grid, expert_gate, preferred_element_type=f32)
    up_pre = jnp.einsum("secd,edh->sech", grid, expert_up, preferred_element_type=f32)
    act = (jax.nn.silu(gate_pre) * up_pre).astype(b16)
    result = jnp.einsum("sech,ehd->secd", act, expert_down, preferred_element_type=f32).astype(b16)
    returned = lax.all_to_all(
        result.reshape(n_ctx * owned, count, width), "ctx", split_axis=0, concat_axis=0, tiled=True
    )
    hidden = gate_pre.shape[-1]
    returned, kept_in, kept_gate, kept_up = (
        returned,
        received,
        gate_pre.reshape(n_ctx * owned, count, hidden),
        up_pre.reshape(n_ctx * owned, count, hidden),
    )
    picked = returned.reshape(experts * cap, width)[dest].reshape(rows, topk, width).astype(f32)
    moe = jnp.einsum("tk,tkd->td", gates, picked, precision=HIGH)
    block_out = (h1 + moe).astype(b16)
    grad_top = out_grad.astype(f32)
    gate_grad = jnp.einsum("td,tkd->tk", grad_top, picked, precision=HIGH)
    down_in = (gates[:, :, None] * grad_top[:, None, :]).astype(b16).reshape(rows * topk, width)
    back_send = jnp.where(filled[:, None], down_in[source], jnp.zeros((), b16)).reshape(
        experts, cap, width
    )
    back_recv = lax.all_to_all(back_send, "ctx", split_axis=0, concat_axis=0, tiled=True)
    hidden = kept_gate.shape[-1]
    grid_dy = back_recv.reshape(n_ctx, owned, cap, width)
    grid_x = kept_in.reshape(n_ctx, owned, cap, width)
    gate_pre = kept_gate.reshape(n_ctx, owned, cap, hidden)
    up_pre = kept_up.reshape(n_ctx, owned, cap, hidden)
    sigma = jax.nn.sigmoid(gate_pre)
    silu = jax.nn.silu(gate_pre)
    act = (silu * up_pre).astype(b16)
    dact = jnp.einsum("secd,ehd->sech", grid_dy, expert_down, preferred_element_type=f32)
    dgate_pre = (dact * up_pre * sigma * (1.0 + gate_pre * (1.0 - sigma))).astype(b16)
    dup_pre = (dact * silu).astype(b16)
    down_term = jnp.einsum("sech,secd->ehd", act, grid_dy, preferred_element_type=f32)
    gate_term = jnp.einsum("secd,sech->edh", grid_x, dgate_pre, preferred_element_type=f32)
    up_term = jnp.einsum("secd,sech->edh", grid_x, dup_pre, preferred_element_type=f32)
    entry_grad = (
        jnp.einsum("sech,edh->secd", dgate_pre, expert_gate, preferred_element_type=f32)
        + jnp.einsum("sech,edh->secd", dup_pre, expert_up, preferred_element_type=f32)
    ).astype(b16)
    entry_back = lax.all_to_all(
        entry_grad.reshape(n_ctx * owned, cap, width),
        "ctx",
        split_axis=0,
        concat_axis=0,
        tiled=True,
    )
    route_grad = jnp.sum(
        entry_back.reshape(experts * cap, width)[dest].reshape(rows, topk, width).astype(f32),
        axis=1,
    )
    gate_grad_out, up_grad_out, down_grad_out = (
        lax.psum_scatter(
            gate_term.astype(jnp.bfloat16), "dp", scatter_dimension=2, tiled=True
        ).astype(jnp.float32),
        lax.psum_scatter(
            up_term.astype(jnp.bfloat16), "dp", scatter_dimension=2, tiled=True
        ).astype(jnp.float32),
        lax.psum_scatter(
            down_term.astype(jnp.bfloat16), "dp", scatter_dimension=1, tiled=True
        ).astype(jnp.float32),
    )
    prob_grad = jnp.sum(jnp.where(choice_mask, gate_grad[:, :, None], 0.0), axis=1)
    logit_grad = probs * (prob_grad - jnp.sum(probs * prob_grad, axis=-1, keepdims=True))
    router_term = jnp.dot(n2.astype(f32).T, logit_grad, precision=HIGH)
    n2_grad = route_grad + jnp.dot(logit_grad, router.astype(f32).T, precision=HIGH)
    unused_value, ffn_back = jax.vjp(norm_rows, h1, norm_ffn)
    h1_part, ffn_gain_grad = ffn_back(n2_grad)
    h1_grad = grad_top + h1_part
    h1_low = h1_grad.astype(b16)
    attn_grad = jnp.dot(h1_low, wo.T, preferred_element_type=f32).astype(b16)
    gh = attn_grad.reshape(rows, heads, head_dim)
    delta = jnp.einsum("qhd,qhd->hq", gh.astype(f32), attn_heads, precision=HIGH)
    local_index = jnp.arange(rows, dtype=jnp.int32)

    def key_step(index, state):
        moving, query_grad = state
        k_move, v_move, s_move, key_acc, value_acc = moving
        anchor = (rank - index + n_ctx) % n_ctx
        k_place = anchor * rows + local_index
        dq, dk, dv = pair_grads(
            qh,
            gh,
            lse,
            delta,
            place,
            seg,
            k_move.astype(b16).reshape(rows, heads, head_dim),
            v_move.astype(b16).reshape(rows, heads, head_dim),
            k_place,
            s_move,
            scale,
            needed(place, seg, k_place, s_move),
        )
        moving = (
            shifted(k_move.astype(jnp.bfloat16), "ctx", 1).astype(k_move.dtype),
            shifted(v_move.astype(jnp.bfloat16), "ctx", 1).astype(v_move.dtype),
            shifted(s_move, "ctx", 1),
            shifted((key_acc + dk.reshape(rows, width)).astype(jnp.bfloat16), "ctx", 1).astype(
                jnp.float32
            ),
            shifted((value_acc + dv.reshape(rows, width)).astype(jnp.bfloat16), "ctx", 1).astype(
                jnp.float32
            ),
        )
        return (moving, query_grad + dq)

    start_keys = (
        (
            keys.astype(f32),
            values.astype(f32),
            seg,
            jnp.zeros((rows, width), f32),
            jnp.zeros((rows, width), f32),
        ),
        jnp.zeros((rows, heads, head_dim), f32),
    )
    (unused_k, unused_v, unused_s, key_grad, value_grad), query_grad = lax.fori_loop(
        0, n_ctx, key_step, start_keys
    )
    query_grad = query_grad.reshape(rows, width)
    unused_query, query_back = jax.vjp(
        lambda proj, gain: qk_post(proj, gain, place, heads), qp, norm_query
    )
    qp_grad, query_gain_grad = query_back(query_grad)
    unused_key, key_back = jax.vjp(
        lambda proj, gain: qk_post(proj, gain, place, heads), kp, norm_key
    )
    kp_grad, key_gain_grad = key_back(key_grad)
    qp_low = qp_grad.astype(b16)
    kp_low = kp_grad.astype(b16)
    vp_low = value_grad.astype(b16)
    n1_grad = (
        jnp.dot(qp_low, wq.T, preferred_element_type=f32)
        + jnp.dot(kp_low, wk.T, preferred_element_type=f32)
        + jnp.dot(vp_low, wv.T, preferred_element_type=f32)
    )
    unused_norm, attn_back = jax.vjp(norm_rows, inputs, norm_attn)
    input_part, attn_gain_grad = attn_back(n1_grad)
    tokens_grad = (h1_grad + input_part).astype(b16)
    contract = (((0,), (0,)), ((), ()))
    stacked = lax.psum_scatter(
        jnp.concatenate(
            [
                lax.dot_general(n1, qp_low, contract, preferred_element_type=f32),
                lax.dot_general(n1, kp_low, contract, preferred_element_type=f32),
                lax.dot_general(n1, vp_low, contract, preferred_element_type=f32),
                lax.dot_general(attn_low, h1_low, contract, preferred_element_type=f32),
            ],
            axis=1,
        ),
        ("dp", "ctx"),
        scatter_dimension=0,
        tiled=True,
    )
    wq_grad = stacked[:, :width]
    wk_grad = stacked[:, width : 2 * width]
    wv_grad = stacked[:, 2 * width : 3 * width]
    wo_grad = stacked[:, 3 * width :]
    attn_gain_sum, query_gain_sum, key_gain_sum, ffn_gain_sum, router_sum = lax.psum(
        (attn_gain_grad, query_gain_grad, key_gain_grad, ffn_gain_grad, router_term), ("dp", "ctx")
    )
    return (
        block_out,
        tokens_grad,
        attn_gain_sum,
        query_gain_sum,
        key_gain_sum,
        ffn_gain_sum,
        wq_grad,
        wk_grad,
        wv_grad,
        wo_grad,
        router_sum,
        gate_grad_out,
        up_grad_out,
        down_grad_out,
    )


B16 = jnp.bfloat16
F32 = jnp.float32
LANES = 128
NT = (((1,), (1,)), ((), ()))
TN = (((0,), (0,)), ((), ()))


def dot(a, b, dims=(((1,), (0,)), ((), ()))):
    return lax.dot_general(a, b, dims, preferred_element_type=F32)


def ring_of(chips):
    return [2 * p if p < chips // 2 else 2 * (chips - 1 - p) + 1 for p in range(chips)]


def rows_of(ids_ref, index, rows, core):
    return pl.ds(pl.multiple_of(ids_ref[1 + index] * (2 * rows) + core * rows, rows), rows)


def column(row):
    return jnp.broadcast_to(row, (row.shape[1], row.shape[1])).T


def rows_sum(v):
    return jnp.sum(v.T, axis=0, keepdims=True)


def joined(refs):
    return jnp.concatenate([r[...] for r in refs], axis=0)


def project_kernel(ids_ref, *refs, first):
    x_refs, (near_own, far_own, near_other, far_other, own_ref, other_ref, square_ref) = refs[:-7], refs[-7:]
    blocks, rows, wide = own_ref.shape
    hd = wide // 3
    x = joined(x_refs)
    half = x.shape[1] // 2
    own = dot(x[:, :half], near_own[...]) + dot(x[:, half:], far_own[...])
    other = dot(x[:, :half], near_other[...]) + dot(x[:, half:], far_other[...])
    own_ref[...] = own.reshape(own_ref.shape)
    other_ref[...] = other.reshape(other_ref.shape)
    square_ref[...] = jnp.zeros_like(square_ref)
    chips = square_ref.shape[0] // 3
    for i in range(blocks):
        at = slice(i * rows, (i + 1) * rows)
        for j in range(2):
            cols = slice(j * hd, (j + 1) * hd)
            total = rows_sum(own[at, cols] * own[at, cols] + other[at, cols] * other[at, cols])
            square_ref[pl.ds(j * chips + ids_ref[1 + first + i], 1)] = total


def turned(v, cosine, sine):
    return v * cosine + pltpu.roll(v, v.shape[1] // 2, 1) * sine


def turned_back(v, cosine, sine):
    return v * cosine + pltpu.roll(v * sine, v.shape[1] // 2, 1)


def head_kernel(ids_ref, *refs, width):
    raw, (total_ref, cos_ref, sin_ref, gain_ref, own_ref, other_ref) = refs[:4], refs[4:]
    chips, rows, wide = own_ref.shape
    hd = wide // 3
    cut = raw[0].shape[0]
    for i in range(chips):
        for h, out in ((0, own_ref), (2, other_ref)):
            src = raw[h][i] if i < cut else raw[h + 1][i - cut]
            for j in range(2):
                scale = column(lax.rsqrt(total_ref[pl.ds(j * chips + ids_ref[1 + i], 1)] / width + EPS))
                v = src[:, j * hd : (j + 1) * hd] * scale * gain_ref[h + j : h + j + 1]
                out[i, :, j * hd : (j + 1) * hd] = turned(v, cos_ref[i], sin_ref[i]).astype(B16)
            out[i, :, 2 * hd :] = src[:, 2 * hd :].astype(B16)


def inner_kernel(ids_ref, grad_own, grad_other, *refs, width):
    raw, (total_ref, cos_ref, sin_ref, gain_ref, inner_ref, out_ref) = refs[:4], refs[4:]
    chips, rows, wide = grad_own.shape
    hd = wide // 3
    cut = raw[0].shape[0]
    out = [jnp.zeros((rows, hd), F32)] * 4
    inner_ref[...] = jnp.zeros_like(inner_ref)
    for i in range(chips):
        for j in range(2):
            cols = slice(j * hd, (j + 1) * hd)
            scale = column(lax.rsqrt(total_ref[pl.ds(j * chips + ids_ref[1 + i], 1)] / width + EPS))
            inner = jnp.zeros((rows, hd), F32)
            for h, grad in ((0, grad_own), (2, grad_other)):
                src = (raw[h][i] if i < cut else raw[h + 1][i - cut])[:, cols]
                v = turned_back(grad[i, :, cols].astype(F32), cos_ref[i], sin_ref[i]) * src
                inner += v * gain_ref[h + j : h + j + 1]
                out[h + j] = out[h + j] + v * scale
            inner_ref[pl.ds(j * chips + ids_ref[1 + i], 1)] = rows_sum(inner)
    out_ref[...] = jnp.concatenate([jnp.sum(v, axis=0, keepdims=True) for v in out] * 2, axis=0)


def finish_kernel(ids_ref, grad_own, grad_other, *refs, width):
    raw, refs = refs[:4], refs[4:]
    total_ref, inner_ref, cos_ref, sin_ref, gain_ref, near_own, far_own, near_other, far_other = refs[:9]
    x_refs, (low_own, low_other, part_ref, sum_ref) = refs[9:-4], refs[-4:]
    chips, rows, wide = grad_own.shape
    hd = wide // 3
    cut = raw[0].shape[0]
    for i in range(chips):
        for j in range(3):
            cols = slice(j * hd, (j + 1) * hd)
            if j < 2:
                at = pl.ds(j * chips + ids_ref[1 + i], 1)
                scale = lax.rsqrt(total_ref[at] / width + EPS)
                inner = column(scale * scale * scale * (inner_ref[at] / width))
                scale = column(scale)
            for h, grad, out in ((0, grad_own, low_own), (2, grad_other, low_other)):
                v = grad[i, :, cols].astype(F32)
                if j < 2:
                    src = (raw[h][i] if i < cut else raw[h + 1][i - cut])[:, cols]
                    v = turned_back(v, cos_ref[i], sin_ref[i])
                    v = scale * (v * gain_ref[h + j : h + j + 1]) - src * inner
                out[i, :, cols] = v.astype(B16)
    x = joined(x_refs)
    half = width // 2
    group = min(4, chips)
    for lo in range(0, chips, group):
        own = low_own[lo : lo + group].reshape(group * rows, wide)
        other = low_other[lo : lo + group].reshape(group * rows, wide)
        for first, w_own, w_other in ((0, near_own, near_other), (half, far_own, far_other)):
            part = dot(own, w_own[...], NT) + dot(other, w_other[...], NT)
            part_ref[lo : lo + group, :, first : first + half] = part.astype(B16).reshape(group, rows, half)
            seen = x[lo * rows : (lo + group) * rows, first : first + half].astype(F32)
            term = jnp.sum((part * seen).reshape(group * rows // 8, 8, half), axis=0)
            if lo == 0:
                sum_ref[:, first : first + half] = term
            else:
                sum_ref[:, first : first + half] += term


def outer_kernel(*refs, count):
    outs = refs[-count - 4 : -5] + (refs[-5:-1],)
    left, x_refs, x_all = refs[:count], refs[count : -count - 4], refs[-1]
    x_all[...] = joined(x_refs)
    width = x_all.shape[1]
    tile = min(512, width)
    for l_ref, out in zip(left, outs):
        chips, rows, wide = l_ref.shape
        turn = l_ref[...].reshape(chips * rows, wide).astype(F32).T.astype(B16)
        parts = out if isinstance(out, tuple) else (out,)
        size = parts[0].shape[1]
        for lo in range(0, width, tile):
            parts[lo // size][:, lo % size : lo % size + tile] = dot(turn, x_all[:, lo : lo + tile]).astype(B16 if len(parts) > 1 else out.dtype)


def head_grad_kernel(*refs):
    x_refs, (w_ref, own_ref, other_ref) = refs[:-3], refs[-3:]
    hd = own_ref.shape[2]
    grad = dot(joined(x_refs), w_ref[...], NT).astype(B16)
    own_ref[...] = grad[:, :hd].reshape(own_ref.shape)
    other_ref[...] = grad[:, hd:].reshape(other_ref.shape)


def slab_kernel(ids_ref, *refs):
    w_refs, out_ref = refs[:-1], refs[-1]
    chips, rows, wide = out_ref.shape
    hd = wide // len(w_refs)
    for c in range(chips):
        spot = pl.ds(pl.multiple_of((2 * c + ids_ref[0]) * hd, hd), hd)
        for i, w_ref in enumerate(w_refs):
            out_ref[c, :, i * hd : (i + 1) * hd] = w_ref[:, spot]


def on_core(kernel, shapes, operands, flops, scratch=()):
    scalars = operands[0].dtype == jnp.int32
    memory = [pltpu.SMEM if scalars and i == 0 else pltpu.VMEM for i in range(len(operands))]
    size = sum(v.size * v.dtype.itemsize for v in list(operands) + jax.tree.leaves(shapes))
    return pl.pallas_call(
        kernel,
        in_specs=[pl.BlockSpec(memory_space=m) for m in memory],
        out_shape=shapes,
        scratch_shapes=scratch,
        compiler_params=pltpu.CompilerParams(vmem_limit_bytes=56 * 2**20),
        cost_estimate=pl.CostEstimate(flops=flops, bytes_accessed=size, transcendentals=0),
    )(*operands)


def seg_column(row_ref, col_ref, rows):
    for lo in range(0, row_ref.shape[1], rows):
        col_ref[lo : lo + rows] = jnp.concatenate([column(row_ref[:, lo : lo + rows])] * (col_ref.shape[1] // rows), axis=1)


def attention_forward(
    ids_ref, mine_ref, other_ref, seg_row_ref, out_ref, lse_ref, qkv_ref, low_ref, away_ref, seg_col_ref, *, block, scale
):
    chips, rows, hd = mine_ref.shape[0], mine_ref.shape[1], mine_ref.shape[2] // 3
    core = ids_ref[0]
    for i in range(chips):
        qkv_ref[rows_of(ids_ref, i, rows, core)] = mine_ref[i]
        qkv_ref[rows_of(ids_ref, i, rows, 1 - core)] = other_ref[i]
    total = qkv_ref.shape[0]
    seg_column(seg_row_ref, seg_col_ref, rows)
    vt = qkv_ref[:, 2 * hd :].astype(F32).T.astype(B16)
    for index in range(total // block):
        low, high = index * block, (index + 1) * block
        score = dot(qkv_ref[:high, hd : 2 * hd], qkv_ref[low:high, :hd], NT) * scale
        key = lax.broadcasted_iota(jnp.int32, (high, block), 0)
        query = low + lax.broadcasted_iota(jnp.int32, (high, block), 1)
        seen = (key <= query) & (seg_col_ref[:high] == seg_row_ref[:, low:high])
        score = jnp.where(seen, score, NEGATIVE)
        best = jnp.max(score, axis=0, keepdims=True)
        prob = jnp.exp(score - best)
        norm = jnp.sum(prob, axis=0, keepdims=True)
        out = dot(vt[:, :high], prob.astype(B16)) / norm
        out_ref[low:high] = out.T
        lse_ref[:, low:high] = best + jnp.log(norm)
    for i in range(chips):
        low_ref[i] = out_ref[rows_of(ids_ref, i, rows, core)].astype(B16)
        away_ref[i] = out_ref[rows_of(ids_ref, i, rows, 1 - core)].astype(B16)


def attention_backward(
    ids_ref, qkv_ref, *refs, block, scale
):
    out_ref, lse_ref, seg_row_ref, low_ref, away_ref, g_ref, grad_ref, seg_col_ref = refs[4:]
    chips, rows, wide = low_ref.shape
    hd = wide // 3
    core = ids_ref[0]
    cut = refs[0].shape[0]
    for i in range(chips):
        g_ref[rows_of(ids_ref, i, rows, core)] = refs[0][i] if i < cut else refs[1][i - cut]
        g_ref[rows_of(ids_ref, i, rows, 1 - core)] = refs[2][i] if i < cut else refs[3][i - cut]
    total = qkv_ref.shape[0]
    seg_column(seg_row_ref, seg_col_ref, rows)
    kt = qkv_ref[:, hd : 2 * hd].astype(F32).T.astype(B16)
    grad_ref[...] = jnp.zeros_like(grad_ref)
    for index in range(total // block):
        low, high = index * block, (index + 1) * block
        q, g = qkv_ref[low:high, :hd], g_ref[low:high]
        delta = jnp.sum((g.astype(F32) * out_ref[low:high]).T, axis=0, keepdims=True)
        score = dot(qkv_ref[:high, hd : 2 * hd], q, NT) * scale
        key = lax.broadcasted_iota(jnp.int32, (high, block), 0)
        query = low + lax.broadcasted_iota(jnp.int32, (high, block), 1)
        seen = (key <= query) & (seg_col_ref[:high] == seg_row_ref[:, low:high])
        prob = jnp.where(seen, jnp.exp(score - lse_ref[:, low:high]), 0.0)
        dprob = dot(qkv_ref[:high, 2 * hd :], g, NT)
        dscore = (prob * (dprob - delta)).astype(B16)
        grad_ref[:high, hd : 2 * hd] += dot(dscore, q) * scale
        grad_ref[:high, 2 * hd :] += dot(prob.astype(B16), g)
        grad_ref[low:high, :hd] = dot(kt[:, :high], dscore).T * scale
    for i in range(chips):
        low_ref[i] = grad_ref[rows_of(ids_ref, i, rows, core)]
        away_ref[i] = grad_ref[rows_of(ids_ref, i, rows, 1 - core)].astype(B16)


def expert_kernel(ids_ref, *refs, shards, experts, fresh):
    x_refs, refs = refs[:shards], refs[shards:]
    g_refs, refs = refs[:shards], refs[shards:]
    wg_ref, wu_ref, wd_ref = refs[:3]
    refs = refs[3 if fresh else 8 :]
    moe_ref, dx_ref, ag_ref, dg_ref, du_ref, xs_ref, gs_ref, moe_acc, dx_acc, dgate_acc = refs
    expert, step, steps = pl.program_id(0), pl.program_id(1), pl.num_programs(1)
    rows, width = g_refs[0].shape
    first = (expert == 0) & (step == 0)

    @pl.when(first)
    def _():
        for i in range(shards):
            xs_ref[i] = x_refs[i][:, :width]
            gs_ref[i] = g_refs[i][...]
        dgate_acc[...] = jnp.zeros_like(dgate_acc)

    x = xs_ref[...].reshape(shards * rows, width)
    g = gs_ref[...].reshape(shards * rows, width)
    lane = lax.broadcasted_iota(jnp.int32, (rows, LANES), 1)
    mine = (lane < 3 * experts) & (lax.rem(lane, experts) == ids_ref[expert])
    gate = jnp.concatenate(
        [
            jnp.sum(jnp.where(mine, x_refs[i][:, width:].astype(F32), 0.0), axis=1, keepdims=True)
            for i in range(shards)
        ],
        axis=0,
    )
    wg, wu, wd = wg_ref[0], wu_ref[0], wd_ref[0]
    gate_pre = dot(x, wg)
    up_pre = dot(x, wu)
    dact = dot(g, wd, NT)
    sigma = 1.0 / (1.0 + jnp.exp(-gate_pre))
    silu = gate_pre * sigma
    act = silu * up_pre
    part = jnp.sum(act * dact, axis=1, keepdims=True)
    lane = lax.broadcasted_iota(jnp.int32, (shards * rows, LANES), 1)
    dgate_acc[...] += jnp.where(lane == ids_ref[expert], part, 0.0)
    act_low = (gate * act).astype(B16)
    dact = gate * dact
    dgate_pre = (dact * up_pre * sigma * (1.0 + gate_pre * (1.0 - sigma))).astype(B16)
    dup_pre = (dact * silu).astype(B16)
    ag_ref[...] = act_low.reshape(ag_ref.shape)
    dg_ref[...] = dgate_pre.reshape(dg_ref.shape)
    du_ref[...] = dup_pre.reshape(du_ref.shape)
    moe = dot(act_low, wd)
    dx = dot(dgate_pre, wg, NT) + dot(dup_pre, wu, NT)

    @pl.when(first)
    def _():
        moe_acc[...] = moe
        dx_acc[...] = dx

    @pl.when(jnp.logical_not(first))
    def _():
        moe_acc[...] += moe
        dx_acc[...] += dx

    @pl.when((expert == pl.num_programs(0) - 1) & (step == steps - 1))
    def _():
        moe_ref[...] = moe_acc[...].astype(B16).reshape(moe_ref.shape)
        dx_ref[:, :, :width] = dx_acc[...].astype(B16).reshape(shards, rows, width)
        rest = dgate_acc[...]
        sent = jnp.zeros_like(rest)
        for i in range(3):
            piece = rest.astype(B16).astype(F32)
            rest -= piece
            sent += pltpu.roll(piece, i * experts, 1) if i else piece
        dx_ref[:, :, width:] = sent.astype(B16).reshape(shards, rows, LANES)


def expert_rows(ids, xs, gs, wg, wu, wd, kept, spot, total, experts):
    shards = len(xs)
    rows, width = gs[0].shape
    pair, _, hidden = wg.shape
    tile = min(512, hidden)
    steps = hidden // tile
    whole = lambda a: pl.BlockSpec(a.shape, lambda e, j, ids: (0, 0))
    flat = pl.BlockSpec((shards, rows, tile), lambda e, j, ids: (spot, 0, e * steps + j))
    full = pl.BlockSpec((shards, rows, width), lambda e, j, ids: (spot, 0, 0))
    alone = pl.BlockSpec((shards, rows, width), lambda e, j, ids: (0, 0, 0))
    in_specs = [whole(a) for a in xs + gs] + [
        pl.BlockSpec((1, width, tile), lambda e, j, ids: (e, 0, j)),
        pl.BlockSpec((1, width, tile), lambda e, j, ids: (e, 0, j)),
        pl.BlockSpec((1, tile, width), lambda e, j, ids: (e, j, 0)),
    ]
    operands = list(xs) + list(gs) + [wg, wu, wd]
    aliases = {}
    if kept is not None:
        base = 1 + len(operands)
        in_specs += [pl.BlockSpec(memory_space=pl.ANY)] * len(kept)
        operands += list(kept)
        aliases = {base + i: 2 + i for i in range(len(kept))}
    kept_hidden = jax.ShapeDtypeStruct((total, rows, pair * hidden), B16)
    kept_width = jax.ShapeDtypeStruct((total, rows, width), B16)
    out = pl.pallas_call(
        functools.partial(expert_kernel, shards=shards, experts=experts, fresh=kept is None),
        grid_spec=pltpu.PrefetchScalarGridSpec(
            num_scalar_prefetch=1,
            grid=(pair, steps),
            in_specs=in_specs,
            out_specs=[
                alone,
                pl.BlockSpec((shards, rows, width + LANES), lambda e, j, ids: (0, 0, 0)),
                flat,
                flat,
                flat,
                full,
                full,
            ],
            scratch_shapes=[
                pltpu.VMEM((shards * rows, width), F32),
                pltpu.VMEM((shards * rows, width), F32),
                pltpu.VMEM((shards * rows, LANES), F32),
            ],
        ),
        out_shape=[
            jax.ShapeDtypeStruct((shards, rows, width), B16),
            jax.ShapeDtypeStruct((shards, rows, width + LANES), B16),
            kept_hidden,
            kept_hidden,
            kept_hidden,
            kept_width,
            kept_width,
        ],
        input_output_aliases=aliases,
        compiler_params=pltpu.CompilerParams(vmem_limit_bytes=56 * 2**20),
        cost_estimate=pl.CostEstimate(
            flops=12 * shards * rows * width * hidden * pair,
            bytes_accessed=6 * width * hidden * pair,
            transcendentals=shards * rows * hidden * pair,
        ),
    )(ids, *operands)
    return out[0], out[1], out[2:]


def rows_grad_kernel(ids_ref, there_ref, back_ref, own_ref, grad_ref, rows_ref, gain_ref, out_ref):
    rows, width = grad_ref.shape
    core, blocks = ids_ref[0], width // rows
    spots, parts = [], []
    total, inner = jnp.zeros((rows, rows), F32), jnp.zeros((rows, rows), F32)
    for i in range(blocks):
        at = slice(i * rows, (i + 1) * rows)
        chip, parity = i % (blocks // 2), core if i < blocks // 2 else 1 - core
        spot = pl.ds(pl.multiple_of((2 * chip + parity) * rows, rows), rows)
        part = there_ref[:, at].astype(F32) + back_ref[:, at].astype(F32) + own_ref[:, at].astype(F32)
        part = part * gain_ref[:, spot]
        v = rows_ref[:, spot].astype(F32)
        total += v * v
        inner += v * part
        spots.append(spot)
        parts.append(part)
    scale = lax.rsqrt(jnp.sum(total, axis=1, keepdims=True) / width + EPS)
    inner = scale * scale * scale * (jnp.sum(inner, axis=1, keepdims=True) / width)
    for spot, part in zip(spots, parts):
        out_ref[:, spot] = (grad_ref[:, spot] + part * scale - rows_ref[:, spot].astype(F32) * inner).astype(B16)


def expert_grad_kernel(left_ref, right_ref, *refs, pieces, whole):
    step = pl.program_id(0)
    term = dot(left_ref[...], right_ref[...], TN)
    for i in range(pieces):

        @pl.when(step == i)
        def _():
            if whole:
                refs[-1][...] = (term + refs[i][...].astype(F32)).astype(B16)
            else:
                refs[i][...] = term.astype(B16)


def expert_grad_term(left, right, arrived, left_at, right_at, size, across):
    rows = left.shape[0]
    high, wide = (size, right.shape[1]) if across else (left.shape[1], size)
    pieces = 4
    tile = high // pieces
    first = left_at // tile
    in_specs = [
        pl.BlockSpec((rows, tile), lambda j: (0, first + j)),
        pl.BlockSpec((rows, wide), lambda j: (0, right_at // size)),
    ]
    fixed = pl.BlockSpec((tile, wide), lambda j: (0, 0))
    whole = arrived is not None
    return pl.pallas_call(
        functools.partial(expert_grad_kernel, pieces=pieces, whole=whole),
        grid=(pieces,),
        in_specs=in_specs + ([fixed] * pieces if whole else []),
        out_specs=pl.BlockSpec((tile, wide), lambda j: (j, 0)) if whole else [fixed] * pieces,
        out_shape=jax.ShapeDtypeStruct((high, wide), B16) if whole else [jax.ShapeDtypeStruct((tile, wide), B16)] * pieces,
        compiler_params=pltpu.CompilerParams(vmem_limit_bytes=56 * 2**20),
        cost_estimate=pl.CostEstimate(
            flops=2 * rows * high * wide, bytes_accessed=2 * (rows * (high + wide) + high * wide), transcendentals=0
        ),
    )(left, right, *(arrived if whole else []))


def split_three(v):
    high = lax.reduce_precision(v, exponent_bits=8, mantissa_bits=7)
    middle = lax.reduce_precision(v - high, exponent_bits=8, mantissa_bits=7)
    return [part.astype(B16) for part in (high, middle, v - high - middle)]


def local_fast(
    tokens,
    doc_starts,
    routes,
    norm_attn,
    norm_query,
    norm_key,
    norm_ffn,
    w_query,
    w_key,
    w_value,
    w_output,
    router,
    expert_gate,
    expert_up,
    expert_down,
    out_grad,
):
    devices = lax.axis_size("ctx")
    rank = lax.axis_index("ctx")
    group = lax.axis_index("dp")
    chips = devices // 2
    chip, core = rank // 2, rank % 2
    rows, width = tokens.shape
    experts = router.shape[1]
    hd = width // HEADS
    scale = hd ** (-0.5)
    half = chips // 2
    order = ring_of(chips)
    right = [(2 * order[p] + c, 2 * order[(p + 1) % chips] + c) for p in range(chips) for c in range(2)]
    left = [(b, a) for a, b in right]
    place_in_ring = jnp.where(chip % 2 == 0, chip // 2, chips - 1 - chip // 2)
    same_core = [[2 * c + p for c in range(chips)] for p in range(2)]

    def to_right(v):
        return lax.ppermute(v, "ctx", right)

    def to_left(v):
        return lax.ppermute(v, "ctx", left)

    def core_swap(v):
        return lax.ppermute(v, "ctx", [(i, i ^ 1) for i in range(devices)])

    def group_swap(v):
        return lax.ppermute(v, "dp", [(0, 1), (1, 0)])

    def chip_at(offset):
        spot = (place_in_ring + offset + chips) % chips
        return jnp.where(spot < half, 2 * spot, 2 * (chips - 1 - spot) + 1)

    offsets = [0] + [s * o for o in range(1, half) for s in (1, -1)] + [half]

    def after(v, *others):
        return lax.optimization_barrier((v,) + others)[0]

    places = jnp.stack([chip_at(o) for o in offsets])

    def ring_gather(v, ties=(), first=None):
        ties = list(ties) + [()] * half
        cut = v.shape[0] // 32 * 16
        got = {0: v}

        def send(i, one, two):
            if i == 0 and first:
                return first
            one, two = lax.optimization_barrier((one, two) + tuple(ties[i]))[:2]
            return to_right(one), to_left(two)

        for o in range(1, half):
            got[-o], got[o] = send(o - 1, got[-(o - 1)], got[o - 1])
        first, second = send(half - 1, got[-(half - 1)][:cut], got[half - 1][cut:])
        got[half] = jnp.concatenate([first, second], axis=0)
        got["halves"] = (first, second)
        return got

    def in_ring(got):
        return jnp.concatenate([got[o] for o in offsets], axis=0)

    def ring_steps(part, axis):
        far = part(half)
        cut = far.shape[axis] // 2 // LANES * LANES
        a_cut = lambda v: lax.slice_in_dim(v, 0, cut, axis=axis)
        b_cut = lambda v: lax.slice_in_dim(v, cut, v.shape[axis], axis=axis)
        there, back = lax.optimization_barrier((a_cut(far), b_cut(far)))
        there, back = yield to_right(there), to_left(back)
        near, other = part(half - 1), part(1 - half)
        there = jnp.concatenate([a_cut(near) + there, b_cut(near)], axis=axis)
        back = jnp.concatenate([a_cut(other), b_cut(other) + back], axis=axis)
        for o in range(half - 2, 0, -1):
            there, back = lax.optimization_barrier((there, back))
            there, back = yield to_right(there), to_left(back)
            there, back = there + part(o), back + part(-o)
        there, back = lax.optimization_barrier((there, back))
        there, back = yield to_right(there), to_left(back)
        return there, back, part(0)

    def tied(values, *others, all_of=False):
        return lax.optimization_barrier(tuple(values) + others)[: None if all_of else len(values)]

    def ring_sum(part, axis, work=()):
        work = list(work) + [None] * half
        ring = ring_steps(part, axis)
        values, token = next(ring), None
        for i in range(half):
            arrays, then = work[i](token) if work[i] else ((), None)
            values = tied(values, *arrays, all_of=True)
            if then:
                then(*values[2:])
            values = values[:2]
            token = values[0]
            try:
                values = ring.send(values)
            except StopIteration as end:
                return end.value

    def total_of(terms):
        return sum(v.astype(F32) for v in terms)

    def sum_chips(v):
        step = 2
        while step < devices:
            v = v + lax.ppermute(v, "ctx", [(i, i ^ step) for i in range(devices)])
            step *= 2
        return v

    def by_core(mine, other, axis):
        return jnp.where(core == 0, jnp.stack([mine, other], axis), jnp.stack([other, mine], axis))

    def pick(pair, which):
        return jnp.where(which == 0, pair[0], pair[1])

    def by_parity(v, axis, back=False):
        shape = v.shape
        v = v.reshape(shape[:axis] + ((2, chips, rows) if back else (chips, 2, rows)) + shape[axis + 1 :])
        split = axis if back else axis + 1
        one, two = [lax.index_in_dim(v, i, split, keepdims=False) for i in range(2)]
        one, two = jnp.where(core == 0, one, two), jnp.where(core == 0, two, one)
        return jnp.stack([one, two], axis + 1 if back else axis).reshape(shape)

    wg_pair, wu_pair, wd_pair = [(w, core_swap(w)) for w in (expert_gate, expert_up, expert_down)]

    inputs = tokens.astype(F32)
    n1 = by_parity(norm_rows(inputs, norm_attn).astype(B16), 1)

    slab = on_core(
        slab_kernel,
        jax.ShapeDtypeStruct((chips, rows, 3 * hd), B16),
        [group[None].astype(jnp.int32), w_query, w_key, w_value],
        0,
    )
    first = (to_right(n1), to_left(n1))
    near_head = lax.all_to_all(slab, "ctx", split_axis=0, concat_axis=0, axis_index_groups=same_core, tiled=True)
    far_head = group_swap(near_head)
    near_head, *first = tied((near_head,) + first)
    n1_got = {0: n1, -1: first[0], 1: first[1]}
    for o in range(2, half):
        one, two = lax.optimization_barrier((n1_got[1 - o], n1_got[o - 1]) + ((near_head,) if o == 2 else ()))[:2]
        n1_got[-o], n1_got[o] = to_right(one), to_left(two)
    own = jnp.where(core == group, near_head, far_head)
    other = jnp.where(core == group, far_head, near_head)
    w_in = [v.reshape(chips * rows, 3 * hd) for v in (own, core_swap(other), other, core_swap(own))]
    w_out = jnp.concatenate([w_output, core_swap(w_output)], axis=0)

    count = chips * rows
    place = (2 * places[:, None, None] + core) * rows + lax.broadcasted_iota(jnp.int32, (chips, rows, 1), 1)
    freq = THETA ** (-jnp.arange(hd // 2, dtype=F32) * 2.0 / hd)
    angle = place.astype(F32) * freq[None, None, :]
    cosine, sine = jnp.cos(angle), jnp.sin(angle)
    cosine = jnp.concatenate([cosine] * 2, axis=2)
    sine = jnp.concatenate([-sine, sine], axis=2)
    ids = jnp.concatenate([core[None], places]).astype(jnp.int32)
    ranks = (rank, rank ^ 1)
    gains = jnp.stack([lax.dynamic_slice(g, (r * hd,), (hd,)) for r in ranks for g in (norm_query, norm_key)])
    gains = jnp.concatenate([gains, gains], axis=0)
    early, late = offsets[:5], offsets[5:]
    raw, squares = [None] * 4, [None] * 2

    def project(i, shards):
        blocks = (early, late)[i]
        raw[i], raw[i + 2], squares[i] = on_core(
            functools.partial(project_kernel, first=i * len(early)),
            [jax.ShapeDtypeStruct((len(blocks), rows, 3 * hd), F32)] * 2
            + [jax.ShapeDtypeStruct((3 * chips, rows), F32)],
            [ids] + shards + w_in,
            12 * len(blocks) * rows * width * hd,
        )

    project(0, [n1_got[o] for o in early])
    one, two = lax.optimization_barrier((n1_got[1 - half], n1_got[half - 1], squares[0]))[:2]
    cut = rows // 2
    n1_halves = (to_right(one[:cut]), to_left(two[cut:]))
    project(1, [n1_got[o] for o in late if o != half] + list(n1_halves))
    squares = squares[0] + squares[1]
    top = after(out_grad, *n1_halves)
    top_first = (to_right(top), to_left(top))
    flags = lax.dynamic_update_index_in_dim(jnp.zeros((chips, rows), F32), doc_starts.astype(F32), chip, 0)
    flags = jnp.concatenate([jnp.zeros((2 * chips, rows), F32), flags], axis=0)
    total = sum_chips(after(squares + flags, *top_first))
    one, two = lax.optimization_barrier(top_first + (total,))[:2]
    top_got = {0: out_grad, -1: top_first[0], 1: top_first[1], -2: to_right(one), 2: to_left(two)}
    heads = on_core(
        functools.partial(head_kernel, width=width),
        [jax.ShapeDtypeStruct((chips, rows, 3 * hd), B16)] * 2,
        [ids] + raw + [total, cosine, sine, gains],
        0,
    )

    flags = total[2 * chips :]
    flags = by_core(flags, core_swap(flags), 1).reshape(devices, rows)
    tri = (lax.broadcasted_iota(jnp.int32, (rows, rows), 0) <= lax.broadcasted_iota(jnp.int32, (rows, rows), 1)).astype(F32)
    before = (
        lax.broadcasted_iota(jnp.int32, (devices, devices), 1) < lax.broadcasted_iota(jnp.int32, (devices, devices), 0)
    ).astype(F32)
    seg = jnp.dot(flags, tri) + jnp.dot(before, jnp.broadcast_to(jnp.sum(flags, axis=1, keepdims=True), (devices, rows)))
    everything = devices * rows
    seg_row = seg.reshape(1, everything)
    block = min(256, everything)
    half_wide = everything * everything // 2
    attn, lse, head_qkv, low_own, low_away = on_core(
        functools.partial(attention_forward, block=block, scale=scale),
        [
            jax.ShapeDtypeStruct((everything, hd), F32),
            jax.ShapeDtypeStruct((1, everything), F32),
            jax.ShapeDtypeStruct((everything, 3 * hd), B16),
            jax.ShapeDtypeStruct((chips, rows, hd), B16),
            jax.ShapeDtypeStruct((chips, rows, hd), B16),
        ],
        [ids, heads[0], core_swap(heads[1]), seg_row],
        8 * half_wide * hd,
        [pltpu.VMEM((everything, block), F32)],
    )
    low_other = after(core_swap(low_away), top_got[2], top_got[-2])
    attn_low = jnp.concatenate([low_own, low_other], axis=2).reshape(count, 2 * hd)
    out_part = dot(attn_low, w_out).astype(B16).reshape(chips, rows, width)
    weights = [jnp.concatenate(pair, axis=0) for pair in (wg_pair, wu_pair, wd_pair)]
    h1 = inputs + total_of(
        ring_sum(
            lambda o: out_part[offsets.index(o)], 1, [None] + [lambda token, w=w: ((w,), None) for w in weights]
        )
    )

    n2 = norm_rows(h1, norm_ffn).astype(B16)
    probs = jax.nn.softmax(dot(n2, router), axis=-1)
    chosen = jnp.sum(
        (routes[:, :, None] == jnp.arange(experts, dtype=jnp.int32)[None, None, :]).astype(F32), axis=1
    )
    sent = split_three(probs * chosen)
    sent.append(jnp.zeros((rows, LANES - 3 * experts), B16))
    names = jnp.stack(ranks).astype(jnp.int32)
    moe_part, dn2_part = {}, {}
    kept = None

    def run_experts(which, spot):
        moe, dn2, kept_now = expert_rows(
            names, [n2_got[o] for o in which], [top_got[o] for o in which], *weights, kept, spot, chips, experts
        )
        for i, o in enumerate(which):
            moe_part[o], dn2_part[o] = moe[i], dn2[i]
        return kept_now

    n2_got = {0: jnp.concatenate([n2] + sent, axis=1)}
    n2_got[-1], n2_got[1] = to_right(n2_got[0]), to_left(n2_got[0])
    one, two, three, four = lax.optimization_barrier((n2_got[-1], n2_got[1], top_got[-2], top_got[2]))
    n2_got[-2], n2_got[2] = to_right(one), to_left(two)
    top_got[-3], top_got[3] = to_right(three), to_left(four)
    kept = run_experts([0, 1, -1], 0)
    one, two, three, four = lax.optimization_barrier((n2_got[-2], n2_got[2], top_got[-3], top_got[3], kept[0]))[:4]
    n2_got[-3], n2_got[3] = to_right(one), to_left(two)
    top_got[half] = jnp.concatenate([to_right(three[:cut]), to_left(four[cut:])], axis=0)
    kept = run_experts([2, -2], 3)
    one, two = lax.optimization_barrier((n2_got[-3], n2_got[3], kept[0]))[:2]
    n2_got[half] = jnp.concatenate([to_right(one[:cut]), to_left(two[cut:])], axis=0)
    kept = run_experts([3, -3, half], 1)
    kept = [v.reshape(count, -1) for v in kept]
    act_all, dgate_pre_all, dup_pre_all, x_all, top_all = kept

    hidden = expert_gate.shape[2]
    pairs = [(act_all, top_all), (x_all, dgate_pre_all), (x_all, dup_pre_all)]

    def expert_term(i, expert, token, plus):
        left_side, right_side = pairs[i]
        across = i == 0
        at = expert * hidden
        return expert_grad_term(
            left_side if token is None else after(left_side, token), right_side, plus, at if across else 0, 0 if across else at, hidden, across
        )

    arrived, expert_grads = [], []

    def own_term(i):
        def run(token):
            return (expert_term(i, 0, token, arrived[i]),), then

        def then(mine):
            expert_grads.append(lax.psum_scatter(mine, "dp", scatter_dimension=0 if i == 0 else 1, tiled=True))

        return run

    def other_term(i):
        def run(token):
            return tuple(expert_term(i, 1, token, None)), then

        def then(*other):
            arrived.append([core_swap(v) for v in other])

        return run

    n2_sum = total_of(
        ring_sum(lambda o: dn2_part[o], 1, [other_term(0), own_term(0), other_term(1), other_term(2)])
    )
    dgates = n2_sum[:, width : width + 3 * experts].reshape(rows, 3, experts)
    n2_sum = n2_sum[:, :width]
    prob_grad = (dgates[:, 0] + dgates[:, 1] + dgates[:, 2]) * chosen
    logit_grad = probs * (prob_grad - jnp.sum(probs * prob_grad, axis=-1, keepdims=True))
    router_term = lax.dot_general(logit_grad, n2.astype(F32), TN, precision=HIGH)
    n2_grad = n2_sum + jnp.dot(logit_grad, router.astype(F32).T, precision=HIGH)
    grad_top = out_grad.astype(F32)
    unused_value, ffn_back = jax.vjp(norm_rows, h1, norm_ffn)
    h1_part, ffn_gain_grad = ffn_back(n2_grad)
    h1_grad = grad_top + h1_part
    h1_low = h1_grad.astype(B16)

    grad_parts = [None] * 4

    def head_grad(i, shards):
        blocks = (early, late)[i]
        grad_parts[i], away = on_core(
            head_grad_kernel,
            [jax.ShapeDtypeStruct((len(blocks), rows, hd), B16)] * 2,
            shards + [w_out],
            4 * len(blocks) * rows * width * hd,
        )
        grad_parts[i + 2] = core_swap(away)
        return away

    h1_got = {0: h1_low, -1: to_right(h1_low), 1: to_left(h1_low)}

    def from_across(v, step, token):
        return lax.ppermute(after(v, token), "ctx", [(i, i ^ step) for i in range(devices)])

    early_sum = jnp.concatenate([router_term, ffn_gain_grad[None]], axis=0)
    early_sum = early_sum + core_swap(early_sum)
    one, two = h1_got[-1], h1_got[1]
    for o in range(1, half):
        mine, then = own_term(o)(h1_low if o == 1 else one) if o < 3 else ((), lambda: None)
        h1_got[-o], h1_got[o], *mine = tied((h1_got[-o], h1_got[o]), *mine, all_of=True)
        then(*mine)
        one, two = h1_got[-o], h1_got[o]
        if o < half - 1:
            h1_got[-o - 1], h1_got[o + 1] = to_right(one), to_left(two)
    cut = rows // 2
    h1_halves = (to_right(one[:cut]), to_left(two[cut:]))
    away = head_grad(0, [after(h1_got[0], one)] + [h1_got[o] for o in early[1:]])
    h1_halves = tied(h1_halves, away)
    away = head_grad(1, [h1_got[o] for o in late if o != half] + list(h1_halves))
    moe_ring = ring_steps(lambda o: after(moe_part[o], *h1_halves) if o == half else moe_part[o], 1)
    moe_got = next(moe_ring)
    attn = after(attn, *moe_got)
    moe_got = moe_ring.send(moe_got)
    early_recv = from_across(early_sum, 2, away)
    grads_own, grads_away = on_core(
        functools.partial(attention_backward, block=block, scale=scale),
        [jax.ShapeDtypeStruct((chips, rows, 3 * hd), t) for t in (F32, B16)],
        [ids, head_qkv] + grad_parts + [attn, lse, seg_row],
        20 * half_wide * hd,
        [
            pltpu.VMEM((everything, hd), B16),
            pltpu.VMEM((everything, 3 * hd), F32),
            pltpu.VMEM((everything, block), F32),
        ],
    )
    grads = [grads_own, core_swap(grads_away)]
    inner, gain_grads = on_core(
        functools.partial(inner_kernel, width=width),
        [jax.ShapeDtypeStruct((3 * chips, rows), F32), jax.ShapeDtypeStruct((8, hd), F32)],
        [ids] + grads + raw + [total, cosine, sine, gains],
        0,
    )
    n1_shards = [n1_got[o] for o in offsets if o != half] + list(n1_halves)
    h1_shards = [h1_got[o] for o in offsets if o != half] + list(h1_halves)
    o_own, *o_away = on_core(
        functools.partial(outer_kernel, count=2),
        [jax.ShapeDtypeStruct((hd, width), F32)] + [jax.ShapeDtypeStruct((hd, width // 4), B16)] * 4,
        [low_own, after(low_other, gain_grads)] + h1_shards,
        4 * count * width * hd,
        [pltpu.VMEM((count, width), B16)],
    )
    o_head = o_own + jnp.concatenate([core_swap(v) for v in o_away], axis=1).astype(F32)
    o_recv = group_swap(o_head.astype(B16))

    early_recv, *moe_got = tied((early_recv,) + tuple(moe_got), grads_own)
    moe_got = moe_ring.send(tuple(moe_got))
    early_sum = early_sum + early_recv
    early_recv = from_across(early_sum, 4, grads_own)
    inner, *moe_got = tied((inner,) + tuple(moe_got), o_own)
    inner = sum_chips(inner)
    moe_got = moe_ring.send(tied(moe_got, inner))
    early_sum = early_sum + after(early_recv, inner)
    early_recv = from_across(early_sum, 8, inner)
    low_grad_own, low_grad_other, n1_part, attn_gain = on_core(
        functools.partial(finish_kernel, width=width),
        [
            jax.ShapeDtypeStruct((chips, rows, 3 * hd), B16),
            jax.ShapeDtypeStruct((chips, rows, 3 * hd), B16),
            jax.ShapeDtypeStruct((chips, rows, width), B16),
            jax.ShapeDtypeStruct((8, width), F32),
        ],
        [ids] + grads + raw + [total, inner, cosine, sine, gains] + w_in + n1_shards,
        12 * count * width * hd,
    )
    attn_gain = by_parity(jnp.sum(attn_gain, axis=0), 0, back=True) / norm_attn

    n1_part, *moe_got = tied((n1_part,) + tuple(moe_got))
    try:
        moe_ring.send(tuple(moe_got))
    except StopIteration as end:
        moe_sum = total_of(end.value)

    def heads_grads(token):
        return on_core(
            functools.partial(outer_kernel, count=2),
            [jax.ShapeDtypeStruct((3 * hd, width), F32)] + [jax.ShapeDtypeStruct((3 * hd, width // 4), B16)] * 4,
            [low_grad_own, after(low_grad_other, token)] + n1_shards,
            12 * count * width * hd,
            [pltpu.VMEM((count, width), B16)],
        )

    def placed(parts):
        out = jnp.zeros((width,), F32)
        for r, v in zip(ranks, parts):
            out = lax.dynamic_update_slice(out, v, (r * hd,))
        return out

    gain_grads = after(gain_grads, n1_part)
    late_sum = jnp.stack([attn_gain, placed(gain_grads[0::2][:2]), placed(gain_grads[1::2][:2])])
    late_sum = [late_sum + core_swap(late_sum)]
    w_got, grads_out = [], []

    def kept_by(which):
        size = width // 4
        return jnp.concatenate(
            [lax.dynamic_slice_in_dim(w_got[0], i * (width // 2) + which * size, size, 1) for i in range(2)], axis=1
        )

    early = []

    expert_done = []

    def swap_heads(early_recv, w_own, *w_away):
        expert_done.extend(w_away[4:])
        w_away = w_away[:4]
        early.append(group_swap(early_sum + early_recv))
        early.append(early_sum + early_recv)
        w_away = [core_swap(v) for v in w_away]
        w_got.append(w_own + jnp.concatenate(w_away[2:] + w_away[:2], axis=1).astype(F32))
        w_got.append(group_swap(kept_by(1 - group).astype(B16)))

    def in_slabs(w_mine):
        w_mine = w_mine.T.astype(B16).reshape(2, chips // 2, rows, 3 * hd)
        return by_core(w_mine[0], w_mine[1], 1).reshape(devices, -1, 3 * hd)

    def join(w_mine):
        w_got.append(lax.all_to_all(w_mine, "ctx", split_axis=0, concat_axis=0, tiled=True))

    def small_step(step, others=lambda token: (), then=None):
        def run(token):
            return (from_across(late_sum[-1], step, token),) + tuple(others(token)), finish

        def finish(v, *rest):
            late_sum.append(late_sum[-1] + v)
            if then:
                then(*rest)

        return run

    n1_grad = ring_sum(
        lambda o: n1_part[offsets.index(o)],
        1,
        [
            lambda token: ([early_recv] + list(heads_grads(n1_part)) + expert_grads, swap_heads),
            small_step(2, lambda token: [in_slabs(kept_by(group) + after(w_got[1], token).astype(F32))], join),
            small_step(4),
            small_step(
                8,
                lambda token: [after(v, token).astype(F32)[None] for v in expert_done] + w_got[2:],
                lambda *v: grads_out.extend(v),
            ),
        ],
    )
    down_grad_out, gate_grad_out, up_grad_out, w_got = grads_out
    o_head = (o_head + after(o_recv, n1_grad[0]).astype(F32)).astype(B16)
    wo_grad = None
    for i in range(2):
        moves = [
            (g * devices + devices // 2 * g + j, g * devices + 2 * j + i) for g in range(2) for j in range(devices // 2)
        ]
        size = width // (2 * devices)
        piece = lax.ppermute(o_head[i * size : (i + 1) * size], ("dp", "ctx"), moves)
        wo_grad = piece if wo_grad is None else jnp.where(core == 0, wo_grad, piece)
    wo_grad = wo_grad.astype(F32)
    late_sum = after(late_sum[-1], n1_grad[0])
    late_sum = late_sum + group_swap(late_sum)
    early_sum = early[1] + after(early[0], n1_grad[0])
    w_got = w_got.transpose(1, 0, 2).astype(F32)
    slab_rows = w_got.shape[0]
    wq_grad, wk_grad, wv_grad = [
        w_got[:, :, i * hd : (i + 1) * hd].reshape(slab_rows, width) for i in range(3)
    ]
    tokens_grad = on_core(
        rows_grad_kernel,
        jax.ShapeDtypeStruct((rows, width), B16),
        [ids, *n1_grad, h1_grad, tokens, norm_attn.reshape(1, width)],
        0,
    )

    block_out = (h1 + moe_sum).astype(B16)
    router_sum, gain_sums = early_sum[:experts].T, [early_sum[experts]] + [late_sum[i] for i in range(3)]
    return (
        block_out,
        tokens_grad,
        gain_sums[1],
        gain_sums[2],
        gain_sums[3],
        gain_sums[0],
        wq_grad,
        wk_grad,
        wv_grad,
        wo_grad,
        router_sum,
        gate_grad_out,
        up_grad_out,
        down_grad_out,
    )


def local(*args):
    devices, groups = lax.axis_size("ctx"), lax.axis_size("dp")
    experts, owned = args[11].shape[1], args[12].shape[0]
    fits = devices == HEADS == experts and groups == 2 and owned == 1 and 3 * experts <= LANES
    return (local_fast if fits else local_general)(*args)


def solution(mesh):
    return jax.shard_map(
        local,
        mesh=mesh,
        in_specs=(
            P(("dp", "ctx"), None),
            P(("dp", "ctx")),
            P(("dp", "ctx"), None),
            P(),
            P(),
            P(),
            P(),
            P("ctx", None),
            P("ctx", None),
            P("ctx", None),
            P("ctx", None),
            P(),
            P("ctx", None, None),
            P("ctx", None, None),
            P("ctx", None, None),
            P(("dp", "ctx"), None),
        ),
        out_specs=(
            P(("dp", "ctx"), None),
            P(("dp", "ctx"), None),
            P(),
            P(),
            P(),
            P(),
            P(("dp", "ctx"), None),
            P(("dp", "ctx"), None),
            P(("dp", "ctx"), None),
            P(("dp", "ctx"), None),
            P(),
            P("ctx", None, "dp"),
            P("ctx", None, "dp"),
            P("ctx", "dp", None),
        ),
        check_vma=False,
    )
```

```python
import functools

import jax
import jax.numpy as jnp
from jax import lax
from jax.experimental import pallas as pl
from jax.experimental.pallas import tpu as pltpu
from jax.sharding import PartitionSpec as P

HEADS = 16


EPS = 1e-05
THETA = 10000.0
NEGATIVE = -1e30
HIGH = lax.Precision.HIGHEST


def spread(block, axis, holder):
    block = jnp.where(lax.axis_index(axis) == holder, block, jnp.zeros_like(block))
    return lax.psum(block, axis)


def shifted(shard, axis, by):
    devices = lax.axis_size(axis)
    return lax.ppermute(shard, axis, [(i, (i + by) % devices) for i in range(devices)])


def norm_rows(v, gain):
    return v * lax.rsqrt(jnp.mean(v * v, axis=-1, keepdims=True) + EPS) * gain


def rotate(v, place):
    half = v.shape[-1] // 2
    freq = THETA ** (-jnp.arange(half, dtype=jnp.float32) * 2.0 / v.shape[-1])
    angle = place.astype(jnp.float32)[:, None] * freq[None, :]
    cosine = jnp.cos(angle)[:, None, :]
    sine = jnp.sin(angle)[:, None, :]
    first = v[..., :half]
    second = v[..., half:]
    return jnp.concatenate(
        [first * cosine - second * sine, second * cosine + first * sine], axis=-1
    )


def qk_post(proj, gain, place, heads):
    count, width = proj.shape
    normed = norm_rows(proj, gain).reshape(count, heads, width // heads)
    return rotate(normed, place).reshape(count, width)


def needed(q_place, q_seg, k_place, k_seg):
    return (k_place[0] <= q_place[-1]) & (k_seg[-1] >= q_seg[0])


def pair_mask(q_place, q_seg, k_place, k_seg):
    return (k_place[None, :] <= q_place[:, None]) & (k_seg[None, :] == q_seg[:, None])


def pair_grads(qh, gh, lse, delta, q_place, q_seg, kh, vh, k_place, k_seg, scale, wanted):

    def pair_compute(unused):
        score = jnp.einsum("qhd,khd->hqk", qh, kh, preferred_element_type=jnp.float32) * scale
        mask = pair_mask(q_place, q_seg, k_place, k_seg)
        prob = jnp.where(mask[None], jnp.exp(score - lse[:, :, None]), 0.0)
        dprob = jnp.einsum("qhd,khd->hqk", gh, vh, preferred_element_type=jnp.float32)
        dscore = (prob * (dprob - delta[:, :, None])).astype(jnp.bfloat16)
        prob_low = prob.astype(jnp.bfloat16)
        dq = jnp.einsum("hqk,khd->qhd", dscore, kh, preferred_element_type=jnp.float32) * scale
        dk = jnp.einsum("hqk,qhd->khd", dscore, qh, preferred_element_type=jnp.float32) * scale
        dv = jnp.einsum("hqk,qhd->khd", prob_low, gh, preferred_element_type=jnp.float32)
        return (dq, dk, dv)

    def skip(unused):
        return (
            jnp.zeros(qh.shape, jnp.float32),
            jnp.zeros(kh.shape, jnp.float32),
            jnp.zeros(vh.shape, jnp.float32),
        )

    return lax.cond(wanted, pair_compute, skip, 0)


def local_general(
    tokens,
    doc_starts,
    routes,
    norm_attn,
    norm_query,
    norm_key,
    norm_ffn,
    w_query,
    w_key,
    w_value,
    w_output,
    router,
    expert_gate,
    expert_up,
    expert_down,
    out_grad,
):
    f32 = jnp.float32
    b16 = jnp.bfloat16
    n_ctx = lax.axis_size("ctx")
    rank = lax.axis_index("ctx")
    rows, width = tokens.shape
    heads = HEADS
    head_dim = width // heads
    scale = head_dim ** (-0.5)
    experts = router.shape[1]
    topk = routes.shape[1]
    owned = expert_gate.shape[0]
    cap = max(2, rows * topk * 3 // (2 * experts))
    starts = jnp.sum(doc_starts)
    first_count = spread(starts, "ctx", 0)
    before = jnp.where(rank > 0, first_count, 0)
    seg = before + jnp.cumsum(doc_starts)
    place = rank * rows + jnp.arange(rows, dtype=jnp.int32)
    wq, wk, wv, wo = (
        lax.all_gather(w_query, "ctx", axis=0, tiled=True),
        lax.all_gather(w_key, "ctx", axis=0, tiled=True),
        lax.all_gather(w_value, "ctx", axis=0, tiled=True),
        lax.all_gather(w_output, "ctx", axis=0, tiled=True),
    )
    inputs = tokens.astype(f32)
    n1 = norm_rows(inputs, norm_attn).astype(b16)
    qp = jnp.dot(n1, wq, preferred_element_type=f32)
    kp = jnp.dot(n1, wk, preferred_element_type=f32)
    vp = jnp.dot(n1, wv, preferred_element_type=f32)
    query = qk_post(qp, norm_query, place, heads).astype(b16)
    keys = qk_post(kp, norm_key, place, heads).astype(b16)
    values = vp.astype(b16)
    qh = query.reshape(rows, heads, head_dim)
    start_state = (
        jnp.full((heads, rows), NEGATIVE, f32),
        jnp.zeros((heads, rows), f32),
        jnp.zeros((rows, heads, head_dim), f32),
    )
    k_piece = lax.all_gather(keys, "ctx", axis=0, tiled=True)
    v_piece = lax.all_gather(values, "ctx", axis=0, tiled=True)
    s_piece = lax.all_gather(seg, "ctx", axis=0, tiled=True)
    total_rows = k_piece.shape[0]
    block = min(rows, total_rows)
    count = total_rows // block

    def step(index, state):
        best, total, acc = state
        offset = index * block
        kh = lax.dynamic_slice_in_dim(k_piece, offset, block, 0).reshape(block, heads, head_dim)
        vh = lax.dynamic_slice_in_dim(v_piece, offset, block, 0).reshape(block, heads, head_dim)
        k_seg = lax.dynamic_slice_in_dim(s_piece, offset, block, 0)
        k_place = offset + jnp.arange(block, dtype=jnp.int32)

        def step_compute(unused):
            score = jnp.einsum("qhd,khd->hqk", qh, kh, preferred_element_type=f32) * scale
            mask = pair_mask(place, seg, k_place, k_seg)
            score = jnp.where(mask[None], score, NEGATIVE)
            new_best = jnp.maximum(best, jnp.max(score, axis=-1))
            shrink = jnp.exp(best - new_best)
            prob = jnp.exp(score - new_best[:, :, None])
            new_total = total * shrink + jnp.sum(prob, axis=-1)
            new_acc = acc * shrink.T[:, :, None] + jnp.einsum(
                "hqk,khd->qhd", prob.astype(b16), vh, preferred_element_type=f32
            )
            return (new_best, new_total, new_acc)

        return lax.cond(needed(place, seg, k_place, k_seg), step_compute, lambda unused: state, 0)

    best, total, acc = lax.fori_loop(0, count, step, start_state)
    attn_heads = acc / total.T[:, :, None]
    lse = best + jnp.log(total)
    attn = attn_heads.reshape(rows, width)
    attn_low = attn.astype(b16)
    h1 = inputs + jnp.dot(attn_low, wo, preferred_element_type=f32)
    n2 = norm_rows(h1, norm_ffn).astype(b16)
    probs = jax.nn.softmax(jnp.dot(n2, router, preferred_element_type=f32), axis=-1)
    choice_mask = routes[:, :, None] == jnp.arange(experts, dtype=jnp.int32)[None, None, :]
    gates = jnp.sum(jnp.where(choice_mask, probs[:, None, :], 0.0), axis=-1)
    flat = routes.reshape(-1)
    hits = (flat[:, None] == jnp.arange(experts, dtype=jnp.int32)[None, :]).astype(jnp.int32)
    slot = jnp.sum(jnp.cumsum(hits, axis=0) * hits, axis=1) - 1
    dest = flat * cap + slot
    route_ids = jnp.arange(rows * topk, dtype=jnp.int32)
    source = jnp.zeros((experts * cap,), jnp.int32).at[dest].set(route_ids)
    filled = jnp.zeros((experts * cap,), jnp.bool_).at[dest].set(True)
    send = jnp.where(filled[:, None], n2[source // topk], jnp.zeros((), b16)).reshape(
        experts, cap, width
    )
    received = lax.all_to_all(send, "ctx", split_axis=0, concat_axis=0, tiled=True)
    count = received.shape[1]
    grid = received.reshape(n_ctx, owned, count, width)
    gate_pre = jnp.einsum("secd,edh->sech", grid, expert_gate, preferred_element_type=f32)
    up_pre = jnp.einsum("secd,edh->sech", grid, expert_up, preferred_element_type=f32)
    act = (jax.nn.silu(gate_pre) * up_pre).astype(b16)
    result = jnp.einsum("sech,ehd->secd", act, expert_down, preferred_element_type=f32).astype(b16)
    returned = lax.all_to_all(
        result.reshape(n_ctx * owned, count, width), "ctx", split_axis=0, concat_axis=0, tiled=True
    )
    hidden = gate_pre.shape[-1]
    returned, kept_in, kept_gate, kept_up = (
        returned,
        received,
        gate_pre.reshape(n_ctx * owned, count, hidden),
        up_pre.reshape(n_ctx * owned, count, hidden),
    )
    picked = returned.reshape(experts * cap, width)[dest].reshape(rows, topk, width).astype(f32)
    moe = jnp.einsum("tk,tkd->td", gates, picked, precision=HIGH)
    block_out = (h1 + moe).astype(b16)
    grad_top = out_grad.astype(f32)
    gate_grad = jnp.einsum("td,tkd->tk", grad_top, picked, precision=HIGH)
    down_in = (gates[:, :, None] * grad_top[:, None, :]).astype(b16).reshape(rows * topk, width)
    back_send = jnp.where(filled[:, None], down_in[source], jnp.zeros((), b16)).reshape(
        experts, cap, width
    )
    back_recv = lax.all_to_all(back_send, "ctx", split_axis=0, concat_axis=0, tiled=True)
    hidden = kept_gate.shape[-1]
    grid_dy = back_recv.reshape(n_ctx, owned, cap, width)
    grid_x = kept_in.reshape(n_ctx, owned, cap, width)
    gate_pre = kept_gate.reshape(n_ctx, owned, cap, hidden)
    up_pre = kept_up.reshape(n_ctx, owned, cap, hidden)
    sigma = jax.nn.sigmoid(gate_pre)
    silu = jax.nn.silu(gate_pre)
    act = (silu * up_pre).astype(b16)
    dact = jnp.einsum("secd,ehd->sech", grid_dy, expert_down, preferred_element_type=f32)
    dgate_pre = (dact * up_pre * sigma * (1.0 + gate_pre * (1.0 - sigma))).astype(b16)
    dup_pre = (dact * silu).astype(b16)
    down_term = jnp.einsum("sech,secd->ehd", act, grid_dy, preferred_element_type=f32)
    gate_term = jnp.einsum("secd,sech->edh", grid_x, dgate_pre, preferred_element_type=f32)
    up_term = jnp.einsum("secd,sech->edh", grid_x, dup_pre, preferred_element_type=f32)
    entry_grad = (
        jnp.einsum("sech,edh->secd", dgate_pre, expert_gate, preferred_element_type=f32)
        + jnp.einsum("sech,edh->secd", dup_pre, expert_up, preferred_element_type=f32)
    ).astype(b16)
    entry_back = lax.all_to_all(
        entry_grad.reshape(n_ctx * owned, cap, width),
        "ctx",
        split_axis=0,
        concat_axis=0,
        tiled=True,
    )
    route_grad = jnp.sum(
        entry_back.reshape(experts * cap, width)[dest].reshape(rows, topk, width).astype(f32),
        axis=1,
    )
    gate_grad_out, up_grad_out, down_grad_out = (
        lax.psum_scatter(
            gate_term.astype(jnp.bfloat16), "dp", scatter_dimension=2, tiled=True
        ).astype(jnp.float32),
        lax.psum_scatter(
            up_term.astype(jnp.bfloat16), "dp", scatter_dimension=2, tiled=True
        ).astype(jnp.float32),
        lax.psum_scatter(
            down_term.astype(jnp.bfloat16), "dp", scatter_dimension=1, tiled=True
        ).astype(jnp.float32),
    )
    prob_grad = jnp.sum(jnp.where(choice_mask, gate_grad[:, :, None], 0.0), axis=1)
    logit_grad = probs * (prob_grad - jnp.sum(probs * prob_grad, axis=-1, keepdims=True))
    router_term = jnp.dot(n2.astype(f32).T, logit_grad, precision=HIGH)
    n2_grad = route_grad + jnp.dot(logit_grad, router.astype(f32).T, precision=HIGH)
    unused_value, ffn_back = jax.vjp(norm_rows, h1, norm_ffn)
    h1_part, ffn_gain_grad = ffn_back(n2_grad)
    h1_grad = grad_top + h1_part
    h1_low = h1_grad.astype(b16)
    attn_grad = jnp.dot(h1_low, wo.T, preferred_element_type=f32).astype(b16)
    gh = attn_grad.reshape(rows, heads, head_dim)
    delta = jnp.einsum("qhd,qhd->hq", gh.astype(f32), attn_heads, precision=HIGH)
    local_index = jnp.arange(rows, dtype=jnp.int32)

    def key_step(index, state):
        moving, query_grad = state
        k_move, v_move, s_move, key_acc, value_acc = moving
        anchor = (rank - index + n_ctx) % n_ctx
        k_place = anchor * rows + local_index
        dq, dk, dv = pair_grads(
            qh,
            gh,
            lse,
            delta,
            place,
            seg,
            k_move.astype(b16).reshape(rows, heads, head_dim),
            v_move.astype(b16).reshape(rows, heads, head_dim),
            k_place,
            s_move,
            scale,
            needed(place, seg, k_place, s_move),
        )
        moving = (
            shifted(k_move.astype(jnp.bfloat16), "ctx", 1).astype(k_move.dtype),
            shifted(v_move.astype(jnp.bfloat16), "ctx", 1).astype(v_move.dtype),
            shifted(s_move, "ctx", 1),
            shifted((key_acc + dk.reshape(rows, width)).astype(jnp.bfloat16), "ctx", 1).astype(
                jnp.float32
            ),
            shifted((value_acc + dv.reshape(rows, width)).astype(jnp.bfloat16), "ctx", 1).astype(
                jnp.float32
            ),
        )
        return (moving, query_grad + dq)

    start_keys = (
        (
            keys.astype(f32),
            values.astype(f32),
            seg,
            jnp.zeros((rows, width), f32),
            jnp.zeros((rows, width), f32),
        ),
        jnp.zeros((rows, heads, head_dim), f32),
    )
    (unused_k, unused_v, unused_s, key_grad, value_grad), query_grad = lax.fori_loop(
        0, n_ctx, key_step, start_keys
    )
    query_grad = query_grad.reshape(rows, width)
    unused_query, query_back = jax.vjp(
        lambda proj, gain: qk_post(proj, gain, place, heads), qp, norm_query
    )
    qp_grad, query_gain_grad = query_back(query_grad)
    unused_key, key_back = jax.vjp(
        lambda proj, gain: qk_post(proj, gain, place, heads), kp, norm_key
    )
    kp_grad, key_gain_grad = key_back(key_grad)
    qp_low = qp_grad.astype(b16)
    kp_low = kp_grad.astype(b16)
    vp_low = value_grad.astype(b16)
    n1_grad = (
        jnp.dot(qp_low, wq.T, preferred_element_type=f32)
        + jnp.dot(kp_low, wk.T, preferred_element_type=f32)
        + jnp.dot(vp_low, wv.T, preferred_element_type=f32)
    )
    unused_norm, attn_back = jax.vjp(norm_rows, inputs, norm_attn)
    input_part, attn_gain_grad = attn_back(n1_grad)
    tokens_grad = (h1_grad + input_part).astype(b16)
    contract = (((0,), (0,)), ((), ()))
    stacked = lax.psum_scatter(
        jnp.concatenate(
            [
                lax.dot_general(n1, qp_low, contract, preferred_element_type=f32),
                lax.dot_general(n1, kp_low, contract, preferred_element_type=f32),
                lax.dot_general(n1, vp_low, contract, preferred_element_type=f32),
                lax.dot_general(attn_low, h1_low, contract, preferred_element_type=f32),
            ],
            axis=1,
        ),
        ("dp", "ctx"),
        scatter_dimension=0,
        tiled=True,
    )
    wq_grad = stacked[:, :width]
    wk_grad = stacked[:, width : 2 * width]
    wv_grad = stacked[:, 2 * width : 3 * width]
    wo_grad = stacked[:, 3 * width :]
    attn_gain_sum, query_gain_sum, key_gain_sum, ffn_gain_sum, router_sum = lax.psum(
        (attn_gain_grad, query_gain_grad, key_gain_grad, ffn_gain_grad, router_term), ("dp", "ctx")
    )
    return (
        block_out,
        tokens_grad,
        attn_gain_sum,
        query_gain_sum,
        key_gain_sum,
        ffn_gain_sum,
        wq_grad,
        wk_grad,
        wv_grad,
        wo_grad,
        router_sum,
        gate_grad_out,
        up_grad_out,
        down_grad_out,
    )


B16 = jnp.bfloat16
F32 = jnp.float32
LANES = 128
NT = (((1,), (1,)), ((), ()))
TN = (((0,), (0,)), ((), ()))


def dot(a, b, dims=(((1,), (0,)), ((), ()))):
    return lax.dot_general(a, b, dims, preferred_element_type=F32)


def ring_of(chips):
    return [2 * p if p < chips // 2 else 2 * (chips - 1 - p) + 1 for p in range(chips)]


def rows_of(ids_ref, index, rows, core):
    return pl.ds(pl.multiple_of(ids_ref[1 + index] * (2 * rows) + core * rows, rows), rows)


def column(row):
    return jnp.broadcast_to(row, (row.shape[1], row.shape[1])).T


def rows_sum(v):
    return jnp.sum(v.T, axis=0, keepdims=True)


def joined(refs):
    return jnp.concatenate([r[...] for r in refs], axis=0)


def project_kernel(ids_ref, *refs, first):
    x_refs, (near_own, far_own, near_other, far_other, own_ref, other_ref, square_ref) = refs[:-7], refs[-7:]
    blocks, rows, wide = own_ref.shape
    hd = wide // 3
    x = joined(x_refs)
    half = x.shape[1] // 2
    own = dot(x[:, :half], near_own[...]) + dot(x[:, half:], far_own[...])
    other = dot(x[:, :half], near_other[...]) + dot(x[:, half:], far_other[...])
    own_ref[...] = own.reshape(own_ref.shape)
    other_ref[...] = other.reshape(other_ref.shape)
    square_ref[...] = jnp.zeros_like(square_ref)
    chips = square_ref.shape[0] // 3
    for i in range(blocks):
        at = slice(i * rows, (i + 1) * rows)
        for j in range(2):
            cols = slice(j * hd, (j + 1) * hd)
            total = rows_sum(own[at, cols] * own[at, cols] + other[at, cols] * other[at, cols])
            square_ref[pl.ds(j * chips + ids_ref[1 + first + i], 1)] = total


def turned(v, cosine, sine):
    return v * cosine + pltpu.roll(v, v.shape[1] // 2, 1) * sine


def turned_back(v, cosine, sine):
    return v * cosine + pltpu.roll(v * sine, v.shape[1] // 2, 1)


def head_kernel(ids_ref, *refs, width):
    raw, (total_ref, cos_ref, sin_ref, gain_ref, own_ref, other_ref) = refs[:4], refs[4:]
    chips, rows, wide = own_ref.shape
    hd = wide // 3
    cut = raw[0].shape[0]
    for i in range(chips):
        for h, out in ((0, own_ref), (2, other_ref)):
            src = raw[h][i] if i < cut else raw[h + 1][i - cut]
            for j in range(2):
                scale = column(lax.rsqrt(total_ref[pl.ds(j * chips + ids_ref[1 + i], 1)] / width + EPS))
                v = src[:, j * hd : (j + 1) * hd] * scale * gain_ref[h + j : h + j + 1]
                out[i, :, j * hd : (j + 1) * hd] = turned(v, cos_ref[i], sin_ref[i]).astype(B16)
            out[i, :, 2 * hd :] = src[:, 2 * hd :].astype(B16)


def inner_kernel(ids_ref, grad_own, grad_other, *refs, width):
    raw, (total_ref, cos_ref, sin_ref, gain_ref, inner_ref, out_ref) = refs[:4], refs[4:]
    chips, rows, wide = grad_own.shape
    hd = wide // 3
    cut = raw[0].shape[0]
    out = [jnp.zeros((rows, hd), F32)] * 4
    inner_ref[...] = jnp.zeros_like(inner_ref)
    for i in range(chips):
        for j in range(2):
            cols = slice(j * hd, (j + 1) * hd)
            scale = column(lax.rsqrt(total_ref[pl.ds(j * chips + ids_ref[1 + i], 1)] / width + EPS))
            inner = jnp.zeros((rows, hd), F32)
            for h, grad in ((0, grad_own), (2, grad_other)):
                src = (raw[h][i] if i < cut else raw[h + 1][i - cut])[:, cols]
                v = turned_back(grad[i, :, cols].astype(F32), cos_ref[i], sin_ref[i]) * src
                inner += v * gain_ref[h + j : h + j + 1]
                out[h + j] = out[h + j] + v * scale
            inner_ref[pl.ds(j * chips + ids_ref[1 + i], 1)] = rows_sum(inner)
    out_ref[...] = jnp.concatenate([jnp.sum(v, axis=0, keepdims=True) for v in out] * 2, axis=0)


def finish_kernel(ids_ref, grad_own, grad_other, *refs, width):
    raw, refs = refs[:4], refs[4:]
    total_ref, inner_ref, cos_ref, sin_ref, gain_ref, near_own, far_own, near_other, far_other = refs[:9]
    x_refs, (low_own, low_other, part_ref, sum_ref) = refs[9:-4], refs[-4:]
    chips, rows, wide = grad_own.shape
    hd = wide // 3
    cut = raw[0].shape[0]
    for i in range(chips):
        for j in range(3):
            cols = slice(j * hd, (j + 1) * hd)
            if j < 2:
                at = pl.ds(j * chips + ids_ref[1 + i], 1)
                scale = lax.rsqrt(total_ref[at] / width + EPS)
                inner = column(scale * scale * scale * (inner_ref[at] / width))
                scale = column(scale)
            for h, grad, out in ((0, grad_own, low_own), (2, grad_other, low_other)):
                v = grad[i, :, cols].astype(F32)
                if j < 2:
                    src = (raw[h][i] if i < cut else raw[h + 1][i - cut])[:, cols]
                    v = turned_back(v, cos_ref[i], sin_ref[i])
                    v = scale * (v * gain_ref[h + j : h + j + 1]) - src * inner
                out[i, :, cols] = v.astype(B16)
    x = joined(x_refs)
    half = width // 2
    group = min(4, chips)
    for lo in range(0, chips, group):
        own = low_own[lo : lo + group].reshape(group * rows, wide)
        other = low_other[lo : lo + group].reshape(group * rows, wide)
        for first, w_own, w_other in ((0, near_own, near_other), (half, far_own, far_other)):
            part = dot(own, w_own[...], NT) + dot(other, w_other[...], NT)
            part_ref[lo : lo + group, :, first : first + half] = part.astype(B16).reshape(group, rows, half)
            seen = x[lo * rows : (lo + group) * rows, first : first + half].astype(F32)
            term = jnp.sum((part * seen).reshape(group * rows // 8, 8, half), axis=0)
            if lo == 0:
                sum_ref[:, first : first + half] = term
            else:
                sum_ref[:, first : first + half] += term


def outer_kernel(*refs, count):
    outs = refs[-count - 4 : -5] + (refs[-5:-1],)
    left, x_refs, x_all = refs[:count], refs[count : -count - 4], refs[-1]
    x_all[...] = joined(x_refs)
    width = x_all.shape[1]
    tile = min(512, width)
    for l_ref, out in zip(left, outs):
        chips, rows, wide = l_ref.shape
        turn = l_ref[...].reshape(chips * rows, wide).astype(F32).T.astype(B16)
        parts = out if isinstance(out, tuple) else (out,)
        size = parts[0].shape[1]
        for lo in range(0, width, tile):
            parts[lo // size][:, lo % size : lo % size + tile] = dot(turn, x_all[:, lo : lo + tile]).astype(B16 if len(parts) > 1 else out.dtype)


def head_grad_kernel(*refs):
    x_refs, (w_ref, own_ref, other_ref) = refs[:-3], refs[-3:]
    hd = own_ref.shape[2]
    grad = dot(joined(x_refs), w_ref[...], NT).astype(B16)
    own_ref[...] = grad[:, :hd].reshape(own_ref.shape)
    other_ref[...] = grad[:, hd:].reshape(other_ref.shape)


def slab_kernel(ids_ref, *refs):
    w_refs, out_ref = refs[:-1], refs[-1]
    chips, rows, wide = out_ref.shape
    hd = wide // len(w_refs)
    for c in range(chips):
        spot = pl.ds(pl.multiple_of((2 * c + ids_ref[0]) * hd, hd), hd)
        for i, w_ref in enumerate(w_refs):
            out_ref[c, :, i * hd : (i + 1) * hd] = w_ref[:, spot]


def on_core(kernel, shapes, operands, flops, scratch=()):
    scalars = operands[0].dtype == jnp.int32
    memory = [pltpu.SMEM if scalars and i == 0 else pltpu.VMEM for i in range(len(operands))]
    size = sum(v.size * v.dtype.itemsize for v in list(operands) + jax.tree.leaves(shapes))
    return pl.pallas_call(
        kernel,
        in_specs=[pl.BlockSpec(memory_space=m) for m in memory],
        out_shape=shapes,
        scratch_shapes=scratch,
        compiler_params=pltpu.CompilerParams(vmem_limit_bytes=56 * 2**20),
        cost_estimate=pl.CostEstimate(flops=flops, bytes_accessed=size, transcendentals=0),
    )(*operands)


def seg_column(row_ref, col_ref, rows):
    for lo in range(0, row_ref.shape[1], rows):
        col_ref[lo : lo + rows] = jnp.concatenate([column(row_ref[:, lo : lo + rows])] * (col_ref.shape[1] // rows), axis=1)


def attention_forward(
    ids_ref, mine_ref, other_ref, seg_row_ref, out_ref, lse_ref, qkv_ref, low_ref, away_ref, seg_col_ref, *, block, scale
):
    chips, rows, hd = mine_ref.shape[0], mine_ref.shape[1], mine_ref.shape[2] // 3
    core = ids_ref[0]
    for i in range(chips):
        qkv_ref[rows_of(ids_ref, i, rows, core)] = mine_ref[i]
        qkv_ref[rows_of(ids_ref, i, rows, 1 - core)] = other_ref[i]
    total = qkv_ref.shape[0]
    seg_column(seg_row_ref, seg_col_ref, rows)
    vt = qkv_ref[:, 2 * hd :].astype(F32).T.astype(B16)
    for index in range(total // block):
        low, high = index * block, (index + 1) * block
        score = dot(qkv_ref[:high, hd : 2 * hd], qkv_ref[low:high, :hd], NT) * scale
        key = lax.broadcasted_iota(jnp.int32, (high, block), 0)
        query = low + lax.broadcasted_iota(jnp.int32, (high, block), 1)
        seen = (key <= query) & (seg_col_ref[:high] == seg_row_ref[:, low:high])
        score = jnp.where(seen, score, NEGATIVE)
        best = jnp.max(score, axis=0, keepdims=True)
        prob = jnp.exp(score - best)
        norm = jnp.sum(prob, axis=0, keepdims=True)
        out = dot(vt[:, :high], prob.astype(B16)) / norm
        out_ref[low:high] = out.T
        lse_ref[:, low:high] = best + jnp.log(norm)
    for i in range(chips):
        low_ref[i] = out_ref[rows_of(ids_ref, i, rows, core)].astype(B16)
        away_ref[i] = out_ref[rows_of(ids_ref, i, rows, 1 - core)].astype(B16)


def attention_backward(
    ids_ref, qkv_ref, *refs, block, scale
):
    out_ref, lse_ref, seg_row_ref, low_ref, away_ref, g_ref, grad_ref, seg_col_ref = refs[4:]
    chips, rows, wide = low_ref.shape
    hd = wide // 3
    core = ids_ref[0]
    cut = refs[0].shape[0]
    for i in range(chips):
        g_ref[rows_of(ids_ref, i, rows, core)] = refs[0][i] if i < cut else refs[1][i - cut]
        g_ref[rows_of(ids_ref, i, rows, 1 - core)] = refs[2][i] if i < cut else refs[3][i - cut]
    total = qkv_ref.shape[0]
    seg_column(seg_row_ref, seg_col_ref, rows)
    kt = qkv_ref[:, hd : 2 * hd].astype(F32).T.astype(B16)
    grad_ref[...] = jnp.zeros_like(grad_ref)
    for index in range(total // block):
        low, high = index * block, (index + 1) * block
        q, g = qkv_ref[low:high, :hd], g_ref[low:high]
        delta = jnp.sum((g.astype(F32) * out_ref[low:high]).T, axis=0, keepdims=True)
        score = dot(qkv_ref[:high, hd : 2 * hd], q, NT) * scale
        key = lax.broadcasted_iota(jnp.int32, (high, block), 0)
        query = low + lax.broadcasted_iota(jnp.int32, (high, block), 1)
        seen = (key <= query) & (seg_col_ref[:high] == seg_row_ref[:, low:high])
        prob = jnp.where(seen, jnp.exp(score - lse_ref[:, low:high]), 0.0)
        dprob = dot(qkv_ref[:high, 2 * hd :], g, NT)
        dscore = (prob * (dprob - delta)).astype(B16)
        grad_ref[:high, hd : 2 * hd] += dot(dscore, q) * scale
        grad_ref[:high, 2 * hd :] += dot(prob.astype(B16), g)
        grad_ref[low:high, :hd] = dot(kt[:, :high], dscore).T * scale
    for i in range(chips):
        low_ref[i] = grad_ref[rows_of(ids_ref, i, rows, core)]
        away_ref[i] = grad_ref[rows_of(ids_ref, i, rows, 1 - core)].astype(B16)


def expert_kernel(ids_ref, *refs, shards, experts, fresh):
    x_refs, refs = refs[:shards], refs[shards:]
    g_refs, refs = refs[:shards], refs[shards:]
    wg_ref, wu_ref, wd_ref = refs[:3]
    refs = refs[3 if fresh else 8 :]
    moe_ref, dx_ref, ag_ref, dg_ref, du_ref, xs_ref, gs_ref, moe_acc, dx_acc, dgate_acc = refs
    expert, step, steps = pl.program_id(0), pl.program_id(1), pl.num_programs(1)
    rows, width = g_refs[0].shape
    first = (expert == 0) & (step == 0)

    @pl.when(first)
    def _():
        for i in range(shards):
            xs_ref[i] = x_refs[i][:, :width]
            gs_ref[i] = g_refs[i][...]
        dgate_acc[...] = jnp.zeros_like(dgate_acc)

    x = xs_ref[...].reshape(shards * rows, width)
    g = gs_ref[...].reshape(shards * rows, width)
    lane = lax.broadcasted_iota(jnp.int32, (rows, LANES), 1)
    mine = (lane < 3 * experts) & (lax.rem(lane, experts) == ids_ref[expert])
    gate = jnp.concatenate(
        [
            jnp.sum(jnp.where(mine, x_refs[i][:, width:].astype(F32), 0.0), axis=1, keepdims=True)
            for i in range(shards)
        ],
        axis=0,
    )
    wg, wu, wd = wg_ref[0], wu_ref[0], wd_ref[0]
    gate_pre = dot(x, wg)
    up_pre = dot(x, wu)
    dact = dot(g, wd, NT)
    sigma = 1.0 / (1.0 + jnp.exp(-gate_pre))
    silu = gate_pre * sigma
    act = silu * up_pre
    part = jnp.sum(act * dact, axis=1, keepdims=True)
    lane = lax.broadcasted_iota(jnp.int32, (shards * rows, LANES), 1)
    dgate_acc[...] += jnp.where(lane == ids_ref[expert], part, 0.0)
    act_low = (gate * act).astype(B16)
    dact = gate * dact
    dgate_pre = (dact * up_pre * sigma * (1.0 + gate_pre * (1.0 - sigma))).astype(B16)
    dup_pre = (dact * silu).astype(B16)
    ag_ref[...] = act_low.reshape(ag_ref.shape)
    dg_ref[...] = dgate_pre.reshape(dg_ref.shape)
    du_ref[...] = dup_pre.reshape(du_ref.shape)
    moe = dot(act_low, wd)
    dx = dot(dgate_pre, wg, NT) + dot(dup_pre, wu, NT)

    @pl.when(first)
    def _():
        moe_acc[...] = moe
        dx_acc[...] = dx

    @pl.when(jnp.logical_not(first))
    def _():
        moe_acc[...] += moe
        dx_acc[...] += dx

    @pl.when((expert == pl.num_programs(0) - 1) & (step == steps - 1))
    def _():
        moe_ref[...] = moe_acc[...].astype(B16).reshape(moe_ref.shape)
        dx_ref[:, :, :width] = dx_acc[...].astype(B16).reshape(shards, rows, width)
        rest = dgate_acc[...]
        sent = jnp.zeros_like(rest)
        for i in range(3):
            piece = rest.astype(B16).astype(F32)
            rest -= piece
            sent += pltpu.roll(piece, i * experts, 1) if i else piece
        dx_ref[:, :, width:] = sent.astype(B16).reshape(shards, rows, LANES)


def expert_rows(ids, xs, gs, wg, wu, wd, kept, spot, total, experts):
    shards = len(xs)
    rows, width = gs[0].shape
    pair, _, hidden = wg.shape
    tile = min(512, hidden)
    steps = hidden // tile
    whole = lambda a: pl.BlockSpec(a.shape, lambda e, j, ids: (0, 0))
    flat = pl.BlockSpec((shards, rows, tile), lambda e, j, ids: (spot, 0, e * steps + j))
    full = pl.BlockSpec((shards, rows, width), lambda e, j, ids: (spot, 0, 0))
    alone = pl.BlockSpec((shards, rows, width), lambda e, j, ids: (0, 0, 0))
    in_specs = [whole(a) for a in xs + gs] + [
        pl.BlockSpec((1, width, tile), lambda e, j, ids: (e, 0, j)),
        pl.BlockSpec((1, width, tile), lambda e, j, ids: (e, 0, j)),
        pl.BlockSpec((1, tile, width), lambda e, j, ids: (e, j, 0)),
    ]
    operands = list(xs) + list(gs) + [wg, wu, wd]
    aliases = {}
    if kept is not None:
        base = 1 + len(operands)
        in_specs += [pl.BlockSpec(memory_space=pl.ANY)] * len(kept)
        operands += list(kept)
        aliases = {base + i: 2 + i for i in range(len(kept))}
    kept_hidden = jax.ShapeDtypeStruct((total, rows, pair * hidden), B16)
    kept_width = jax.ShapeDtypeStruct((total, rows, width), B16)
    out = pl.pallas_call(
        functools.partial(expert_kernel, shards=shards, experts=experts, fresh=kept is None),
        grid_spec=pltpu.PrefetchScalarGridSpec(
            num_scalar_prefetch=1,
            grid=(pair, steps),
            in_specs=in_specs,
            out_specs=[
                alone,
                pl.BlockSpec((shards, rows, width + LANES), lambda e, j, ids: (0, 0, 0)),
                flat,
                flat,
                flat,
                full,
                full,
            ],
            scratch_shapes=[
                pltpu.VMEM((shards * rows, width), F32),
                pltpu.VMEM((shards * rows, width), F32),
                pltpu.VMEM((shards * rows, LANES), F32),
            ],
        ),
        out_shape=[
            jax.ShapeDtypeStruct((shards, rows, width), B16),
            jax.ShapeDtypeStruct((shards, rows, width + LANES), B16),
            kept_hidden,
            kept_hidden,
            kept_hidden,
            kept_width,
            kept_width,
        ],
        input_output_aliases=aliases,
        compiler_params=pltpu.CompilerParams(vmem_limit_bytes=56 * 2**20),
        cost_estimate=pl.CostEstimate(
            flops=12 * shards * rows * width * hidden * pair,
            bytes_accessed=6 * width * hidden * pair,
            transcendentals=shards * rows * hidden * pair,
        ),
    )(ids, *operands)
    return out[0], out[1], out[2:]


def rows_grad_kernel(ids_ref, there_ref, back_ref, own_ref, grad_ref, rows_ref, gain_ref, out_ref):
    rows, width = grad_ref.shape
    core, blocks = ids_ref[0], width // rows
    spots, parts = [], []
    total, inner = jnp.zeros((rows, rows), F32), jnp.zeros((rows, rows), F32)
    for i in range(blocks):
        at = slice(i * rows, (i + 1) * rows)
        chip, parity = i % (blocks // 2), core if i < blocks // 2 else 1 - core
        spot = pl.ds(pl.multiple_of((2 * chip + parity) * rows, rows), rows)
        part = there_ref[:, at].astype(F32) + back_ref[:, at].astype(F32) + own_ref[:, at].astype(F32)
        part = part * gain_ref[:, spot]
        v = rows_ref[:, spot].astype(F32)
        total += v * v
        inner += v * part
        spots.append(spot)
        parts.append(part)
    scale = lax.rsqrt(jnp.sum(total, axis=1, keepdims=True) / width + EPS)
    inner = scale * scale * scale * (jnp.sum(inner, axis=1, keepdims=True) / width)
    for spot, part in zip(spots, parts):
        out_ref[:, spot] = (grad_ref[:, spot] + part * scale - rows_ref[:, spot].astype(F32) * inner).astype(B16)


def expert_grad_kernel(left_ref, right_ref, *refs, pieces, whole):
    step = pl.program_id(0)
    term = dot(left_ref[...], right_ref[...], TN)
    for i in range(pieces):

        @pl.when(step == i)
        def _():
            if whole:
                refs[-1][...] = (term + refs[i][...].astype(F32)).astype(B16)
            else:
                refs[i][...] = term.astype(B16)


def expert_grad_term(left, right, arrived, left_at, right_at, size, across):
    rows = left.shape[0]
    high, wide = (size, right.shape[1]) if across else (left.shape[1], size)
    pieces = 4
    tile = high // pieces
    first = left_at // tile
    in_specs = [
        pl.BlockSpec((rows, tile), lambda j: (0, first + j)),
        pl.BlockSpec((rows, wide), lambda j: (0, right_at // size)),
    ]
    fixed = pl.BlockSpec((tile, wide), lambda j: (0, 0))
    whole = arrived is not None
    return pl.pallas_call(
        functools.partial(expert_grad_kernel, pieces=pieces, whole=whole),
        grid=(pieces,),
        in_specs=in_specs + ([fixed] * pieces if whole else []),
        out_specs=pl.BlockSpec((tile, wide), lambda j: (j, 0)) if whole else [fixed] * pieces,
        out_shape=jax.ShapeDtypeStruct((high, wide), B16) if whole else [jax.ShapeDtypeStruct((tile, wide), B16)] * pieces,
        compiler_params=pltpu.CompilerParams(vmem_limit_bytes=56 * 2**20),
        cost_estimate=pl.CostEstimate(
            flops=2 * rows * high * wide, bytes_accessed=2 * (rows * (high + wide) + high * wide), transcendentals=0
        ),
    )(left, right, *(arrived if whole else []))


def split_three(v):
    high = lax.reduce_precision(v, exponent_bits=8, mantissa_bits=7)
    middle = lax.reduce_precision(v - high, exponent_bits=8, mantissa_bits=7)
    return [part.astype(B16) for part in (high, middle, v - high - middle)]


def local_fast(
    tokens,
    doc_starts,
    routes,
    norm_attn,
    norm_query,
    norm_key,
    norm_ffn,
    w_query,
    w_key,
    w_value,
    w_output,
    router,
    expert_gate,
    expert_up,
    expert_down,
    out_grad,
):
    devices = lax.axis_size("ctx")
    rank = lax.axis_index("ctx")
    group = lax.axis_index("dp")
    chips = devices // 2
    chip, core = rank // 2, rank % 2
    rows, width = tokens.shape
    experts = router.shape[1]
    hd = width // HEADS
    scale = hd ** (-0.5)
    half = chips // 2
    order = ring_of(chips)
    right = [(2 * order[p] + c, 2 * order[(p + 1) % chips] + c) for p in range(chips) for c in range(2)]
    left = [(b, a) for a, b in right]
    place_in_ring = jnp.where(chip % 2 == 0, chip // 2, chips - 1 - chip // 2)
    same_core = [[2 * c + p for c in range(chips)] for p in range(2)]

    def to_right(v):
        return lax.ppermute(v, "ctx", right)

    def to_left(v):
        return lax.ppermute(v, "ctx", left)

    def core_swap(v):
        return lax.ppermute(v, "ctx", [(i, i ^ 1) for i in range(devices)])

    def group_swap(v):
        return lax.ppermute(v, "dp", [(0, 1), (1, 0)])

    def chip_at(offset):
        spot = (place_in_ring + offset + chips) % chips
        return jnp.where(spot < half, 2 * spot, 2 * (chips - 1 - spot) + 1)

    offsets = [0] + [s * o for o in range(1, half) for s in (1, -1)] + [half]

    def after(v, *others):
        return lax.optimization_barrier((v,) + others)[0]

    places = jnp.stack([chip_at(o) for o in offsets])

    def ring_gather(v, ties=(), first=None):
        ties = list(ties) + [()] * half
        cut = v.shape[0] // 32 * 16
        got = {0: v}

        def send(i, one, two):
            if i == 0 and first:
                return first
            one, two = lax.optimization_barrier((one, two) + tuple(ties[i]))[:2]
            return to_right(one), to_left(two)

        for o in range(1, half):
            got[-o], got[o] = send(o - 1, got[-(o - 1)], got[o - 1])
        first, second = send(half - 1, got[-(half - 1)][:cut], got[half - 1][cut:])
        got[half] = jnp.concatenate([first, second], axis=0)
        got["halves"] = (first, second)
        return got

    def in_ring(got):
        return jnp.concatenate([got[o] for o in offsets], axis=0)

    def ring_steps(part, axis):
        far = part(half)
        cut = far.shape[axis] // 2 // LANES * LANES
        a_cut = lambda v: lax.slice_in_dim(v, 0, cut, axis=axis)
        b_cut = lambda v: lax.slice_in_dim(v, cut, v.shape[axis], axis=axis)
        there, back = lax.optimization_barrier((a_cut(far), b_cut(far)))
        there, back = yield to_right(there), to_left(back)
        near, other = part(half - 1), part(1 - half)
        there = jnp.concatenate([a_cut(near) + there, b_cut(near)], axis=axis)
        back = jnp.concatenate([a_cut(other), b_cut(other) + back], axis=axis)
        for o in range(half - 2, 0, -1):
            there, back = lax.optimization_barrier((there, back))
            there, back = yield to_right(there), to_left(back)
            there, back = there + part(o), back + part(-o)
        there, back = lax.optimization_barrier((there, back))
        there, back = yield to_right(there), to_left(back)
        return there, back, part(0)

    def tied(values, *others, all_of=False):
        return lax.optimization_barrier(tuple(values) + others)[: None if all_of else len(values)]

    def ring_sum(part, axis, work=()):
        work = list(work) + [None] * half
        ring = ring_steps(part, axis)
        values, token = next(ring), None
        for i in range(half):
            arrays, then = work[i](token) if work[i] else ((), None)
            values = tied(values, *arrays, all_of=True)
            if then:
                then(*values[2:])
            values = values[:2]
            token = values[0]
            try:
                values = ring.send(values)
            except StopIteration as end:
                return end.value

    def total_of(terms):
        return sum(v.astype(F32) for v in terms)

    def sum_chips(v):
        step = 2
        while step < devices:
            v = v + lax.ppermute(v, "ctx", [(i, i ^ step) for i in range(devices)])
            step *= 2
        return v

    def by_core(mine, other, axis):
        return jnp.where(core == 0, jnp.stack([mine, other], axis), jnp.stack([other, mine], axis))

    def pick(pair, which):
        return jnp.where(which == 0, pair[0], pair[1])

    def by_parity(v, axis, back=False):
        shape = v.shape
        v = v.reshape(shape[:axis] + ((2, chips, rows) if back else (chips, 2, rows)) + shape[axis + 1 :])
        split = axis if back else axis + 1
        one, two = [lax.index_in_dim(v, i, split, keepdims=False) for i in range(2)]
        one, two = jnp.where(core == 0, one, two), jnp.where(core == 0, two, one)
        return jnp.stack([one, two], axis + 1 if back else axis).reshape(shape)

    wg_pair, wu_pair, wd_pair = [(w, core_swap(w)) for w in (expert_gate, expert_up, expert_down)]

    inputs = tokens.astype(F32)
    n1 = by_parity(norm_rows(inputs, norm_attn).astype(B16), 1)

    slab = on_core(
        slab_kernel,
        jax.ShapeDtypeStruct((chips, rows, 3 * hd), B16),
        [group[None].astype(jnp.int32), w_query, w_key, w_value],
        0,
    )
    first = (to_right(n1), to_left(n1))
    near_head = lax.all_to_all(slab, "ctx", split_axis=0, concat_axis=0, axis_index_groups=same_core, tiled=True)
    far_head = group_swap(near_head)
    near_head, *first = tied((near_head,) + first)
    n1_got = {0: n1, -1: first[0], 1: first[1]}
    for o in range(2, half):
        one, two = lax.optimization_barrier((n1_got[1 - o], n1_got[o - 1]) + ((near_head,) if o == 2 else ()))[:2]
        n1_got[-o], n1_got[o] = to_right(one), to_left(two)
    own = jnp.where(core == group, near_head, far_head)
    other = jnp.where(core == group, far_head, near_head)
    w_in = [v.reshape(chips * rows, 3 * hd) for v in (own, core_swap(other), other, core_swap(own))]
    w_out = jnp.concatenate([w_output, core_swap(w_output)], axis=0)

    count = chips * rows
    place = (2 * places[:, None, None] + core) * rows + lax.broadcasted_iota(jnp.int32, (chips, rows, 1), 1)
    freq = THETA ** (-jnp.arange(hd // 2, dtype=F32) * 2.0 / hd)
    angle = place.astype(F32) * freq[None, None, :]
    cosine, sine = jnp.cos(angle), jnp.sin(angle)
    cosine = jnp.concatenate([cosine] * 2, axis=2)
    sine = jnp.concatenate([-sine, sine], axis=2)
    ids = jnp.concatenate([core[None], places]).astype(jnp.int32)
    ranks = (rank, rank ^ 1)
    gains = jnp.stack([lax.dynamic_slice(g, (r * hd,), (hd,)) for r in ranks for g in (norm_query, norm_key)])
    gains = jnp.concatenate([gains, gains], axis=0)
    early, late = offsets[:5], offsets[5:]
    raw, squares = [None] * 4, [None] * 2

    def project(i, shards):
        blocks = (early, late)[i]
        raw[i], raw[i + 2], squares[i] = on_core(
            functools.partial(project_kernel, first=i * len(early)),
            [jax.ShapeDtypeStruct((len(blocks), rows, 3 * hd), F32)] * 2
            + [jax.ShapeDtypeStruct((3 * chips, rows), F32)],
            [ids] + shards + w_in,
            12 * len(blocks) * rows * width * hd,
        )

    project(0, [n1_got[o] for o in early])
    one, two = lax.optimization_barrier((n1_got[1 - half], n1_got[half - 1], squares[0]))[:2]
    cut = rows // 2
    n1_halves = (to_right(one[:cut]), to_left(two[cut:]))
    project(1, [n1_got[o] for o in late if o != half] + list(n1_halves))
    squares = squares[0] + squares[1]
    top = after(out_grad, *n1_halves)
    top_first = (to_right(top), to_left(top))
    flags = lax.dynamic_update_index_in_dim(jnp.zeros((chips, rows), F32), doc_starts.astype(F32), chip, 0)
    flags = jnp.concatenate([jnp.zeros((2 * chips, rows), F32), flags], axis=0)
    total = sum_chips(after(squares + flags, *top_first))
    one, two = lax.optimization_barrier(top_first + (total,))[:2]
    top_got = {0: out_grad, -1: top_first[0], 1: top_first[1], -2: to_right(one), 2: to_left(two)}
    heads = on_core(
        functools.partial(head_kernel, width=width),
        [jax.ShapeDtypeStruct((chips, rows, 3 * hd), B16)] * 2,
        [ids] + raw + [total, cosine, sine, gains],
        0,
    )

    flags = total[2 * chips :]
    flags = by_core(flags, core_swap(flags), 1).reshape(devices, rows)
    tri = (lax.broadcasted_iota(jnp.int32, (rows, rows), 0) <= lax.broadcasted_iota(jnp.int32, (rows, rows), 1)).astype(F32)
    before = (
        lax.broadcasted_iota(jnp.int32, (devices, devices), 1) < lax.broadcasted_iota(jnp.int32, (devices, devices), 0)
    ).astype(F32)
    seg = jnp.dot(flags, tri) + jnp.dot(before, jnp.broadcast_to(jnp.sum(flags, axis=1, keepdims=True), (devices, rows)))
    everything = devices * rows
    seg_row = seg.reshape(1, everything)
    block = min(256, everything)
    half_wide = everything * everything // 2
    attn, lse, head_qkv, low_own, low_away = on_core(
        functools.partial(attention_forward, block=block, scale=scale),
        [
            jax.ShapeDtypeStruct((everything, hd), F32),
            jax.ShapeDtypeStruct((1, everything), F32),
            jax.ShapeDtypeStruct((everything, 3 * hd), B16),
            jax.ShapeDtypeStruct((chips, rows, hd), B16),
            jax.ShapeDtypeStruct((chips, rows, hd), B16),
        ],
        [ids, heads[0], core_swap(heads[1]), seg_row],
        8 * half_wide * hd,
        [pltpu.VMEM((everything, block), F32)],
    )
    low_other = after(core_swap(low_away), top_got[2], top_got[-2])
    attn_low = jnp.concatenate([low_own, low_other], axis=2).reshape(count, 2 * hd)
    out_part = dot(attn_low, w_out).astype(B16).reshape(chips, rows, width)
    weights = [jnp.concatenate(pair, axis=0) for pair in (wg_pair, wu_pair, wd_pair)]
    h1 = inputs + total_of(
        ring_sum(
            lambda o: out_part[offsets.index(o)], 1, [None] + [lambda token, w=w: ((w,), None) for w in weights]
        )
    )

    n2 = norm_rows(h1, norm_ffn).astype(B16)
    probs = jax.nn.softmax(dot(n2, router), axis=-1)
    chosen = jnp.sum(
        (routes[:, :, None] == jnp.arange(experts, dtype=jnp.int32)[None, None, :]).astype(F32), axis=1
    )
    sent = split_three(probs * chosen)
    sent.append(jnp.zeros((rows, LANES - 3 * experts), B16))
    names = jnp.stack(ranks).astype(jnp.int32)
    moe_part, dn2_part = {}, {}
    kept = None

    def run_experts(which, spot):
        moe, dn2, kept_now = expert_rows(
            names, [n2_got[o] for o in which], [top_got[o] for o in which], *weights, kept, spot, chips, experts
        )
        for i, o in enumerate(which):
            moe_part[o], dn2_part[o] = moe[i], dn2[i]
        return kept_now

    n2_got = {0: jnp.concatenate([n2] + sent, axis=1)}
    n2_got[-1], n2_got[1] = to_right(n2_got[0]), to_left(n2_got[0])
    one, two, three, four = lax.optimization_barrier((n2_got[-1], n2_got[1], top_got[-2], top_got[2]))
    n2_got[-2], n2_got[2] = to_right(one), to_left(two)
    top_got[-3], top_got[3] = to_right(three), to_left(four)
    kept = run_experts([0, 1, -1], 0)
    one, two, three, four = lax.optimization_barrier((n2_got[-2], n2_got[2], top_got[-3], top_got[3], kept[0]))[:4]
    n2_got[-3], n2_got[3] = to_right(one), to_left(two)
    top_got[half] = jnp.concatenate([to_right(three[:cut]), to_left(four[cut:])], axis=0)
    kept = run_experts([2, -2], 3)
    one, two = lax.optimization_barrier((n2_got[-3], n2_got[3], kept[0]))[:2]
    n2_got[half] = jnp.concatenate([to_right(one[:cut]), to_left(two[cut:])], axis=0)
    kept = run_experts([3, -3, half], 1)
    kept = [v.reshape(count, -1) for v in kept]
    act_all, dgate_pre_all, dup_pre_all, x_all, top_all = kept

    hidden = expert_gate.shape[2]
    pairs = [(act_all, top_all), (x_all, dgate_pre_all), (x_all, dup_pre_all)]

    def expert_term(i, expert, token, plus):
        left_side, right_side = pairs[i]
        across = i == 0
        at = expert * hidden
        return expert_grad_term(
            left_side if token is None else after(left_side, token), right_side, plus, at if across else 0, 0 if across else at, hidden, across
        )

    arrived, expert_grads = [], []

    def own_term(i):
        def run(token):
            return (expert_term(i, 0, token, arrived[i]),), then

        def then(mine):
            expert_grads.append(lax.psum_scatter(mine, "dp", scatter_dimension=0 if i == 0 else 1, tiled=True))

        return run

    def other_term(i):
        def run(token):
            return tuple(expert_term(i, 1, token, None)), then

        def then(*other):
            arrived.append([core_swap(v) for v in other])

        return run

    n2_sum = total_of(
        ring_sum(lambda o: dn2_part[o], 1, [other_term(0), own_term(0), other_term(1), other_term(2)])
    )
    dgates = n2_sum[:, width : width + 3 * experts].reshape(rows, 3, experts)
    n2_sum = n2_sum[:, :width]
    prob_grad = (dgates[:, 0] + dgates[:, 1] + dgates[:, 2]) * chosen
    logit_grad = probs * (prob_grad - jnp.sum(probs * prob_grad, axis=-1, keepdims=True))
    router_term = lax.dot_general(logit_grad, n2.astype(F32), TN, precision=HIGH)
    n2_grad = n2_sum + jnp.dot(logit_grad, router.astype(F32).T, precision=HIGH)
    grad_top = out_grad.astype(F32)
    unused_value, ffn_back = jax.vjp(norm_rows, h1, norm_ffn)
    h1_part, ffn_gain_grad = ffn_back(n2_grad)
    h1_grad = grad_top + h1_part
    h1_low = h1_grad.astype(B16)

    grad_parts = [None] * 4

    def head_grad(i, shards):
        blocks = (early, late)[i]
        grad_parts[i], away = on_core(
            head_grad_kernel,
            [jax.ShapeDtypeStruct((len(blocks), rows, hd), B16)] * 2,
            shards + [w_out],
            4 * len(blocks) * rows * width * hd,
        )
        grad_parts[i + 2] = core_swap(away)
        return away

    h1_got = {0: h1_low, -1: to_right(h1_low), 1: to_left(h1_low)}

    def from_across(v, step, token):
        return lax.ppermute(after(v, token), "ctx", [(i, i ^ step) for i in range(devices)])

    early_sum = jnp.concatenate([router_term, ffn_gain_grad[None]], axis=0)
    early_sum = early_sum + core_swap(early_sum)
    one, two = h1_got[-1], h1_got[1]
    for o in range(1, half):
        mine, then = own_term(o)(h1_low if o == 1 else one) if o < 3 else ((), lambda: None)
        h1_got[-o], h1_got[o], *mine = tied((h1_got[-o], h1_got[o]), *mine, all_of=True)
        then(*mine)
        one, two = h1_got[-o], h1_got[o]
        if o < half - 1:
            h1_got[-o - 1], h1_got[o + 1] = to_right(one), to_left(two)
    cut = rows // 2
    h1_halves = (to_right(one[:cut]), to_left(two[cut:]))
    away = head_grad(0, [after(h1_got[0], one)] + [h1_got[o] for o in early[1:]])
    h1_halves = tied(h1_halves, away)
    away = head_grad(1, [h1_got[o] for o in late if o != half] + list(h1_halves))
    moe_ring = ring_steps(lambda o: after(moe_part[o], *h1_halves) if o == half else moe_part[o], 1)
    moe_got = next(moe_ring)
    attn = after(attn, *moe_got)
    moe_got = moe_ring.send(moe_got)
    early_recv = from_across(early_sum, 2, away)
    grads_own, grads_away = on_core(
        functools.partial(attention_backward, block=block, scale=scale),
        [jax.ShapeDtypeStruct((chips, rows, 3 * hd), t) for t in (F32, B16)],
        [ids, head_qkv] + grad_parts + [attn, lse, seg_row],
        20 * half_wide * hd,
        [
            pltpu.VMEM((everything, hd), B16),
            pltpu.VMEM((everything, 3 * hd), F32),
            pltpu.VMEM((everything, block), F32),
        ],
    )
    grads = [grads_own, core_swap(grads_away)]
    inner, gain_grads = on_core(
        functools.partial(inner_kernel, width=width),
        [jax.ShapeDtypeStruct((3 * chips, rows), F32), jax.ShapeDtypeStruct((8, hd), F32)],
        [ids] + grads + raw + [total, cosine, sine, gains],
        0,
    )
    n1_shards = [n1_got[o] for o in offsets if o != half] + list(n1_halves)
    h1_shards = [h1_got[o] for o in offsets if o != half] + list(h1_halves)
    o_own, *o_away = on_core(
        functools.partial(outer_kernel, count=2),
        [jax.ShapeDtypeStruct((hd, width), F32)] + [jax.ShapeDtypeStruct((hd, width // 4), B16)] * 4,
        [low_own, after(low_other, gain_grads)] + h1_shards,
        4 * count * width * hd,
        [pltpu.VMEM((count, width), B16)],
    )
    o_head = o_own + jnp.concatenate([core_swap(v) for v in o_away], axis=1).astype(F32)
    o_recv = group_swap(o_head.astype(B16))

    early_recv, *moe_got = tied((early_recv,) + tuple(moe_got), grads_own)
    moe_got = moe_ring.send(tuple(moe_got))
    early_sum = early_sum + early_recv
    early_recv = from_across(early_sum, 4, grads_own)
    inner, *moe_got = tied((inner,) + tuple(moe_got), o_own)
    inner = sum_chips(inner)
    moe_got = moe_ring.send(tied(moe_got, inner))
    early_sum = early_sum + after(early_recv, inner)
    early_recv = from_across(early_sum, 8, inner)
    low_grad_own, low_grad_other, n1_part, attn_gain = on_core(
        functools.partial(finish_kernel, width=width),
        [
            jax.ShapeDtypeStruct((chips, rows, 3 * hd), B16),
            jax.ShapeDtypeStruct((chips, rows, 3 * hd), B16),
            jax.ShapeDtypeStruct((chips, rows, width), B16),
            jax.ShapeDtypeStruct((8, width), F32),
        ],
        [ids] + grads + raw + [total, inner, cosine, sine, gains] + w_in + n1_shards,
        12 * count * width * hd,
    )
    attn_gain = by_parity(jnp.sum(attn_gain, axis=0), 0, back=True) / norm_attn

    n1_part, *moe_got = tied((n1_part,) + tuple(moe_got))
    try:
        moe_ring.send(tuple(moe_got))
    except StopIteration as end:
        moe_sum = total_of(end.value)

    def heads_grads(token):
        return on_core(
            functools.partial(outer_kernel, count=2),
            [jax.ShapeDtypeStruct((3 * hd, width), F32)] + [jax.ShapeDtypeStruct((3 * hd, width // 4), B16)] * 4,
            [low_grad_own, after(low_grad_other, token)] + n1_shards,
            12 * count * width * hd,
            [pltpu.VMEM((count, width), B16)],
        )

    def placed(parts):
        out = jnp.zeros((width,), F32)
        for r, v in zip(ranks, parts):
            out = lax.dynamic_update_slice(out, v, (r * hd,))
        return out

    gain_grads = after(gain_grads, n1_part)
    late_sum = jnp.stack([attn_gain, placed(gain_grads[0::2][:2]), placed(gain_grads[1::2][:2])])
    late_sum = [late_sum + core_swap(late_sum)]
    w_got, grads_out = [], []

    def kept_by(which):
        size = width // 4
        return jnp.concatenate(
            [lax.dynamic_slice_in_dim(w_got[0], i * (width // 2) + which * size, size, 1) for i in range(2)], axis=1
        )

    early = []

    expert_done = []

    def swap_heads(early_recv, w_own, *w_away):
        expert_done.extend(w_away[4:])
        w_away = w_away[:4]
        early.append(group_swap(early_sum + early_recv))
        early.append(early_sum + early_recv)
        w_away = [core_swap(v) for v in w_away]
        w_got.append(w_own + jnp.concatenate(w_away[2:] + w_away[:2], axis=1).astype(F32))
        w_got.append(group_swap(kept_by(1 - group).astype(B16)))

    def in_slabs(w_mine):
        w_mine = w_mine.T.astype(B16).reshape(2, chips // 2, rows, 3 * hd)
        return by_core(w_mine[0], w_mine[1], 1).reshape(devices, -1, 3 * hd)

    def join(w_mine):
        w_got.append(lax.all_to_all(w_mine, "ctx", split_axis=0, concat_axis=0, tiled=True))

    def small_step(step, others=lambda token: (), then=None):
        def run(token):
            return (from_across(late_sum[-1], step, token),) + tuple(others(token)), finish

        def finish(v, *rest):
            late_sum.append(late_sum[-1] + v)
            if then:
                then(*rest)

        return run

    n1_grad = ring_sum(
        lambda o: n1_part[offsets.index(o)],
        1,
        [
            lambda token: ([early_recv] + list(heads_grads(n1_part)) + expert_grads, swap_heads),
            small_step(2, lambda token: [in_slabs(kept_by(group) + after(w_got[1], token).astype(F32))], join),
            small_step(4),
            small_step(
                8,
                lambda token: [after(v, token).astype(F32)[None] for v in expert_done] + w_got[2:],
                lambda *v: grads_out.extend(v),
            ),
        ],
    )
    down_grad_out, gate_grad_out, up_grad_out, w_got = grads_out
    o_head = (o_head + after(o_recv, n1_grad[0]).astype(F32)).astype(B16)
    moves = [
        (g * devices + devices // 2 * g + j, g * devices + 2 * j + j % 2) for g in range(2) for j in range(devices // 2)
    ]
    whole = lax.ppermute(o_head, ("dp", "ctx"), moves)
    size = width // (2 * devices)
    pieces = (whole[:size], whole[size:])
    wo_grad = jnp.where(core == chip % 2, pick(pieces, core), core_swap(pick(pieces, 1 - core)))
    wo_grad = wo_grad.astype(F32)
    late_sum = after(late_sum[-1], n1_grad[0])
    late_sum = late_sum + group_swap(late_sum)
    early_sum = early[1] + after(early[0], n1_grad[0])
    w_got = w_got.transpose(1, 0, 2).astype(F32)
    slab_rows = w_got.shape[0]
    wq_grad, wk_grad, wv_grad = [
        w_got[:, :, i * hd : (i + 1) * hd].reshape(slab_rows, width) for i in range(3)
    ]
    tokens_grad = on_core(
        rows_grad_kernel,
        jax.ShapeDtypeStruct((rows, width), B16),
        [ids, *n1_grad, h1_grad, tokens, norm_attn.reshape(1, width)],
        0,
    )

    block_out = (h1 + moe_sum).astype(B16)
    router_sum, gain_sums = early_sum[:experts].T, [early_sum[experts]] + [late_sum[i] for i in range(3)]
    return (
        block_out,
        tokens_grad,
        gain_sums[1],
        gain_sums[2],
        gain_sums[3],
        gain_sums[0],
        wq_grad,
        wk_grad,
        wv_grad,
        wo_grad,
        router_sum,
        gate_grad_out,
        up_grad_out,
        down_grad_out,
    )


def local(*args):
    devices, groups = lax.axis_size("ctx"), lax.axis_size("dp")
    experts, owned = args[11].shape[1], args[12].shape[0]
    fits = devices == HEADS == experts and groups == 2 and owned == 1 and 3 * experts <= LANES
    return (local_fast if fits else local_general)(*args)


def solution(mesh):
    return jax.shard_map(
        local,
        mesh=mesh,
        in_specs=(
            P(("dp", "ctx"), None),
            P(("dp", "ctx")),
            P(("dp", "ctx"), None),
            P(),
            P(),
            P(),
            P(),
            P("ctx", None),
            P("ctx", None),
            P("ctx", None),
            P("ctx", None),
            P(),
            P("ctx", None, None),
            P("ctx", None, None),
            P("ctx", None, None),
            P(("dp", "ctx"), None),
        ),
        out_specs=(
            P(("dp", "ctx"), None),
            P(("dp", "ctx"), None),
            P(),
            P(),
            P(),
            P(),
            P(("dp", "ctx"), None),
            P(("dp", "ctx"), None),
            P(("dp", "ctx"), None),
            P(("dp", "ctx"), None),
            P(),
            P("ctx", None, "dp"),
            P("ctx", None, "dp"),
            P("ctx", "dp", None),
        ),
        check_vma=False,
    )
```
